32 devices in a mesh: grp: 4 (over x, core), dev: 8 (over z, y).
Axes of the slice: x: 2, y: 2, z: 4, core: 2. Of those that a mesh axis runs over, the one named last changes fastest.
Arguments:
- records: bfloat16 [128, 4, 2048], P(('grp', 'dev')), may hold values from -6 to 6
- usable: int32 [128, 4], replicated, may hold values 0 or 1
- panel_ids: int32 [2], replicated, may hold values from 0 to 7
Outputs:
- xcorr: bfloat16 [2, 16, 128, 512], P(None, None, ('grp', 'dev'))
The draws below stay inside these ranges and needn't reach their ends.
Inputs may be any that keep to these rules, and one draw needn't show every extreme that they name: `panel_ids`: each entry names a panel.
All inputs are finite; a program needn't handle non-finite values.
Results may differ from the reference program's by a relative error of at most 0.0075.
Values may be sent and summed in bfloat16 or wider, within the bound.
No kernel may reach another device: no remote copies, remote signals or barrier semaphores. Data moves between devices by JAX's collectives and lax.ppermute only.
A program may use at most 64 MiB of HBM per device.

```python
import math
import jax
import jax.numpy as jnp
from jax import lax

L = 2048
NF = 1024
SMOOTH = 64
NLAG = 512
WINS = 4
CH_DEV = 4
SRC_DEV = 2
STEPS = 2
NPANEL = 8
CHANNELS = 128
N_GRP = 4
N_DEV = 8


def plant(array, stream_key, least, largest):
    longest = array.shape.index(max(array.shape))
    spots = []
    for shift in (0, 1):
        where = [jax.random.randint(jax.random.fold_in(stream_key, axis), (), 0, length) for axis, length in enumerate(array.shape)]
        where[longest] = (where[longest] + shift) % array.shape[longest]
        spots.append(tuple(where))
    return array.at[spots[0]].set(least).at[spots[1]].set(largest)


def block_levels(key, dims, cuts, smallest, largest):
    def one(axis_at, blocks):
        steps = jax.random.uniform(jax.random.fold_in(jax.random.fold_in(key, 6), axis_at), (blocks,), jnp.float32, smallest / len(cuts), largest / len(cuts))
        return jnp.repeat(jnp.exp(steps), dims[axis_at] // blocks).reshape((-1,) + (1,) * (len(dims) - axis_at - 1))

    loudness = one(*cuts[0])
    for cut in cuts[1:]:
        loudness = loudness * one(*cut)
    return loudness


def normal_values(key, shape, deviation, reach, split=(), kind=jnp.bfloat16):
    values = jax.random.normal(key, shape, jnp.float32) * deviation
    if len(split) > 0:
        values = block_levels(key, shape, split, -0.22, 0.18) * values
    return jnp.clip(values, min=-reach, max=reach).astype(kind)


def setup_inputs(seed: int = 0) -> dict:
    splits = jax.random.split(jax.random.key(seed), 4)
    return {
        "records": normal_values(splits[0], (CHANNELS, WINS, L), 1.0, 6.0, ((0, 32),)),
        "usable": plant((jax.random.randint(splits[1], (CHANNELS, WINS), 0, 4) < 3).astype(jnp.int32), jax.random.fold_in(splits[1], 1), 0, 1),
        "panel_ids": jax.random.randint(splits[2], (STEPS,), 0, NPANEL).astype(jnp.int32),
    }


def forward_table(length, bin_count):
    samples = jnp.arange(length, dtype=jnp.int32)[:, None]
    bin_index = jnp.arange(1, bin_count + 1, dtype=jnp.int32)[None, :]
    phases = 2.0 * math.pi / length * (samples * bin_index % length).astype(jnp.float32)
    return jnp.concatenate([jnp.cos(phases), -jnp.sin(phases)], axis=1).astype(jnp.bfloat16)

def lag_table(length, bin_count, lag_count):
    bin_index = jnp.arange(1, bin_count + 1, dtype=jnp.int32)[:, None]
    lag_index = jnp.arange(lag_count, dtype=jnp.int32)[None, :] - lag_count // 2
    phases = 2.0 * math.pi / length * (bin_index * lag_index % length).astype(jnp.float32)
    factor = 1.0 / math.sqrt(bin_count)
    return jnp.concatenate([jnp.cos(phases) * factor, -jnp.sin(phases) * factor], axis=0).astype(jnp.bfloat16)

def band_matrix(bin_count, radius):
    positions = jnp.arange(bin_count, dtype=jnp.int32)
    nearby = jnp.abs(positions[:, None] - positions[None, :]) <= radius
    return nearby.astype(jnp.float32) / (2 * radius + 1)

def whiten(records, bin_count, radius):
    row_count, windows, length = records.shape
    flattened = records.reshape(row_count * windows, length)
    spectra = jnp.dot(flattened, forward_table(length, bin_count), preferred_element_type=jnp.float32)
    real_part = spectra[:, :bin_count]
    imag_part = spectra[:, bin_count:]
    amplitude = jnp.sqrt(real_part * real_part + imag_part * imag_part)
    smooth = jnp.dot(amplitude, band_matrix(bin_count, radius), precision=lax.Precision.HIGHEST)
    whitened = spectra / (jnp.concatenate([smooth, smooth], axis=1) + 1e-06)
    return whitened.astype(jnp.bfloat16).reshape(row_count, windows, 2 * bin_count)

def paired(left, right):
    return jnp.einsum('swf,rwf->srf', left.astype(jnp.float32), right.astype(jnp.float32))

def cross_spectra(sources, source_mask, receivers, receiver_mask, ltable, bin_count):
    source_re = sources[:, :, :bin_count]
    source_im = sources[:, :, bin_count:]
    recv_re = receivers[:, :, :bin_count]
    recv_im = receivers[:, :, bin_count:]
    real_sum = paired(source_re, recv_re) + paired(source_im, recv_im)
    imag_sum = paired(source_im, recv_re) - paired(source_re, recv_im)
    counts = jnp.dot(source_mask, receiver_mask.T, precision=lax.Precision.HIGHEST)
    denom = jnp.maximum(counts, 1.0)[:, :, None]
    stacked = jnp.concatenate([real_sum / denom, imag_sum / denom], axis=2).astype(jnp.bfloat16)
    source_count = sources.shape[0]
    recv_count = receivers.shape[0]
    lagged = jnp.dot(stacked.reshape(source_count * recv_count, 2 * bin_count), ltable, preferred_element_type=jnp.float32)
    return lagged.reshape(source_count, recv_count, ltable.shape[1]).astype(jnp.bfloat16)

def reference(records, usable, panel_ids):
    halves = CH_DEV // SRC_DEV
    whitened = whiten(records, NF, SMOOTH)
    masked = whitened * usable.astype(jnp.bfloat16)[:, :, None]
    mask_float = usable.astype(jnp.float32)
    grouped = masked.reshape(N_GRP, N_DEV, halves, SRC_DEV, WINS, 2 * NF)
    grouped_mask = mask_float.reshape(N_GRP, N_DEV, halves, SRC_DEV, WINS)
    recv_blocks = masked.reshape(N_GRP, N_DEV * CH_DEV, WINS, 2 * NF)
    mask_blocks = mask_float.reshape(N_GRP, N_DEV * CH_DEV, WINS)
    ltable = lag_table(L, NF, NLAG)
    results = []
    for step_index in range(STEPS):
        chosen = panel_ids[step_index]
        owning = chosen // halves
        within = chosen % halves
        sources = grouped[owning][:, within].reshape(N_DEV * SRC_DEV, WINS, 2 * NF)
        source_mask = grouped_mask[owning][:, within].reshape(N_DEV * SRC_DEV, WINS)

        def one_block(pieces):
            return cross_spectra(sources, source_mask, pieces[0], pieces[1], ltable, NF)
        mapped = lax.map(one_block, (recv_blocks, mask_blocks))
        results.append(jnp.transpose(mapped, (1, 0, 2, 3)).reshape(N_DEV * SRC_DEV, CHANNELS, NLAG))
    return jnp.stack(results)
```

```python
import functools
import math

import jax
import jax.numpy as jnp
import ml_dtypes
import numpy as np
from jax import lax
from jax.experimental import pallas as pl
from jax.experimental.pallas import tpu as pltpu
from jax.sharding import PartitionSpec as P

NLAG = 512
SRC_DEV = 2
STEPS = 2
RADIX = 16
AXES = ("grp", "dev")
SMEM = pl.BlockSpec(memory_space=pltpu.SMEM)
VMEM = pl.BlockSpec(memory_space=pltpu.VMEM)
AHEAD = pl.CostEstimate(flops=5_000_000_000, bytes_accessed=1_000_000, transcendentals=0)
PARAMS = pltpu.CompilerParams(vmem_limit_bytes=16 * 1024 * 1024)


def bin_order(bin_count):
    per = bin_count // RADIX
    order = []
    for q in range(RADIX // 2):
        for h in range(2):
            order.append(RADIX * np.arange(per) + 2 * q + h + 1)
    return np.concatenate(order)


def tables_kernel(length, table_ref, twiddle_ref):
    points = length // RADIX
    per = points // 2
    row = lax.broadcasted_iota(jnp.int32, (points, points), 0)
    lane = lax.broadcasted_iota(jnp.int32, (points, points), 1)
    phases = (2.0 * math.pi / points) * (row * (lane % per) % points).astype(jnp.float32)
    cosine, sine = jnp.cos(phases), jnp.sin(phases)
    for h in range(2):
        inside = (lane >= per) if h else (lane < per)
        c, s = jnp.where(inside, cosine, 0.0), jnp.where(inside, sine, 0.0)
        for part, values in enumerate(((c, -s), (s, c))):
            rows = slice((2 * h + part) * points, (2 * h + part + 1) * points)
            whole = jnp.concatenate(values, axis=1)
            high = whole.astype(jnp.bfloat16)
            table_ref[0, rows, :] = high
            table_ref[1, rows, :] = (whole - high.astype(jnp.float32)).astype(jnp.bfloat16)
    residue = lax.broadcasted_iota(jnp.int32, (RADIX, points), 0) + 1
    sample = lax.broadcasted_iota(jnp.int32, (RADIX, points), 1)
    phases = (2.0 * math.pi / length) * (residue * sample).astype(jnp.float32)
    twiddle_ref[0] = jnp.cos(phases)
    twiddle_ref[1] = -jnp.sin(phases)


def lag_table(length, bin_count, lag_count):
    bins = bin_order(bin_count)[:, None]
    lags = np.arange(lag_count)[None, :] - lag_count // 2
    phases = 2.0 * np.pi / length * (bins * lags % length)
    factor = 1.0 / math.sqrt(bin_count)
    cosine, sine = np.cos(phases) * factor, -np.sin(phases) * factor
    return np.concatenate([cosine, sine], axis=0).astype(ml_dtypes.bfloat16)


def real_dft(values):
    n = len(values)
    if n == 1:
        return [(values[0], None)]
    if n == 2:
        return [(values[0] + values[1], None), (values[0] - values[1], None)]
    even, odd = real_dft(values[0::2]), real_dft(values[1::2])
    quarter = n // 4
    out = [None] * (n // 2 + 1)
    for r in range(quarter + 1):
        (er, ei), (orr, oi) = even[r], odd[r]
        cosine, sine = math.cos(2 * math.pi * r / n), math.sin(2 * math.pi * r / n)
        if r == 0:
            tr, ti = orr, None
        elif r == quarter:
            tr, ti = None, -orr
        elif 8 * r == n:
            tr, ti = (orr + oi) * cosine, (oi - orr) * cosine
        else:
            tr, ti = orr * cosine + oi * sine, oi * cosine - orr * sine
        plus_re = er if tr is None else er + tr
        minus_re = er if tr is None else er - tr
        if ei is None:
            plus_im, minus_im = ti, ti
        elif ti is None:
            plus_im, minus_im = ei, -ei
        else:
            plus_im, minus_im = ei + ti, ti - ei
        out[r] = (plus_re, plus_im)
        if r < quarter:
            out[n // 2 - r] = (minus_re, minus_im)
    return out


def spectrum(samples, twiddle_ref, table_ref):
    rows, length = samples.shape
    points = length // RADIX
    half = real_dft([samples[:, i * points : (i + 1) * points] for i in range(RADIX)])
    lanes = []
    for residue in range(1, RADIX + 1):
        folded = min(residue, RADIX - residue)
        re, im = half[folded]
        if residue > RADIX // 2 and im is not None:
            im = -im
        cosine = twiddle_ref[0, residue - 1 : residue, :]
        sine = twiddle_ref[1, residue - 1 : residue, :]
        if im is None:
            lanes.append((re * cosine, re * sine))
        else:
            lanes.append((re * cosine - im * sine, re * sine + im * cosine))
    blocks = []
    for q in range(RADIX // 2):
        (ar, ai), (br, bi) = lanes[2 * q], lanes[2 * q + 1]
        blocks.append(jnp.concatenate([ar, ai, br, bi], axis=1))
    stacked = jnp.concatenate(blocks, axis=0)
    high = stacked.astype(jnp.bfloat16)
    low = (stacked - high.astype(jnp.float32)).astype(jnp.bfloat16)
    both = jnp.dot(
        jnp.concatenate([high, low], axis=0), table_ref[0], preferred_element_type=jnp.float32
    )
    count = stacked.shape[0]
    out = both[:count] + both[count:]
    out = out + jnp.dot(high, table_ref[1], preferred_element_type=jnp.float32)
    width = out.shape[1] // 2
    re = [out[q * rows : (q + 1) * rows, :width] for q in range(RADIX // 2)]
    im = [out[q * rows : (q + 1) * rows, width:] for q in range(RADIX // 2)]
    return re, im


def scales(re, im, radius, mask):
    amp = [jnp.sqrt(a * a + b * b) for a, b in zip(re, im)]
    rows, width = amp[0].shape
    per = width // 2
    reach = radius // RADIX
    lane = lax.broadcasted_iota(jnp.int32, (rows, width), 1)
    place = lane % per
    upper = lane >= per
    swapped = [pltpu.roll(a, per, 1) for a in amp]
    pair = [a + b for a, b in zip(amp, swapped)]
    total = pair[0]
    for value in pair[1:]:
        total = total + value

    def shifted(value, by):
        moved = pltpu.roll(value, (-by) % width, 1)
        inside = (place + by >= 0) & (place + by < per)
        return jnp.where(inside, moved, 0.0)

    centre = total
    for by in range(1, reach):
        centre = centre + shifted(total, by) + shifted(total, -by)
    before = jnp.zeros_like(total)
    out = []
    for a, b, both in zip(amp, swapped, pair):
        upto = before + a + jnp.where(upper, b, 0.0)
        before_here = before + jnp.where(upper, b, 0.0)
        onward = total - before_here
        before = before + both
        out.append((upto, onward))
    result = []
    for upto, onward in out:
        summed = centre + shifted(upto, reach) + shifted(onward, -reach)
        result.append(mask / (summed * (1.0 / (2 * radius + 1)) + 1e-06))
    return result


def whiten_rows(samples, radius, mask, twiddle_ref, table_ref, relay_ref, out_ref):
    rows = samples.shape[0]
    blocks = RADIX // 2
    re, im = spectrum(samples, twiddle_ref, table_ref)
    scale = scales(re, im, radius, mask)
    for part, values in enumerate((re, im)):
        for q in range(blocks):
            relay_ref[pl.ds(part * rows * blocks + q, rows, stride=blocks), :] = (
                values[q] * scale[q]
            )
    out_ref[...] = relay_ref[...].astype(jnp.bfloat16)


def holdings(member_bits):
    held = [(0, 0)]
    for bit in member_bits[:-1]:
        held += [(k ^ bit, 1 - odd) for k, odd in held]
    brought = [(k ^ member_bits[-1], 1 - odd) for k, odd in held]
    return held, brought


def panel_order(member_bits):
    held, brought = holdings(member_bits)
    flip = lambda pieces: [(k, 1 - odd) for k, odd in pieces]
    return held + flip(held) + brought + flip(brought)


def prepare_kernel(radius, order, ids_ref, usable_ref, raw_ref, twiddle_ref, table_ref, *rest):
    spectra_ref, inverse_ref, choice_ref, mask_ref, samples, relay = rest
    channels, windows, _ = raw_ref.shape
    halves = channels // SRC_DEV
    groups, members = lax.axis_size("grp"), lax.axis_size("dev")
    group, member = lax.axis_index("grp"), lax.axis_index("dev")
    core = group % SRC_DEV
    first = (group * members + member) * channels
    flags = usable_ref[...].astype(jnp.float32).astype(jnp.bfloat16)
    total = flags.shape[1]

    def flags_of(picks):
        return lax.dot_general(
            picks.astype(jnp.bfloat16), flags, (((1,), (1,)), ((), ())),
            preferred_element_type=jnp.float32,
        )

    def at_window(rows_flags):
        rows = rows_flags.shape[0]
        row = lax.broadcasted_iota(jnp.int32, (rows, windows), 0)
        column = lax.broadcasted_iota(jnp.int32, (rows, windows), 1)
        kept = jnp.where(row % windows == column, rows_flags, 0.0)
        return jnp.sum(kept, axis=1, keepdims=True)

    owning = [ids_ref[t] // halves for t in range(STEPS)]
    within = [ids_ref[t] % halves for t in range(STEPS)]

    for r in range(channels):
        samples[r * windows : (r + 1) * windows, :] = raw_ref[r].astype(jnp.float32)
    rows = channels * windows
    row = lax.broadcasted_iota(jnp.int32, (rows, total), 0)
    lane = lax.broadcasted_iota(jnp.int32, (rows, total), 1)
    own = jnp.where(lane == first + row // windows, 1.0, 0.0)
    mask = at_window(flags_of(own))
    whiten_rows(samples[...], radius, mask, twiddle_ref, table_ref, relay, spectra_ref)

    rows = STEPS * windows
    row = lax.broadcasted_iota(jnp.int32, (rows, total), 0)
    lane = lax.broadcasted_iota(jnp.int32, (rows, total), 1)
    picks = jnp.zeros((rows, total), jnp.float32)
    for t in range(STEPS):
        channel = (owning[t] * members + member) * channels + within[t] * SRC_DEV + core
        picks = jnp.where((row // windows == t) & (lane == channel), 1.0, picks)
    mask_ref[...] = jnp.broadcast_to(at_window(flags_of(picks)), mask_ref.shape)

    row = lax.broadcasted_iota(jnp.int32, choice_ref.shape, 0)
    choice = jnp.zeros(choice_ref.shape, jnp.float32)
    for t in range(STEPS):
        picked = (t * groups + (owning[t] ^ group)) * halves + within[t]
        choice = jnp.where(row == picked, 1.0, choice)
    choice_ref[...] = choice

    rows = STEPS * channels
    row = lax.broadcasted_iota(jnp.int32, (rows, total), 0)
    lane = lax.broadcasted_iota(jnp.int32, (rows, total), 1)
    received = flags_of(jnp.where(lane == first + row % channels, 1.0, 0.0))
    blocks = []
    for k, odd in order:
        picks = jnp.zeros((rows, total), jnp.float32)
        for t in range(STEPS):
            channel = (
                (owning[t] * members + (member ^ k)) * channels
                + within[t] * SRC_DEV
                + (core + odd) % SRC_DEV
            )
            picks = jnp.where((row // channels == t) & (lane == channel), 1.0, picks)
        blocks.append(picks)
    sent = flags_of(jnp.concatenate(blocks, axis=0))
    both = sent * jnp.concatenate([received] * len(order), axis=0)
    counts = jnp.sum(both, axis=1, keepdims=True)
    inverse_ref[...] = jnp.broadcast_to(1.0 / jnp.maximum(counts, 1.0), inverse_ref.shape)


def source_kernel(radius, *refs):
    choice_ref, mask_ref = refs[:2]
    twiddle_ref, table_ref, out_ref, samples, relay = refs[-5:]
    raws = refs[2:-5]
    channels, windows, length = raws[0].shape
    halves = channels // SRC_DEV
    core = lax.axis_index("grp") % SRC_DEV
    points = length // RADIX
    for step in range(STEPS):
        held = [jnp.zeros((windows, points), jnp.float32)] * RADIX
        for k, raw_ref in enumerate(raws):
            for h in range(halves):
                index = (step * len(raws) + k) * halves + h
                here = jnp.broadcast_to(choice_ref[index : index + 1, :], (windows, points)) > 0.0
                row = raw_ref[h * SRC_DEV + core].astype(jnp.float32)
                for n in range(RADIX):
                    held[n] = jnp.where(here, row[:, n * points : (n + 1) * points], held[n])
        for n in range(RADIX):
            samples[step * windows : (step + 1) * windows, n * points : (n + 1) * points] = held[n]
    whiten_rows(samples[...], radius, mask_ref[:, :1], twiddle_ref, table_ref, relay, out_ref)


def lagged_rows(windows, pieces, recv_ref, inverse, table_ref, products, stacked):
    blocks = RADIX // 2
    receivers = recv_ref.shape[0] // (2 * windows * blocks)

    def row_set(ref, base, first, rows):
        out = []
        for part in range(2):
            held = []
            for w in range(0, windows, 2):
                start = base + (part * rows + first + w) * blocks
                both = ref[start : start + 2 * blocks, :].astype(jnp.float32)
                held += [both[:blocks], both[blocks:]]
            out.append(held)
        return out

    own = [row_set(recv_ref, 0, r * windows, receivers * windows) for r in range(receivers)]
    pairs = len(pieces) * STEPS * receivers
    for p, (ref, base) in enumerate(pieces):
        for step in range(STEPS):
            a, b = row_set(ref, base, step * windows, STEPS * windows)
            for r in range(receivers):
                c, e = own[r]
                re = im = None
                for w in range(windows):
                    re_w = a[w] * c[w] + b[w] * e[w]
                    im_w = b[w] * c[w] - a[w] * e[w]
                    re = re_w if re is None else re + re_w
                    im = im_w if im is None else im + im_w
                pair = (p * STEPS + step) * receivers + r
                products[0, pair * blocks : (pair + 1) * blocks, :] = re
                products[1, pair * blocks : (pair + 1) * blocks, :] = im
    width = products.shape[2]
    for part in range(2):
        for q in range(blocks):
            column = (part * blocks + q) * width
            values = products[part, pl.ds(q, pairs, stride=blocks), :] * inverse
            stacked[:, column : column + width] = values.astype(jnp.bfloat16)
    return jnp.dot(stacked[...], table_ref[...], preferred_element_type=jnp.float32)


def pieces_of(ref, windows):
    rows = 2 * STEPS * windows * (RADIX // 2)
    return [(ref, base) for base in range(0, ref.shape[0], rows)]


def part_kernel(windows, first, inverse_ref, recv_ref, table_ref, *refs):
    out_ref, products, stacked = refs[-3:]
    pieces = [piece for ref in refs[:-3] for piece in pieces_of(ref, windows)]
    inverse = inverse_ref[first : first + out_ref.shape[0], :]
    out_ref[...] = lagged_rows(windows, pieces, recv_ref, inverse, table_ref, products, stacked)


def last_kernel(windows, order, inverse_ref, recv_ref, table_ref, piece_ref, *refs):
    out_ref, products, stacked = refs[-3:]
    pieces = pieces_of(piece_ref, windows)
    rows = stacked.shape[0]
    inverse = inverse_ref[inverse_ref.shape[0] - rows :, :]
    member = lax.axis_index("dev")
    core = lax.axis_index("grp") % SRC_DEV
    receivers = out_ref.shape[2]

    def place(rows_ref, some):
        for p, (k, odd) in enumerate(some):
            source = (member ^ k) * SRC_DEV + (core + odd) % SRC_DEV
            for step in range(STEPS):
                pair = (p * STEPS + step) * receivers
                out_ref[step, source] = rows_ref[pair : pair + receivers, :].astype(jnp.bfloat16)

    done = 0
    for ref in refs[:-3]:
        count = ref.shape[0] // (STEPS * receivers)
        place(ref, order[done : done + count])
        done += count
    lagged = lagged_rows(windows, pieces, recv_ref, inverse, table_ref, products, stacked)
    place(lagged, order[done:])


def on_device(records, usable, panel_ids):
    channels, windows, length = records.shape
    bin_count = length // 2
    radius = bin_count // 16
    halves = channels // SRC_DEV
    groups = lax.axis_size("grp")
    members = lax.axis_size("dev")
    blocks = RADIX // 2
    width = bin_count // blocks

    def exchange(value, group_bit, member_bit):
        flip = group_bit * members + member_bit
        pairs = [(i, i ^ flip) for i in range(groups * members)]
        return lax.ppermute(value, AXES, pairs)

    points = length // RADIX
    table, twiddle = pl.pallas_call(
        functools.partial(tables_kernel, length),
        out_shape=[
            jax.ShapeDtypeStruct((2, 4 * points, 2 * points), jnp.bfloat16),
            jax.ShapeDtypeStruct((2, RADIX, points), jnp.float32),
        ],
        in_specs=[],
        out_specs=[VMEM] * 2,
        compiler_params=PARAMS,
        cost_estimate=AHEAD,
        name="short_tables",
    )()
    ltable = jnp.asarray(lag_table(length, bin_count, NLAG))
    member_bits = []
    bit = members // 2
    while bit:
        member_bits.append(bit)
        bit //= 2
    order = panel_order(member_bits)

    raws = {0: records}
    bit = groups // 2
    while bit > 1:
        raws.update({k ^ bit ^ 1: exchange(v, bit ^ 1, 0) for k, v in raws.items()})
        bit //= 2
    raws.update({k ^ 1: exchange(v, 1, 0) for k, v in raws.items()})
    raws = [raws[k] for k in range(groups)]

    row_count = channels * windows
    pairs = len(order) * STEPS * channels
    receivers, inverse, choice, mask = pl.pallas_call(
        functools.partial(prepare_kernel, radius, order),
        out_shape=[
            jax.ShapeDtypeStruct((2 * row_count * blocks, width), jnp.bfloat16),
            jax.ShapeDtypeStruct((pairs, width), jnp.float32),
            jax.ShapeDtypeStruct((STEPS * groups * halves, width), jnp.float32),
            jax.ShapeDtypeStruct((STEPS * windows, width), jnp.float32),
        ],
        in_specs=[SMEM] + [VMEM] * 4,
        out_specs=[VMEM] * 4,
        scratch_shapes=[
            pltpu.VMEM((row_count, length), jnp.float32),
            pltpu.VMEM((2 * row_count * blocks, width), jnp.float32),
        ],
        compiler_params=PARAMS,
        cost_estimate=AHEAD,
        name="receiver_spectra",
    )(panel_ids, usable.T, records, twiddle, table)

    source_rows = STEPS * windows
    piece = pl.pallas_call(
        functools.partial(source_kernel, radius),
        out_shape=jax.ShapeDtypeStruct((2 * source_rows * blocks, width), jnp.bfloat16),
        in_specs=[VMEM] * (groups + 4),
        out_specs=VMEM,
        scratch_shapes=[
            pltpu.VMEM((source_rows, length), jnp.float32),
            pltpu.VMEM((2 * source_rows * blocks, width), jnp.float32),
        ],
        compiler_params=PARAMS,
        name="source_spectra",
    )(choice, mask, *raws, twiddle, table)

    held = piece
    for bit in member_bits[:-1]:
        held = jnp.concatenate([held, exchange(held, 1, bit)], axis=0)
    brought = exchange(held, 1, member_bits[-1])
    held_other = exchange(held, 1, 0)
    brought_other = exchange(brought, 1, 0)

    def part(first, *buffers):
        rows = sum(b.shape[0] for b in buffers) // (2 * windows * blocks) * channels
        return pl.pallas_call(
            functools.partial(part_kernel, windows, first),
            out_shape=jax.ShapeDtypeStruct((rows, NLAG), jnp.float32),
            in_specs=[VMEM] * (3 + len(buffers)),
            out_specs=VMEM,
            scratch_shapes=[
                pltpu.VMEM((2, rows * blocks, width), jnp.float32),
                pltpu.VMEM((rows, 2 * bin_count), jnp.bfloat16),
            ],
            compiler_params=PARAMS,
            name="correlate_part",
        )(inverse, receivers, ltable, *buffers)

    early = part(0, held, held_other)
    middle = part(pairs // 2, brought)
    rows = pairs // 4
    return pl.pallas_call(
        functools.partial(last_kernel, windows, order),
        out_shape=jax.ShapeDtypeStruct(
            (STEPS, members * SRC_DEV, channels, NLAG), jnp.bfloat16
        ),
        in_specs=[VMEM] * 6,
        out_specs=VMEM,
        scratch_shapes=[
            pltpu.VMEM((2, rows * blocks, width), jnp.float32),
            pltpu.VMEM((rows, 2 * bin_count), jnp.bfloat16),
        ],
        compiler_params=PARAMS,
        name="correlate_last",
    )(inverse, receivers, ltable, brought_other, early, middle)


def solution(mesh):
    placed = (P(AXES, None, None), P(), P())
    return jax.shard_map(
        on_device,
        mesh=mesh,
        in_specs=placed,
        out_specs=P(None, None, AXES, None),
        check_vma=False,
    )
```

```python
import functools
import math

import jax
import jax.numpy as jnp
import ml_dtypes
import numpy as np
from jax import lax
from jax.experimental import pallas as pl
from jax.experimental.pallas import tpu as pltpu
from jax.sharding import PartitionSpec as P

NLAG = 512
SRC_DEV = 2
STEPS = 2
RADIX = 16
AXES = ("grp", "dev")
SMEM = pl.BlockSpec(memory_space=pltpu.SMEM)
VMEM = pl.BlockSpec(memory_space=pltpu.VMEM)
AHEAD = pl.CostEstimate(flops=5_000_000_000, bytes_accessed=1_000_000, transcendentals=0)
BESIDE = pl.CostEstimate(flops=1_000_000_000, bytes_accessed=1_000_000, transcendentals=0)
PARAMS = pltpu.CompilerParams(vmem_limit_bytes=16 * 1024 * 1024)


def bin_order(bin_count):
    per = bin_count // RADIX
    order = []
    for q in range(RADIX // 2):
        for h in range(2):
            order.append(RADIX * np.arange(per) + 2 * q + h + 1)
    return np.concatenate(order)


def tables_kernel(length, table_ref, twiddle_ref):
    points = length // RADIX
    per = points // 2
    row = lax.broadcasted_iota(jnp.int32, (points, points), 0)
    lane = lax.broadcasted_iota(jnp.int32, (points, points), 1)
    phases = (2.0 * math.pi / points) * (row * (lane % per) % points).astype(jnp.float32)
    cosine, sine = jnp.cos(phases), jnp.sin(phases)
    for h in range(2):
        inside = (lane >= per) if h else (lane < per)
        c, s = jnp.where(inside, cosine, 0.0), jnp.where(inside, sine, 0.0)
        for part, values in enumerate(((c, -s), (s, c))):
            rows = slice((2 * h + part) * points, (2 * h + part + 1) * points)
            whole = jnp.concatenate(values, axis=1)
            high = whole.astype(jnp.bfloat16)
            table_ref[0, rows, :] = high
            table_ref[1, rows, :] = (whole - high.astype(jnp.float32)).astype(jnp.bfloat16)
    residue = lax.broadcasted_iota(jnp.int32, (RADIX, points), 0) + 1
    sample = lax.broadcasted_iota(jnp.int32, (RADIX, points), 1)
    phases = (2.0 * math.pi / length) * (residue * sample).astype(jnp.float32)
    twiddle_ref[0] = jnp.cos(phases)
    twiddle_ref[1] = -jnp.sin(phases)


def lag_table(length, bin_count, lag_count):
    bins = bin_order(bin_count)[:, None]
    lags = np.arange(lag_count)[None, :] - lag_count // 2
    phases = 2.0 * np.pi / length * (bins * lags % length)
    factor = 1.0 / math.sqrt(bin_count)
    cosine, sine = np.cos(phases) * factor, -np.sin(phases) * factor
    return np.concatenate([cosine, sine], axis=0).astype(ml_dtypes.bfloat16)


def real_dft(values):
    n = len(values)
    if n == 1:
        return [(values[0], None)]
    if n == 2:
        return [(values[0] + values[1], None), (values[0] - values[1], None)]
    even, odd = real_dft(values[0::2]), real_dft(values[1::2])
    quarter = n // 4
    out = [None] * (n // 2 + 1)
    for r in range(quarter + 1):
        (er, ei), (orr, oi) = even[r], odd[r]
        cosine, sine = math.cos(2 * math.pi * r / n), math.sin(2 * math.pi * r / n)
        if r == 0:
            tr, ti = orr, None
        elif r == quarter:
            tr, ti = None, -orr
        elif 8 * r == n:
            tr, ti = (orr + oi) * cosine, (oi - orr) * cosine
        else:
            tr, ti = orr * cosine + oi * sine, oi * cosine - orr * sine
        plus_re = er if tr is None else er + tr
        minus_re = er if tr is None else er - tr
        if ei is None:
            plus_im, minus_im = ti, ti
        elif ti is None:
            plus_im, minus_im = ei, -ei
        else:
            plus_im, minus_im = ei + ti, ti - ei
        out[r] = (plus_re, plus_im)
        if r < quarter:
            out[n // 2 - r] = (minus_re, minus_im)
    return out


def spectrum(samples, twiddle_ref, table_ref):
    rows, length = samples.shape
    points = length // RADIX
    half = real_dft([samples[:, i * points : (i + 1) * points] for i in range(RADIX)])
    lanes = []
    for residue in range(1, RADIX + 1):
        folded = min(residue, RADIX - residue)
        re, im = half[folded]
        if residue > RADIX // 2 and im is not None:
            im = -im
        cosine = twiddle_ref[0, residue - 1 : residue, :]
        sine = twiddle_ref[1, residue - 1 : residue, :]
        if im is None:
            lanes.append((re * cosine, re * sine))
        else:
            lanes.append((re * cosine - im * sine, re * sine + im * cosine))
    blocks = []
    for q in range(RADIX // 2):
        (ar, ai), (br, bi) = lanes[2 * q], lanes[2 * q + 1]
        blocks.append(jnp.concatenate([ar, ai, br, bi], axis=1))
    stacked = jnp.concatenate(blocks, axis=0)
    high = stacked.astype(jnp.bfloat16)
    low = (stacked - high.astype(jnp.float32)).astype(jnp.bfloat16)
    both = jnp.dot(
        jnp.concatenate([high, low], axis=0), table_ref[0], preferred_element_type=jnp.float32
    )
    count = stacked.shape[0]
    out = both[:count] + both[count:]
    out = out + jnp.dot(high, table_ref[1], preferred_element_type=jnp.float32)
    width = out.shape[1] // 2
    re = [out[q * rows : (q + 1) * rows, :width] for q in range(RADIX // 2)]
    im = [out[q * rows : (q + 1) * rows, width:] for q in range(RADIX // 2)]
    return re, im


def scales(re, im, radius, mask):
    amp = [jnp.sqrt(a * a + b * b) for a, b in zip(re, im)]
    rows, width = amp[0].shape
    per = width // 2
    reach = radius // RADIX
    lane = lax.broadcasted_iota(jnp.int32, (rows, width), 1)
    place = lane % per
    upper = lane >= per
    swapped = [pltpu.roll(a, per, 1) for a in amp]
    pair = [a + b for a, b in zip(amp, swapped)]
    total = pair[0]
    for value in pair[1:]:
        total = total + value

    def shifted(value, by):
        moved = pltpu.roll(value, (-by) % width, 1)
        inside = (place + by >= 0) & (place + by < per)
        return jnp.where(inside, moved, 0.0)

    centre = total
    for by in range(1, reach):
        centre = centre + shifted(total, by) + shifted(total, -by)
    before = jnp.zeros_like(total)
    out = []
    for a, b, both in zip(amp, swapped, pair):
        upto = before + a + jnp.where(upper, b, 0.0)
        before_here = before + jnp.where(upper, b, 0.0)
        onward = total - before_here
        before = before + both
        out.append((upto, onward))
    result = []
    for upto, onward in out:
        summed = centre + shifted(upto, reach) + shifted(onward, -reach)
        result.append(mask / (summed * (1.0 / (2 * radius + 1)) + 1e-06))
    return result


def whiten_rows(samples, radius, mask, twiddle_ref, table_ref, relay_ref, out_ref):
    rows = samples.shape[0]
    blocks = RADIX // 2
    re, im = spectrum(samples, twiddle_ref, table_ref)
    scale = scales(re, im, radius, mask)
    for part, values in enumerate((re, im)):
        for q in range(blocks):
            relay_ref[pl.ds(part * rows * blocks + q, rows, stride=blocks), :] = (
                values[q] * scale[q]
            )
    out_ref[...] = relay_ref[...].astype(jnp.bfloat16)


def holdings(member_bits):
    held = [(0, 0)]
    for bit in member_bits[:-1]:
        held += [(k ^ bit, 1 - odd) for k, odd in held]
    brought = [(k ^ member_bits[-1], 1 - odd) for k, odd in held]
    return held, brought


def panel_order(member_bits):
    held, brought = holdings(member_bits)
    flip = lambda pieces: [(k, 1 - odd) for k, odd in pieces]
    return held + flip(held) + brought + flip(brought)


def flags_of(picks, flags):
    return lax.dot_general(
        picks.astype(jnp.bfloat16),
        flags,
        (((1,), (1,)), ((), ())),
        preferred_element_type=jnp.float32,
    )


def at_window(rows_flags):
    row = lax.broadcasted_iota(jnp.int32, rows_flags.shape, 0)
    column = lax.broadcasted_iota(jnp.int32, rows_flags.shape, 1)
    kept = jnp.where(row % rows_flags.shape[1] == column, rows_flags, 0.0)
    return jnp.sum(kept, axis=1, keepdims=True)


def choice_kernel(halves, channels, ids_ref, usable_ref, after_ref, choice_ref, mask_ref, take_ref):
    del after_ref
    windows, total = usable_ref.shape
    members = lax.axis_size("dev")
    group, member = lax.axis_index("grp"), lax.axis_index("dev")
    core, plane = group % SRC_DEV, group // SRC_DEV
    flags = usable_ref[...].astype(jnp.float32).astype(jnp.bfloat16)
    owning = [ids_ref[t] // halves for t in range(STEPS)]
    within = [ids_ref[t] % halves for t in range(STEPS)]

    row = lax.broadcasted_iota(jnp.int32, choice_ref.shape, 0)
    choice = jnp.zeros(choice_ref.shape, jnp.float32)
    for t in range(STEPS):
        apart = (owning[t] + core) % SRC_DEV
        choice = jnp.where(row == (t * SRC_DEV + apart) * halves + within[t], 1.0, choice)
    choice_ref[...] = choice

    rows = STEPS * windows
    row = lax.broadcasted_iota(jnp.int32, (rows, total), 0)
    lane = lax.broadcasted_iota(jnp.int32, (rows, total), 1)
    picks = jnp.zeros((rows, total), jnp.float32)
    for t in range(STEPS):
        channel = (owning[t] * members + member) * channels + within[t] * SRC_DEV + core
        picks = jnp.where((row // windows == t) & (lane == channel), 1.0, picks)
    mask_ref[...] = jnp.broadcast_to(at_window(flags_of(picks, flags)), mask_ref.shape)

    row = lax.broadcasted_iota(jnp.int32, take_ref.shape[1:], 0)
    for index in range(take_ref.shape[0]):
        take = jnp.zeros(take_ref.shape[1:], jnp.float32)
        for t in range(STEPS):
            differs = ((owning[t] // SRC_DEV) ^ plane) >> index & 1
            take = jnp.where(row // windows == t, differs.astype(jnp.float32), take)
        take_ref[index] = take


def pick_kernel(flip, choice_ref, own_ref, other_ref, out_ref, samples):
    channels, windows, length = own_ref.shape
    halves = channels // SRC_DEV
    half = (lax.axis_index("grp") + flip) % SRC_DEV
    points = length // RADIX
    for step in range(STEPS):
        held = [jnp.zeros((windows, points), jnp.float32)] * RADIX
        for k, raw_ref in enumerate((own_ref, other_ref)):
            for h in range(halves):
                index = (step * SRC_DEV + k) * halves + h
                here = jnp.broadcast_to(choice_ref[index : index + 1, :], (windows, points)) > 0.0
                row = raw_ref[h * SRC_DEV + half].astype(jnp.float32)
                for n in range(RADIX):
                    held[n] = jnp.where(here, row[:, n * points : (n + 1) * points], held[n])
        for n in range(RADIX):
            samples[step * windows : (step + 1) * windows, n * points : (n + 1) * points] = held[n]
    out_ref[...] = samples[...].astype(out_ref.dtype)


def receiver_kernel(radius, order, ids_ref, usable_ref, raw_ref, twiddle_ref, table_ref, *rest):
    spectra_ref, inverse_ref, samples, relay = rest
    channels, windows, _ = raw_ref.shape
    halves = channels // SRC_DEV
    members = lax.axis_size("dev")
    group, member = lax.axis_index("grp"), lax.axis_index("dev")
    core = group % SRC_DEV
    first = (group * members + member) * channels
    flags = usable_ref[...].astype(jnp.float32).astype(jnp.bfloat16)
    total = flags.shape[1]
    owning = [ids_ref[t] // halves for t in range(STEPS)]
    within = [ids_ref[t] % halves for t in range(STEPS)]

    for r in range(channels):
        samples[r * windows : (r + 1) * windows, :] = raw_ref[r].astype(jnp.float32)
    rows = channels * windows
    row = lax.broadcasted_iota(jnp.int32, (rows, total), 0)
    lane = lax.broadcasted_iota(jnp.int32, (rows, total), 1)
    own = jnp.where(lane == first + row // windows, 1.0, 0.0)
    mask = at_window(flags_of(own, flags))
    whiten_rows(samples[...], radius, mask, twiddle_ref, table_ref, relay, spectra_ref)

    rows = STEPS * channels
    row = lax.broadcasted_iota(jnp.int32, (rows, total), 0)
    lane = lax.broadcasted_iota(jnp.int32, (rows, total), 1)
    received = flags_of(jnp.where(lane == first + row % channels, 1.0, 0.0), flags)
    blocks = []
    for k, odd in order:
        picks = jnp.zeros((rows, total), jnp.float32)
        for t in range(STEPS):
            channel = (
                (owning[t] * members + (member ^ k)) * channels
                + within[t] * SRC_DEV
                + (core + odd) % SRC_DEV
            )
            picks = jnp.where((row // channels == t) & (lane == channel), 1.0, picks)
        blocks.append(picks)
    sent = flags_of(jnp.concatenate(blocks, axis=0), flags)
    both = sent * jnp.concatenate([received] * len(order), axis=0)
    counts = jnp.sum(both, axis=1, keepdims=True)
    inverse_ref[...] = jnp.broadcast_to(1.0 / jnp.maximum(counts, 1.0), inverse_ref.shape)


def source_kernel(radius, *refs):
    take_ref, mask_ref, kept_ref, came_ref, twiddle_ref, table_ref = refs[:6]
    out_ref, relay = refs[-2:]
    rows, length = kept_ref.shape
    points = length // RADIX
    here = take_ref[...] > 0.0
    kept, came = kept_ref[...].astype(jnp.float32), came_ref[...].astype(jnp.float32)
    here = jnp.concatenate([here] * RADIX, axis=1)
    samples = jnp.where(here, came, kept)
    whiten_rows(samples, radius, mask_ref[:, :1], twiddle_ref, table_ref, relay, out_ref)


def lagged_rows(windows, pieces, recv_ref, inverse, table_ref, products, stacked):
    blocks = RADIX // 2
    receivers = recv_ref.shape[0] // (2 * windows * blocks)

    def row_set(ref, base, first, rows):
        out = []
        for part in range(2):
            held = []
            for w in range(0, windows, 2):
                start = base + (part * rows + first + w) * blocks
                both = ref[start : start + 2 * blocks, :].astype(jnp.float32)
                held += [both[:blocks], both[blocks:]]
            out.append(held)
        return out

    own = [row_set(recv_ref, 0, r * windows, receivers * windows) for r in range(receivers)]
    pairs = len(pieces) * STEPS * receivers
    for p, (ref, base) in enumerate(pieces):
        for step in range(STEPS):
            a, b = row_set(ref, base, step * windows, STEPS * windows)
            for r in range(receivers):
                c, e = own[r]
                re = im = None
                for w in range(windows):
                    re_w = a[w] * c[w] + b[w] * e[w]
                    im_w = b[w] * c[w] - a[w] * e[w]
                    re = re_w if re is None else re + re_w
                    im = im_w if im is None else im + im_w
                pair = (p * STEPS + step) * receivers + r
                products[0, pair * blocks : (pair + 1) * blocks, :] = re
                products[1, pair * blocks : (pair + 1) * blocks, :] = im
    width = products.shape[2]
    for part in range(2):
        for q in range(blocks):
            column = (part * blocks + q) * width
            values = products[part, pl.ds(q, pairs, stride=blocks), :] * inverse
            stacked[:, column : column + width] = values.astype(jnp.bfloat16)
    return jnp.dot(stacked[...], table_ref[...], preferred_element_type=jnp.float32)


def pieces_of(ref, windows):
    rows = 2 * STEPS * windows * (RADIX // 2)
    return [(ref, base) for base in range(0, ref.shape[0], rows)]


def part_kernel(windows, first, inverse_ref, recv_ref, table_ref, *refs):
    out_ref, products, stacked = refs[-3:]
    pieces = [piece for ref in refs[:-3] for piece in pieces_of(ref, windows)]
    inverse = inverse_ref[first : first + out_ref.shape[0], :]
    out_ref[...] = lagged_rows(windows, pieces, recv_ref, inverse, table_ref, products, stacked)


def last_kernel(windows, order, inverse_ref, recv_ref, table_ref, piece_ref, *refs):
    out_ref, products, stacked = refs[-3:]
    pieces = pieces_of(piece_ref, windows)
    rows = stacked.shape[0]
    inverse = inverse_ref[inverse_ref.shape[0] - rows :, :]
    member = lax.axis_index("dev")
    core = lax.axis_index("grp") % SRC_DEV
    receivers = out_ref.shape[2]

    def place(rows_ref, some):
        for p, (k, odd) in enumerate(some):
            source = (member ^ k) * SRC_DEV + (core + odd) % SRC_DEV
            for step in range(STEPS):
                pair = (p * STEPS + step) * receivers
                out_ref[step, source] = rows_ref[pair : pair + receivers, :].astype(jnp.bfloat16)

    done = 0
    for ref in refs[:-3]:
        count = ref.shape[0] // (STEPS * receivers)
        place(ref, order[done : done + count])
        done += count
    lagged = lagged_rows(windows, pieces, recv_ref, inverse, table_ref, products, stacked)
    place(lagged, order[done:])


def on_device(records, usable, panel_ids):
    channels, windows, length = records.shape
    bin_count = length // 2
    radius = bin_count // 16
    halves = channels // SRC_DEV
    groups = lax.axis_size("grp")
    members = lax.axis_size("dev")
    blocks = RADIX // 2
    width = bin_count // blocks

    def exchange(value, group_bit, member_bit):
        flip = group_bit * members + member_bit
        pairs = [(i, i ^ flip) for i in range(groups * members)]
        return lax.ppermute(value, AXES, pairs)

    points = length // RADIX
    table, twiddle = pl.pallas_call(
        functools.partial(tables_kernel, length),
        out_shape=[
            jax.ShapeDtypeStruct((2, 4 * points, 2 * points), jnp.bfloat16),
            jax.ShapeDtypeStruct((2, RADIX, points), jnp.float32),
        ],
        in_specs=[],
        out_specs=[VMEM] * 2,
        compiler_params=PARAMS,
        cost_estimate=AHEAD,
        name="short_tables",
    )()
    ltable = jnp.asarray(lag_table(length, bin_count, NLAG))
    member_bits = []
    bit = members // 2
    while bit:
        member_bits.append(bit)
        bit //= 2
    order = panel_order(member_bits)

    usable_rows = usable.T
    planes = groups // SRC_DEV
    source_rows = STEPS * windows
    plane_bits = planes.bit_length() - 1

    records_other = exchange(records, 1, 0)
    choice, mask, take = pl.pallas_call(
        functools.partial(choice_kernel, halves, channels),
        out_shape=[
            jax.ShapeDtypeStruct((STEPS * SRC_DEV * halves, width), jnp.float32),
            jax.ShapeDtypeStruct((source_rows, width), jnp.float32),
            jax.ShapeDtypeStruct((plane_bits, source_rows, width), jnp.float32),
        ],
        in_specs=[SMEM] + [VMEM] * 2,
        out_specs=[VMEM] * 3,
        compiler_params=PARAMS,
        name="choose_rows",
    )(panel_ids, usable_rows, twiddle)

    def pick(flip):
        return pl.pallas_call(
            functools.partial(pick_kernel, flip),
            out_shape=jax.ShapeDtypeStruct((source_rows, length), records.dtype),
            in_specs=[VMEM] * 3,
            out_specs=VMEM,
            scratch_shapes=[pltpu.VMEM((source_rows, length), jnp.float32)],
            compiler_params=PARAMS,
            name="pick_rows",
        )(choice, records, records_other)

    came = exchange(pick(1), SRC_DEV * (planes // 2) + 1, 0)
    kept = pick(0)
    for index in range(plane_bits - 2, -1, -1):
        kept = jnp.where(take[index + 1][:, :1] > 0.0, came, kept)
        came = exchange(kept, SRC_DEV << index, 0)

    row_count = channels * windows
    pairs = len(order) * STEPS * channels
    receivers, inverse = pl.pallas_call(
        functools.partial(receiver_kernel, radius, order),
        out_shape=[
            jax.ShapeDtypeStruct((2 * row_count * blocks, width), jnp.bfloat16),
            jax.ShapeDtypeStruct((pairs, width), jnp.float32),
        ],
        in_specs=[SMEM] + [VMEM] * 4,
        out_specs=[VMEM] * 2,
        scratch_shapes=[
            pltpu.VMEM((row_count, length), jnp.float32),
            pltpu.VMEM((2 * row_count * blocks, width), jnp.float32),
        ],
        compiler_params=PARAMS,
        cost_estimate=AHEAD,
        name="receiver_spectra",
    )(panel_ids, usable_rows, records, twiddle, table)

    piece = pl.pallas_call(
        functools.partial(source_kernel, radius),
        out_shape=jax.ShapeDtypeStruct((2 * source_rows * blocks, width), jnp.bfloat16),
        in_specs=[VMEM] * 7,
        out_specs=VMEM,
        scratch_shapes=[pltpu.VMEM((2 * source_rows * blocks, width), jnp.float32)],
        compiler_params=PARAMS,
        name="source_spectra",
    )(take[0], mask, kept, came, twiddle, table, inverse)

    held = piece
    for bit in member_bits[:-1]:
        held = jnp.concatenate([held, exchange(held, 1, bit)], axis=0)
    brought = exchange(held, 1, member_bits[-1])
    held_other = exchange(held, 1, 0)
    brought_other = exchange(brought, 1, 0)

    def part(first, cost, *buffers):
        rows = sum(b.shape[0] for b in buffers) // (2 * windows * blocks) * channels
        return pl.pallas_call(
            functools.partial(part_kernel, windows, first),
            out_shape=jax.ShapeDtypeStruct((rows, NLAG), jnp.float32),
            in_specs=[VMEM] * (3 + len(buffers)),
            out_specs=VMEM,
            scratch_shapes=[
                pltpu.VMEM((2, rows * blocks, width), jnp.float32),
                pltpu.VMEM((rows, 2 * bin_count), jnp.bfloat16),
            ],
            compiler_params=PARAMS,
            cost_estimate=cost,
            name="correlate_part",
        )(inverse, receivers, ltable, *buffers)

    early = part(0, BESIDE, held, held_other)
    middle = part(pairs // 2, BESIDE, brought)
    rows = pairs // 4
    return pl.pallas_call(
        functools.partial(last_kernel, windows, order),
        out_shape=jax.ShapeDtypeStruct(
            (STEPS, members * SRC_DEV, channels, NLAG), jnp.bfloat16
        ),
        in_specs=[VMEM] * 6,
        out_specs=VMEM,
        scratch_shapes=[
            pltpu.VMEM((2, rows * blocks, width), jnp.float32),
            pltpu.VMEM((rows, 2 * bin_count), jnp.bfloat16),
        ],
        compiler_params=PARAMS,
        name="correlate_last",
    )(inverse, receivers, ltable, brought_other, early, middle)


def solution(mesh):
    placed = (P(AXES, None, None), P(), P())
    return jax.shard_map(
        on_device,
        mesh=mesh,
        in_specs=placed,
        out_specs=P(None, None, AXES, None),
        check_vma=False,
    )
```

```python
import functools
import math

import jax
import jax.numpy as jnp
import ml_dtypes
import numpy as np
from jax import lax
from jax.experimental import pallas as pl
from jax.experimental.pallas import tpu as pltpu
from jax.sharding import PartitionSpec as P

NLAG = 512
SRC_DEV = 2
STEPS = 2
RADIX = 16
AXES = ("grp", "dev")
SMEM = pl.BlockSpec(memory_space=pltpu.SMEM)
VMEM = pl.BlockSpec(memory_space=pltpu.VMEM)
AHEAD = pl.CostEstimate(flops=5_000_000_000, bytes_accessed=1_000_000, transcendentals=0)
BESIDE = pl.CostEstimate(flops=1_000_000_000, bytes_accessed=1_000_000, transcendentals=0)
PARAMS = pltpu.CompilerParams(vmem_limit_bytes=16 * 1024 * 1024)


def bin_order(bin_count):
    per = bin_count // RADIX
    order = []
    for q in range(RADIX // 2):
        for h in range(2):
            order.append(RADIX * np.arange(per) + 2 * q + h + 1)
    return np.concatenate(order)


def tables_kernel(length, table_ref, twiddle_ref):
    points = length // RADIX
    per = points // 2
    row = lax.broadcasted_iota(jnp.int32, (points, points), 0)
    lane = lax.broadcasted_iota(jnp.int32, (points, points), 1)
    phases = (2.0 * math.pi / points) * (row * (lane % per) % points).astype(jnp.float32)
    cosine, sine = jnp.cos(phases), jnp.sin(phases)
    for h in range(2):
        inside = (lane >= per) if h else (lane < per)
        c, s = jnp.where(inside, cosine, 0.0), jnp.where(inside, sine, 0.0)
        for part, values in enumerate(((c, -s), (s, c))):
            rows = slice((2 * h + part) * points, (2 * h + part + 1) * points)
            whole = jnp.concatenate(values, axis=1)
            high = whole.astype(jnp.bfloat16)
            table_ref[0, rows, :] = high
            table_ref[1, rows, :] = (whole - high.astype(jnp.float32)).astype(jnp.bfloat16)
    residue = lax.broadcasted_iota(jnp.int32, (RADIX, points), 0) + 1
    sample = lax.broadcasted_iota(jnp.int32, (RADIX, points), 1)
    phases = (2.0 * math.pi / length) * (residue * sample).astype(jnp.float32)
    twiddle_ref[0] = jnp.cos(phases)
    twiddle_ref[1] = -jnp.sin(phases)


def lag_table(length, bin_count, lag_count):
    bins = bin_order(bin_count)[:, None]
    lags = np.arange(lag_count)[None, :] - lag_count // 2
    phases = 2.0 * np.pi / length * (bins * lags % length)
    factor = 1.0 / math.sqrt(bin_count)
    cosine, sine = np.cos(phases) * factor, -np.sin(phases) * factor
    return np.concatenate([cosine, sine], axis=0).astype(ml_dtypes.bfloat16)


def real_dft(values):
    n = len(values)
    if n == 1:
        return [(values[0], None)]
    if n == 2:
        return [(values[0] + values[1], None), (values[0] - values[1], None)]
    even, odd = real_dft(values[0::2]), real_dft(values[1::2])
    quarter = n // 4
    out = [None] * (n // 2 + 1)
    for r in range(quarter + 1):
        (er, ei), (orr, oi) = even[r], odd[r]
        cosine, sine = math.cos(2 * math.pi * r / n), math.sin(2 * math.pi * r / n)
        if r == 0:
            tr, ti = orr, None
        elif r == quarter:
            tr, ti = None, -orr
        elif 8 * r == n:
            tr, ti = (orr + oi) * cosine, (oi - orr) * cosine
        else:
            tr, ti = orr * cosine + oi * sine, oi * cosine - orr * sine
        plus_re = er if tr is None else er + tr
        minus_re = er if tr is None else er - tr
        if ei is None:
            plus_im, minus_im = ti, ti
        elif ti is None:
            plus_im, minus_im = ei, -ei
        else:
            plus_im, minus_im = ei + ti, ti - ei
        out[r] = (plus_re, plus_im)
        if r < quarter:
            out[n // 2 - r] = (minus_re, minus_im)
    return out


def spectrum(samples, twiddle_ref, table_ref):
    rows, length = samples.shape
    points = length // RADIX
    half = real_dft([samples[:, i * points : (i + 1) * points] for i in range(RADIX)])
    lanes = []
    for residue in range(1, RADIX + 1):
        folded = min(residue, RADIX - residue)
        re, im = half[folded]
        if residue > RADIX // 2 and im is not None:
            im = -im
        cosine = twiddle_ref[0, residue - 1 : residue, :]
        sine = twiddle_ref[1, residue - 1 : residue, :]
        if im is None:
            lanes.append((re * cosine, re * sine))
        else:
            lanes.append((re * cosine - im * sine, re * sine + im * cosine))
    blocks = []
    for q in range(RADIX // 2):
        (ar, ai), (br, bi) = lanes[2 * q], lanes[2 * q + 1]
        blocks.append(jnp.concatenate([ar, ai, br, bi], axis=1))
    stacked = jnp.concatenate(blocks, axis=0)
    high = stacked.astype(jnp.bfloat16)
    low = (stacked - high.astype(jnp.float32)).astype(jnp.bfloat16)
    both = jnp.dot(
        jnp.concatenate([high, low], axis=0), table_ref[0], preferred_element_type=jnp.float32
    )
    count = stacked.shape[0]
    out = both[:count] + both[count:]
    out = out + jnp.dot(high, table_ref[1], preferred_element_type=jnp.float32)
    width = out.shape[1] // 2
    re = [out[q * rows : (q + 1) * rows, :width] for q in range(RADIX // 2)]
    im = [out[q * rows : (q + 1) * rows, width:] for q in range(RADIX // 2)]
    return re, im


def scales(re, im, radius, mask):
    amp = [jnp.sqrt(a * a + b * b) for a, b in zip(re, im)]
    rows, width = amp[0].shape
    per = width // 2
    reach = radius // RADIX
    lane = lax.broadcasted_iota(jnp.int32, (rows, width), 1)
    place = lane % per
    upper = lane >= per
    swapped = [pltpu.roll(a, per, 1) for a in amp]
    pair = [a + b for a, b in zip(amp, swapped)]
    total = pair[0]
    for value in pair[1:]:
        total = total + value

    def shifted(value, by):
        moved = pltpu.roll(value, (-by) % width, 1)
        inside = (place + by >= 0) & (place + by < per)
        return jnp.where(inside, moved, 0.0)

    centre = total
    for by in range(1, reach):
        centre = centre + shifted(total, by) + shifted(total, -by)
    before = jnp.zeros_like(total)
    out = []
    for a, b, both in zip(amp, swapped, pair):
        upto = before + a + jnp.where(upper, b, 0.0)
        before_here = before + jnp.where(upper, b, 0.0)
        onward = total - before_here
        before = before + both
        out.append((upto, onward))
    result = []
    for upto, onward in out:
        summed = centre + shifted(upto, reach) + shifted(onward, -reach)
        result.append(mask / (summed * (1.0 / (2 * radius + 1)) + 1e-06))
    return result


def whiten_rows(samples, radius, mask, twiddle_ref, table_ref, relay_ref, out_ref):
    rows = samples.shape[0]
    blocks = RADIX // 2
    re, im = spectrum(samples, twiddle_ref, table_ref)
    scale = scales(re, im, radius, mask)
    for part, values in enumerate((re, im)):
        for q in range(blocks):
            relay_ref[pl.ds(part * rows * blocks + q, rows, stride=blocks), :] = (
                values[q] * scale[q]
            )
    out_ref[...] = relay_ref[...].astype(jnp.bfloat16)


def holdings(member_bits):
    held = [(0, 0)]
    for bit in member_bits[:-1]:
        held += [(k ^ bit, 1 - odd) for k, odd in held]
    brought = [(k ^ member_bits[-1], 1 - odd) for k, odd in held]
    return held, brought


def panel_order(member_bits):
    held, brought = holdings(member_bits)
    flip = lambda pieces: [(k, 1 - odd) for k, odd in pieces]
    return held + flip(held) + brought + flip(brought)


def flags_of(picks, flags):
    return lax.dot_general(
        picks.astype(jnp.bfloat16),
        flags,
        (((1,), (1,)), ((), ())),
        preferred_element_type=jnp.float32,
    )


def at_window(rows_flags):
    row = lax.broadcasted_iota(jnp.int32, rows_flags.shape, 0)
    column = lax.broadcasted_iota(jnp.int32, rows_flags.shape, 1)
    kept = jnp.where(row % rows_flags.shape[1] == column, rows_flags, 0.0)
    return jnp.sum(kept, axis=1, keepdims=True)


def choice_kernel(halves, channels, ids_ref, usable_ref, after_ref, choice_ref, mask_ref, take_ref):
    del after_ref
    windows, total = usable_ref.shape
    members = lax.axis_size("dev")
    group, member = lax.axis_index("grp"), lax.axis_index("dev")
    core, plane = group % SRC_DEV, group // SRC_DEV
    flags = usable_ref[...].astype(jnp.float32).astype(jnp.bfloat16)
    owning = [ids_ref[t] // halves for t in range(STEPS)]
    within = [ids_ref[t] % halves for t in range(STEPS)]

    row = lax.broadcasted_iota(jnp.int32, choice_ref.shape, 0)
    choice = jnp.zeros(choice_ref.shape, jnp.float32)
    for t in range(STEPS):
        apart = (owning[t] + core) % SRC_DEV
        choice = jnp.where(row == (t * SRC_DEV + apart) * halves + within[t], 1.0, choice)
    choice_ref[...] = choice

    rows = STEPS * windows
    row = lax.broadcasted_iota(jnp.int32, (rows, total), 0)
    lane = lax.broadcasted_iota(jnp.int32, (rows, total), 1)
    picks = jnp.zeros((rows, total), jnp.float32)
    for t in range(STEPS):
        channel = (owning[t] * members + member) * channels + within[t] * SRC_DEV + core
        picks = jnp.where((row // windows == t) & (lane == channel), 1.0, picks)
    mask_ref[...] = jnp.broadcast_to(at_window(flags_of(picks, flags)), mask_ref.shape)

    row = lax.broadcasted_iota(jnp.int32, take_ref.shape[1:], 0)
    for index in range(take_ref.shape[0]):
        take = jnp.zeros(take_ref.shape[1:], jnp.float32)
        for t in range(STEPS):
            differs = ((owning[t] // SRC_DEV) ^ plane) >> index & 1
            take = jnp.where(row // windows == t, differs.astype(jnp.float32), take)
        take_ref[index] = take


def pick_kernel(flip, choice_ref, own_ref, other_ref, out_ref, samples):
    channels, windows, length = own_ref.shape
    halves = channels // SRC_DEV
    half = (lax.axis_index("grp") + flip) % SRC_DEV
    points = length // RADIX
    for step in range(STEPS):
        held = [jnp.zeros((windows, points), jnp.float32)] * RADIX
        for k, raw_ref in enumerate((own_ref, other_ref)):
            for h in range(halves):
                index = (step * SRC_DEV + k) * halves + h
                here = jnp.broadcast_to(choice_ref[index : index + 1, :], (windows, points)) > 0.0
                row = raw_ref[h * SRC_DEV + half].astype(jnp.float32)
                for n in range(RADIX):
                    held[n] = jnp.where(here, row[:, n * points : (n + 1) * points], held[n])
        for n in range(RADIX):
            samples[step * windows : (step + 1) * windows, n * points : (n + 1) * points] = held[n]
    out_ref[...] = samples[...].astype(out_ref.dtype)


def receiver_kernel(radius, order, ids_ref, usable_ref, raw_ref, twiddle_ref, table_ref, *rest):
    spectra_ref, inverse_ref, other_ref, samples, relay = rest
    channels, windows, _ = raw_ref.shape
    halves = channels // SRC_DEV
    members = lax.axis_size("dev")
    group, member = lax.axis_index("grp"), lax.axis_index("dev")
    core = group % SRC_DEV
    first = (group * members + member) * channels
    flags = usable_ref[...].astype(jnp.float32).astype(jnp.bfloat16)
    total = flags.shape[1]
    owning = [ids_ref[t] // halves for t in range(STEPS)]
    within = [ids_ref[t] % halves for t in range(STEPS)]

    for r in range(channels):
        samples[r * windows : (r + 1) * windows, :] = raw_ref[r].astype(jnp.float32)
    rows = channels * windows
    row = lax.broadcasted_iota(jnp.int32, (rows, total), 0)
    lane = lax.broadcasted_iota(jnp.int32, (rows, total), 1)
    own = jnp.where(lane == first + row // windows, 1.0, 0.0)
    mask = at_window(flags_of(own, flags))
    whiten_rows(samples[...], radius, mask, twiddle_ref, table_ref, relay, spectra_ref)

    rows = STEPS * channels
    row = lax.broadcasted_iota(jnp.int32, (rows, total), 0)
    lane = lax.broadcasted_iota(jnp.int32, (rows, total), 1)
    blocks = []
    for k, odd in order:
        picks = jnp.zeros((rows, total), jnp.float32)
        for t in range(STEPS):
            channel = (
                (owning[t] * members + (member ^ k)) * channels
                + within[t] * SRC_DEV
                + (core + odd) % SRC_DEV
            )
            picks = jnp.where((row // channels == t) & (lane == channel), 1.0, picks)
        blocks.append(picks)
    sent = flags_of(jnp.concatenate(blocks, axis=0), flags)
    theirs = ((group ^ 1) * members + (member ^ 1)) * channels
    for ref, start in ((inverse_ref, first), (other_ref, theirs)):
        received = flags_of(jnp.where(lane == start + row % channels, 1.0, 0.0), flags)
        both = sent * jnp.concatenate([received] * len(order), axis=0)
        counts = jnp.sum(both, axis=1, keepdims=True)
        ref[...] = jnp.broadcast_to(1.0 / jnp.maximum(counts, 1.0), ref.shape)


def source_kernel(radius, *refs):
    take_ref, mask_ref, kept_ref, came_ref, twiddle_ref, table_ref, spectra_ref = refs[:7]
    out_ref, passed_ref, relay = refs[7:]
    passed_ref[...] = spectra_ref[...]
    rows, length = kept_ref.shape
    points = length // RADIX
    here = take_ref[...] > 0.0
    kept, came = kept_ref[...].astype(jnp.float32), came_ref[...].astype(jnp.float32)
    here = jnp.concatenate([here] * RADIX, axis=1)
    samples = jnp.where(here, came, kept)
    whiten_rows(samples, radius, mask_ref[:, :1], twiddle_ref, table_ref, relay, out_ref)


def lagged_rows(windows, pieces, sets, table_ref, products, stacked):
    blocks = RADIX // 2

    def row_set(ref, base, first, rows):
        out = []
        for part in range(2):
            held = []
            for w in range(0, windows, 2):
                start = base + (part * rows + first + w) * blocks
                both = ref[start : start + 2 * blocks, :].astype(jnp.float32)
                held += [both[:blocks], both[blocks:]]
            out.append(held)
        return out

    pair = 0
    for recv_ref, _ in sets:
        receivers = recv_ref.shape[0] // (2 * windows * blocks)
        own = [row_set(recv_ref, 0, r * windows, receivers * windows) for r in range(receivers)]
        for ref, base in pieces:
            for step in range(STEPS):
                a, b = row_set(ref, base, step * windows, STEPS * windows)
                for r in range(receivers):
                    c, e = own[r]
                    re = im = None
                    for w in range(windows):
                        re_w = a[w] * c[w] + b[w] * e[w]
                        im_w = b[w] * c[w] - a[w] * e[w]
                        re = re_w if re is None else re + re_w
                        im = im_w if im is None else im + im_w
                    products[0, pair * blocks : (pair + 1) * blocks, :] = re
                    products[1, pair * blocks : (pair + 1) * blocks, :] = im
                    pair += 1
    width = products.shape[2]
    inverse = jnp.concatenate([factors for _, factors in sets], axis=0)
    for part in range(2):
        for q in range(blocks):
            column = (part * blocks + q) * width
            values = products[part, pl.ds(q, pair, stride=blocks), :] * inverse
            stacked[:, column : column + width] = values.astype(jnp.bfloat16)
    return jnp.dot(stacked[...], table_ref[...], preferred_element_type=jnp.float32)


def pieces_of(ref, windows):
    rows = 2 * STEPS * windows * (RADIX // 2)
    return [(ref, base) for base in range(0, ref.shape[0], rows)]


def part_kernel(windows, first, n_sets, *refs):
    table_ref, set_refs, refs = refs[0], refs[1 : 1 + 2 * n_sets], refs[1 + 2 * n_sets :]
    products, stacked = refs[-2:]
    buffers, outs = refs[: -2 - n_sets], refs[-2 - n_sets : -2]
    pieces = [piece for ref in buffers for piece in pieces_of(ref, windows)]
    rows = outs[0].shape[0]
    sets = [
        (set_refs[2 * i], set_refs[2 * i + 1][first : first + rows, :]) for i in range(n_sets)
    ]
    lagged = lagged_rows(windows, pieces, sets, table_ref, products, stacked)
    for i, out_ref in enumerate(outs):
        out_ref[...] = lagged[i * rows : (i + 1) * rows].astype(jnp.bfloat16)


def pass_kernel(value_ref, after_ref, out_ref):
    del after_ref
    out_ref[...] = value_ref[...]


def place_kernel(order, *refs):
    out_ref = refs[-1]
    member = lax.axis_index("dev")
    core = lax.axis_index("grp") % SRC_DEV
    receivers = out_ref.shape[2]
    whole = order + [(k ^ 1, 1 - odd) for k, odd in order]
    block = STEPS * receivers
    done = 0
    for ref in refs[:-1]:
        for p in range(ref.shape[0] // block):
            k, odd = whole[done]
            source = (member ^ k) * SRC_DEV + (core + odd) % SRC_DEV
            for step in range(STEPS):
                row = p * block + step * receivers
                out_ref[step, source] = ref[row : row + receivers, :]
            done += 1


def on_device(records, usable, panel_ids):
    channels, windows, length = records.shape
    bin_count = length // 2
    radius = bin_count // 16
    halves = channels // SRC_DEV
    groups = lax.axis_size("grp")
    members = lax.axis_size("dev")
    blocks = RADIX // 2
    width = bin_count // blocks

    def exchange(value, group_bit, member_bit):
        flip = group_bit * members + member_bit
        pairs = [(i, i ^ flip) for i in range(groups * members)]
        return lax.ppermute(value, AXES, pairs)

    points = length // RADIX
    table, twiddle = pl.pallas_call(
        functools.partial(tables_kernel, length),
        out_shape=[
            jax.ShapeDtypeStruct((2, 4 * points, 2 * points), jnp.bfloat16),
            jax.ShapeDtypeStruct((2, RADIX, points), jnp.float32),
        ],
        in_specs=[],
        out_specs=[VMEM] * 2,
        compiler_params=PARAMS,
        cost_estimate=AHEAD,
        name="short_tables",
    )()
    ltable = jnp.asarray(lag_table(length, bin_count, NLAG))
    member_bits = []
    bit = members // 2
    while bit:
        member_bits.append(bit)
        bit //= 2
    order = panel_order(member_bits[:-1])

    usable_rows = usable.T
    planes = groups // SRC_DEV
    source_rows = STEPS * windows
    plane_bits = planes.bit_length() - 1

    records_other = exchange(records, 1, 0)
    choice, mask, take = pl.pallas_call(
        functools.partial(choice_kernel, halves, channels),
        out_shape=[
            jax.ShapeDtypeStruct((STEPS * SRC_DEV * halves, width), jnp.float32),
            jax.ShapeDtypeStruct((source_rows, width), jnp.float32),
            jax.ShapeDtypeStruct((plane_bits, source_rows, width), jnp.float32),
        ],
        in_specs=[SMEM] + [VMEM] * 2,
        out_specs=[VMEM] * 3,
        compiler_params=PARAMS,
        name="choose_rows",
    )(panel_ids, usable_rows, twiddle)

    def pick(flip):
        return pl.pallas_call(
            functools.partial(pick_kernel, flip),
            out_shape=jax.ShapeDtypeStruct((source_rows, length), records.dtype),
            in_specs=[VMEM] * 3,
            out_specs=VMEM,
            scratch_shapes=[pltpu.VMEM((source_rows, length), jnp.float32)],
            compiler_params=PARAMS,
            name="pick_rows",
        )(choice, records, records_other)

    came = exchange(pick(1), SRC_DEV * (planes // 2) + 1, 0)
    kept = pick(0)
    for index in range(plane_bits - 2, -1, -1):
        kept = jnp.where(take[index + 1][:, :1] > 0.0, came, kept)
        came = exchange(kept, SRC_DEV << index, 0)

    row_count = channels * windows
    pairs = len(order) * STEPS * channels
    receivers, inverse, inverse_theirs = pl.pallas_call(
        functools.partial(receiver_kernel, radius, order),
        out_shape=[
            jax.ShapeDtypeStruct((2 * row_count * blocks, width), jnp.bfloat16),
            jax.ShapeDtypeStruct((pairs, width), jnp.float32),
            jax.ShapeDtypeStruct((pairs, width), jnp.float32),
        ],
        in_specs=[SMEM] + [VMEM] * 4,
        out_specs=[VMEM] * 3,
        scratch_shapes=[
            pltpu.VMEM((row_count, length), jnp.float32),
            pltpu.VMEM((2 * row_count * blocks, width), jnp.float32),
        ],
        compiler_params=PARAMS,
        cost_estimate=AHEAD,
        name="receiver_spectra",
    )(panel_ids, usable_rows, records, twiddle, table)

    piece, passed = pl.pallas_call(
        functools.partial(source_kernel, radius),
        out_shape=[
            jax.ShapeDtypeStruct((2 * source_rows * blocks, width), jnp.bfloat16),
            jax.ShapeDtypeStruct(receivers.shape, receivers.dtype),
        ],
        in_specs=[VMEM] * 7,
        out_specs=[VMEM] * 2,
        scratch_shapes=[pltpu.VMEM((2 * source_rows * blocks, width), jnp.float32)],
        compiler_params=PARAMS,
        name="source_spectra",
    )(take[0], mask, kept, came, twiddle, table, receivers)

    held = piece
    for bit in member_bits[:-2]:
        held = jnp.concatenate([held, exchange(held, 1, bit)], axis=0)
    theirs = exchange(passed, 1, 1)
    held_other = exchange(held, 1, 0)

    def part(first, sets, *buffers):
        rows = sum(b.shape[0] for b in buffers) // (2 * windows * blocks) * channels
        total = rows * len(sets)
        return pl.pallas_call(
            functools.partial(part_kernel, windows, first, len(sets)),
            out_shape=[jax.ShapeDtypeStruct((rows, NLAG), jnp.bfloat16)] * len(sets),
            in_specs=[VMEM] * (1 + 2 * len(sets) + len(buffers)),
            out_specs=[VMEM] * len(sets),
            scratch_shapes=[
                pltpu.VMEM((2, total * blocks, width), jnp.float32),
                pltpu.VMEM((total, 2 * bin_count), jnp.bfloat16),
            ],
            compiler_params=PARAMS,
            cost_estimate=BESIDE,
            name="correlate_part",
        )(ltable, *[array for pair in sets for array in pair], *buffers)

    mine, other = (receivers, inverse), (theirs, inverse_theirs)
    early_theirs, early = part(0, [other, mine], held, held_other)
    brought = exchange(held, 1, member_bits[-2])
    brought = pl.pallas_call(
        pass_kernel,
        out_shape=jax.ShapeDtypeStruct(brought.shape, brought.dtype),
        in_specs=[VMEM] * 2,
        out_specs=VMEM,
        compiler_params=PARAMS,
        name="pass_on",
    )(brought, early_theirs)
    brought_other = exchange(brought, 1, 0)
    (middle_theirs,) = part(pairs // 2, [other], brought)
    (late_theirs,) = part(pairs // 4 * 3, [other], brought_other)
    (late,) = part(pairs // 2, [mine], brought, brought_other)
    back = exchange(jnp.concatenate([early_theirs, middle_theirs, late_theirs], axis=0), 1, 1)
    return pl.pallas_call(
        functools.partial(place_kernel, order),
        out_shape=jax.ShapeDtypeStruct(
            (STEPS, members * SRC_DEV, channels, NLAG), jnp.bfloat16
        ),
        in_specs=[VMEM] * 3,
        out_specs=VMEM,
        compiler_params=PARAMS,
        name="place_rows",
    )(early, late, back)


def solution(mesh):
    placed = (P(AXES, None, None), P(), P())
    return jax.shard_map(
        on_device,
        mesh=mesh,
        in_specs=placed,
        out_specs=P(None, None, AXES, None),
        check_vma=False,
    )
```

```python
import functools
import math

import jax
import jax.numpy as jnp
import ml_dtypes
import numpy as np
from jax import lax
from jax.experimental import pallas as pl
from jax.experimental.pallas import tpu as pltpu
from jax.sharding import PartitionSpec as P

NLAG = 512
SRC_DEV = 2
STEPS = 2
RADIX = 16
AXES = ("grp", "dev")
SMEM = pl.BlockSpec(memory_space=pltpu.SMEM)
VMEM = pl.BlockSpec(memory_space=pltpu.VMEM)
AHEAD = pl.CostEstimate(flops=5_000_000_000, bytes_accessed=1_000_000, transcendentals=0)
BESIDE = pl.CostEstimate(flops=1_000_000_000, bytes_accessed=1_000_000, transcendentals=0)
PARAMS = pltpu.CompilerParams(vmem_limit_bytes=16 * 1024 * 1024)


def bin_order(bin_count):
    per = bin_count // RADIX
    order = []
    for q in range(RADIX // 2):
        for h in range(2):
            order.append(RADIX * np.arange(per) + 2 * q + h + 1)
    return np.concatenate(order)


def tables_kernel(length, after_ref, table_ref, twiddle_ref):
    del after_ref
    points = length // RADIX
    per = points // 2
    row = lax.broadcasted_iota(jnp.int32, (points, points), 0)
    lane = lax.broadcasted_iota(jnp.int32, (points, points), 1)
    phases = (2.0 * math.pi / points) * (row * (lane % per) % points).astype(jnp.float32)
    cosine, sine = jnp.cos(phases), jnp.sin(phases)
    for h in range(2):
        inside = (lane >= per) if h else (lane < per)
        c, s = jnp.where(inside, cosine, 0.0), jnp.where(inside, sine, 0.0)
        for part, values in enumerate(((c, -s), (s, c))):
            rows = slice((2 * h + part) * points, (2 * h + part + 1) * points)
            whole = jnp.concatenate(values, axis=1)
            high = whole.astype(jnp.bfloat16)
            table_ref[0, rows, :] = high
            table_ref[1, rows, :] = (whole - high.astype(jnp.float32)).astype(jnp.bfloat16)
    residue = lax.broadcasted_iota(jnp.int32, (RADIX, points), 0) + 1
    sample = lax.broadcasted_iota(jnp.int32, (RADIX, points), 1)
    phases = (2.0 * math.pi / length) * (residue * sample).astype(jnp.float32)
    twiddle_ref[0] = jnp.cos(phases)
    twiddle_ref[1] = -jnp.sin(phases)


def lag_table(length, bin_count, lag_count):
    bins = bin_order(bin_count)[:, None]
    lags = np.arange(lag_count)[None, :] - lag_count // 2
    phases = 2.0 * np.pi / length * (bins * lags % length)
    factor = 1.0 / math.sqrt(bin_count)
    cosine, sine = np.cos(phases) * factor, -np.sin(phases) * factor
    return np.concatenate([cosine, sine], axis=0).astype(ml_dtypes.bfloat16)


def real_dft(values):
    n = len(values)
    if n == 1:
        return [(values[0], None)]
    if n == 2:
        return [(values[0] + values[1], None), (values[0] - values[1], None)]
    even, odd = real_dft(values[0::2]), real_dft(values[1::2])
    quarter = n // 4
    out = [None] * (n // 2 + 1)
    for r in range(quarter + 1):
        (er, ei), (orr, oi) = even[r], odd[r]
        cosine, sine = math.cos(2 * math.pi * r / n), math.sin(2 * math.pi * r / n)
        if r == 0:
            tr, ti = orr, None
        elif r == quarter:
            tr, ti = None, -orr
        elif 8 * r == n:
            tr, ti = (orr + oi) * cosine, (oi - orr) * cosine
        else:
            tr, ti = orr * cosine + oi * sine, oi * cosine - orr * sine
        plus_re = er if tr is None else er + tr
        minus_re = er if tr is None else er - tr
        if ei is None:
            plus_im, minus_im = ti, ti
        elif ti is None:
            plus_im, minus_im = ei, -ei
        else:
            plus_im, minus_im = ei + ti, ti - ei
        out[r] = (plus_re, plus_im)
        if r < quarter:
            out[n // 2 - r] = (minus_re, minus_im)
    return out


def spectrum(samples, twiddle_ref, table_ref):
    rows, length = samples.shape
    points = length // RADIX
    half = real_dft([samples[:, i * points : (i + 1) * points] for i in range(RADIX)])
    lanes = []
    for residue in range(1, RADIX + 1):
        folded = min(residue, RADIX - residue)
        re, im = half[folded]
        if residue > RADIX // 2 and im is not None:
            im = -im
        cosine = twiddle_ref[0, residue - 1 : residue, :]
        sine = twiddle_ref[1, residue - 1 : residue, :]
        if im is None:
            lanes.append((re * cosine, re * sine))
        else:
            lanes.append((re * cosine - im * sine, re * sine + im * cosine))
    blocks = []
    for q in range(RADIX // 2):
        (ar, ai), (br, bi) = lanes[2 * q], lanes[2 * q + 1]
        blocks.append(jnp.concatenate([ar, ai, br, bi], axis=1))
    stacked = jnp.concatenate(blocks, axis=0)
    high = stacked.astype(jnp.bfloat16)
    low = (stacked - high.astype(jnp.float32)).astype(jnp.bfloat16)
    both = jnp.dot(
        jnp.concatenate([high, low], axis=0), table_ref[0], preferred_element_type=jnp.float32
    )
    count = stacked.shape[0]
    out = both[:count] + both[count:]
    out = out + jnp.dot(high, table_ref[1], preferred_element_type=jnp.float32)
    width = out.shape[1] // 2
    re = [out[q * rows : (q + 1) * rows, :width] for q in range(RADIX // 2)]
    im = [out[q * rows : (q + 1) * rows, width:] for q in range(RADIX // 2)]
    return re, im


def scales(re, im, radius, mask):
    amp = [jnp.sqrt(a * a + b * b) for a, b in zip(re, im)]
    rows, width = amp[0].shape
    per = width // 2
    reach = radius // RADIX
    lane = lax.broadcasted_iota(jnp.int32, (rows, width), 1)
    place = lane % per
    upper = lane >= per
    swapped = [pltpu.roll(a, per, 1) for a in amp]
    pair = [a + b for a, b in zip(amp, swapped)]
    total = pair[0]
    for value in pair[1:]:
        total = total + value

    def shifted(value, by):
        moved = pltpu.roll(value, (-by) % width, 1)
        inside = (place + by >= 0) & (place + by < per)
        return jnp.where(inside, moved, 0.0)

    centre = total
    for by in range(1, reach):
        centre = centre + shifted(total, by) + shifted(total, -by)
    before = jnp.zeros_like(total)
    out = []
    for a, b, both in zip(amp, swapped, pair):
        upto = before + a + jnp.where(upper, b, 0.0)
        before_here = before + jnp.where(upper, b, 0.0)
        onward = total - before_here
        before = before + both
        out.append((upto, onward))
    result = []
    for upto, onward in out:
        summed = centre + shifted(upto, reach) + shifted(onward, -reach)
        result.append(mask / (summed * (1.0 / (2 * radius + 1)) + 1e-06))
    return result


def whiten_rows(samples, radius, mask, twiddle_ref, table_ref, relay_ref, out_ref):
    rows = samples.shape[0]
    blocks = RADIX // 2
    re, im = spectrum(samples, twiddle_ref, table_ref)
    scale = scales(re, im, radius, mask)
    for part, values in enumerate((re, im)):
        for q in range(blocks):
            relay_ref[pl.ds(part * rows * blocks + q, rows, stride=blocks), :] = (
                values[q] * scale[q]
            )
    out_ref[...] = relay_ref[...].astype(jnp.bfloat16)


def holdings(member_bits):
    held = [(0, 0)]
    for bit in member_bits[:-1]:
        held += [(k ^ bit, 1 - odd) for k, odd in held]
    brought = [(k ^ member_bits[-1], 1 - odd) for k, odd in held]
    return held, brought


def panel_order(member_bits):
    held, brought = holdings(member_bits)
    flip = lambda pieces: [(k, 1 - odd) for k, odd in pieces]
    return held + flip(held) + brought + flip(brought)


def flags_of(picks, flags):
    return lax.dot_general(
        picks.astype(jnp.bfloat16),
        flags,
        (((1,), (1,)), ((), ())),
        preferred_element_type=jnp.float32,
    )


def at_window(rows_flags):
    row = lax.broadcasted_iota(jnp.int32, rows_flags.shape, 0)
    column = lax.broadcasted_iota(jnp.int32, rows_flags.shape, 1)
    kept = jnp.where(row % rows_flags.shape[1] == column, rows_flags, 0.0)
    return jnp.sum(kept, axis=1, keepdims=True)


def first_kernel(out_ref):
    out_ref[...] = jnp.zeros_like(out_ref)


def choice_kernel(halves, channels, ids_ref, usable_ref, after_ref, *outs):
    del after_ref
    choice_ref, mask_ref, take_ref, info_ref = outs
    windows, total = usable_ref.shape
    members = lax.axis_size("dev")
    group, member = lax.axis_index("grp"), lax.axis_index("dev")
    core, plane = group % SRC_DEV, group // SRC_DEV
    flags = usable_ref[...].astype(jnp.float32).astype(jnp.bfloat16)
    owning = [ids_ref[t] // halves for t in range(STEPS)]
    within = [ids_ref[t] % halves for t in range(STEPS)]

    row = lax.broadcasted_iota(jnp.int32, choice_ref.shape, 0)
    choice = jnp.zeros(choice_ref.shape, jnp.float32)
    for t in range(STEPS):
        apart = (owning[t] + core) % SRC_DEV
        choice = jnp.where(row == (t * SRC_DEV + apart) * halves + within[t], 1.0, choice)
    choice_ref[...] = choice

    row = lax.broadcasted_iota(jnp.int32, info_ref.shape, 0)
    info = jnp.zeros(info_ref.shape, jnp.int32)
    for t in range(STEPS):
        start = owning[t] * members * channels + within[t] * SRC_DEV
        info = jnp.where(row == t, start, info)
    info_ref[...] = info

    rows = STEPS * windows
    row = lax.broadcasted_iota(jnp.int32, (rows, total), 0)
    lane = lax.broadcasted_iota(jnp.int32, (rows, total), 1)
    picks = jnp.zeros((rows, total), jnp.float32)
    for t in range(STEPS):
        channel = (owning[t] * members + member) * channels + within[t] * SRC_DEV + core
        picks = jnp.where((row // windows == t) & (lane == channel), 1.0, picks)
    mask_ref[...] = jnp.broadcast_to(at_window(flags_of(picks, flags)), mask_ref.shape)

    row = lax.broadcasted_iota(jnp.int32, take_ref.shape[1:], 0)
    for index in range(take_ref.shape[0]):
        take = jnp.zeros(take_ref.shape[1:], jnp.float32)
        for t in range(STEPS):
            differs = ((owning[t] // SRC_DEV) ^ plane) >> index & 1
            take = jnp.where(row // windows == t, differs.astype(jnp.float32), take)
        take_ref[index] = take


def pick_kernel(flip, choice_ref, own_ref, other_ref, out_ref, samples):
    channels, windows, length = own_ref.shape
    halves = channels // SRC_DEV
    half = (lax.axis_index("grp") + flip) % SRC_DEV
    points = length // RADIX
    for step in range(STEPS):
        held = [jnp.zeros((windows, points), jnp.float32)] * RADIX
        for k, raw_ref in enumerate((own_ref, other_ref)):
            for h in range(halves):
                index = (step * SRC_DEV + k) * halves + h
                here = jnp.broadcast_to(choice_ref[index : index + 1, :], (windows, points)) > 0.0
                row = raw_ref[h * SRC_DEV + half].astype(jnp.float32)
                for n in range(RADIX):
                    held[n] = jnp.where(here, row[:, n * points : (n + 1) * points], held[n])
        for n in range(RADIX):
            samples[step * windows : (step + 1) * windows, n * points : (n + 1) * points] = held[n]
    out_ref[...] = samples[...].astype(out_ref.dtype)


def receiver_kernel(radius, order, info_ref, usable_ref, raw_ref, twiddle_ref, table_ref, *rest):
    spectra_ref, inverse_ref, other_ref, samples, relay = rest
    channels, windows, _ = raw_ref.shape
    members = lax.axis_size("dev")
    group, member = lax.axis_index("grp"), lax.axis_index("dev")
    core = group % SRC_DEV
    first = (group * members + member) * channels
    flags = usable_ref[...].astype(jnp.float32).astype(jnp.bfloat16)
    total = flags.shape[1]

    for r in range(channels):
        samples[r * windows : (r + 1) * windows, :] = raw_ref[r].astype(jnp.float32)
    rows = channels * windows
    row = lax.broadcasted_iota(jnp.int32, (rows, total), 0)
    lane = lax.broadcasted_iota(jnp.int32, (rows, total), 1)
    own = jnp.where(lane == first + row // windows, 1.0, 0.0)
    mask = at_window(flags_of(own, flags))
    whiten_rows(samples[...], radius, mask, twiddle_ref, table_ref, relay, spectra_ref)

    rows = STEPS * channels
    row = lax.broadcasted_iota(jnp.int32, (rows, total), 0)
    lane = lax.broadcasted_iota(jnp.int32, (rows, total), 1)
    start = jnp.zeros((rows, total), jnp.int32)
    for t in range(STEPS):
        here = jnp.broadcast_to(info_ref[t : t + 1, :1], (rows, total))
        start = jnp.where(row // channels == t, here, start)
    blocks = []
    for k, odd in order:
        offset = (member ^ k) * channels + (core + odd) % SRC_DEV
        blocks.append(jnp.where(lane == start + offset, 1.0, 0.0))
    sent = flags_of(jnp.concatenate(blocks, axis=0), flags)
    theirs = ((group ^ 1) * members + (member ^ 1)) * channels
    for ref, start in ((inverse_ref, first), (other_ref, theirs)):
        received = flags_of(jnp.where(lane == start + row % channels, 1.0, 0.0), flags)
        both = sent * jnp.concatenate([received] * len(order), axis=0)
        counts = jnp.sum(both, axis=1, keepdims=True)
        ref[...] = jnp.broadcast_to(1.0 / jnp.maximum(counts, 1.0), ref.shape)


def source_kernel(radius, *refs):
    take_ref, mask_ref, kept_ref, came_ref, twiddle_ref, table_ref, spectra_ref = refs[:7]
    out_ref, passed_ref, relay = refs[7:]
    passed_ref[...] = spectra_ref[...]
    rows, length = kept_ref.shape
    points = length // RADIX
    here = take_ref[...] > 0.0
    kept, came = kept_ref[...].astype(jnp.float32), came_ref[...].astype(jnp.float32)
    here = jnp.concatenate([here] * RADIX, axis=1)
    samples = jnp.where(here, came, kept)
    whiten_rows(samples, radius, mask_ref[:, :1], twiddle_ref, table_ref, relay, out_ref)


def lagged_rows(windows, pieces, sets, table_ref, products, stacked):
    blocks = RADIX // 2

    def row_set(ref, base, first, rows):
        out = []
        for part in range(2):
            held = []
            for w in range(0, windows, 2):
                start = base + (part * rows + first + w) * blocks
                both = ref[start : start + 2 * blocks, :].astype(jnp.float32)
                held += [both[:blocks], both[blocks:]]
            out.append(held)
        return out

    pair = 0
    for recv_ref, _ in sets:
        receivers = recv_ref.shape[0] // (2 * windows * blocks)
        own = [row_set(recv_ref, 0, r * windows, receivers * windows) for r in range(receivers)]
        for ref, base in pieces:
            for step in range(STEPS):
                a, b = row_set(ref, base, step * windows, STEPS * windows)
                for r in range(receivers):
                    c, e = own[r]
                    re = im = None
                    for w in range(windows):
                        re_w = a[w] * c[w] + b[w] * e[w]
                        im_w = b[w] * c[w] - a[w] * e[w]
                        re = re_w if re is None else re + re_w
                        im = im_w if im is None else im + im_w
                    products[0, pair * blocks : (pair + 1) * blocks, :] = re
                    products[1, pair * blocks : (pair + 1) * blocks, :] = im
                    pair += 1
    width = products.shape[2]
    inverse = jnp.concatenate([factors for _, factors in sets], axis=0)
    for part in range(2):
        for q in range(blocks):
            column = (part * blocks + q) * width
            values = products[part, pl.ds(q, pair, stride=blocks), :] * inverse
            stacked[:, column : column + width] = values.astype(jnp.bfloat16)
    return jnp.dot(stacked[...], table_ref[...], preferred_element_type=jnp.float32)


def pieces_of(ref, windows):
    rows = 2 * STEPS * windows * (RADIX // 2)
    return [(ref, base) for base in range(0, ref.shape[0], rows)]


def part_kernel(windows, first, n_sets, *refs):
    table_ref, set_refs, refs = refs[0], refs[1 : 1 + 2 * n_sets], refs[1 + 2 * n_sets :]
    products, stacked = refs[-2:]
    buffers, outs = refs[: -2 - n_sets], refs[-2 - n_sets : -2]
    pieces = [piece for ref in buffers for piece in pieces_of(ref, windows)]
    rows = outs[0].shape[0]
    sets = [
        (set_refs[2 * i], set_refs[2 * i + 1][first : first + rows, :]) for i in range(n_sets)
    ]
    lagged = lagged_rows(windows, pieces, sets, table_ref, products, stacked)
    for i, out_ref in enumerate(outs):
        out_ref[...] = lagged[i * rows : (i + 1) * rows].astype(jnp.bfloat16)


def pass_kernel(value_ref, after_ref, out_ref):
    del after_ref
    out_ref[...] = value_ref[...]


def place_kernel(order, *refs):
    out_ref = refs[-1]
    member = lax.axis_index("dev")
    core = lax.axis_index("grp") % SRC_DEV
    receivers = out_ref.shape[2]
    whole = order + [(k ^ 1, 1 - odd) for k, odd in order]
    block = STEPS * receivers
    done = 0
    for ref in refs[:-1]:
        for p in range(ref.shape[0] // block):
            k, odd = whole[done]
            source = (member ^ k) * SRC_DEV + (core + odd) % SRC_DEV
            for step in range(STEPS):
                row = p * block + step * receivers
                out_ref[step, source] = ref[row : row + receivers, :]
            done += 1


def on_device(records, usable, panel_ids):
    channels, windows, length = records.shape
    bin_count = length // 2
    radius = bin_count // 16
    halves = channels // SRC_DEV
    groups = lax.axis_size("grp")
    members = lax.axis_size("dev")
    blocks = RADIX // 2
    width = bin_count // blocks

    def exchange(value, group_bit, member_bit):
        flip = group_bit * members + member_bit
        pairs = [(i, i ^ flip) for i in range(groups * members)]
        return lax.ppermute(value, AXES, pairs)

    ltable = jnp.asarray(lag_table(length, bin_count, NLAG))
    member_bits = []
    bit = members // 2
    while bit:
        member_bits.append(bit)
        bit //= 2
    order = panel_order(member_bits[:-1])

    usable_rows = usable.T
    planes = groups // SRC_DEV
    source_rows = STEPS * windows
    plane_bits = planes.bit_length() - 1

    records_other = exchange(records, 1, 0)
    ahead = pl.pallas_call(
        first_kernel,
        out_shape=jax.ShapeDtypeStruct((8, width), jnp.float32),
        in_specs=[],
        out_specs=VMEM,
        compiler_params=PARAMS,
        cost_estimate=AHEAD,
        name="ahead",
    )()
    choice, mask, take, info = pl.pallas_call(
        functools.partial(choice_kernel, halves, channels),
        out_shape=[
            jax.ShapeDtypeStruct((STEPS * SRC_DEV * halves, width), jnp.float32),
            jax.ShapeDtypeStruct((source_rows, width), jnp.float32),
            jax.ShapeDtypeStruct((plane_bits, source_rows, width), jnp.float32),
            jax.ShapeDtypeStruct((8, width), jnp.int32),
        ],
        in_specs=[SMEM] + [VMEM] * 2,
        out_specs=[VMEM] * 4,
        compiler_params=PARAMS,
        name="choose_rows",
    )(panel_ids, usable_rows, ahead)

    def pick(flip):
        return pl.pallas_call(
            functools.partial(pick_kernel, flip),
            out_shape=jax.ShapeDtypeStruct((source_rows, length), records.dtype),
            in_specs=[VMEM] * 3,
            out_specs=VMEM,
            scratch_shapes=[pltpu.VMEM((source_rows, length), jnp.float32)],
            compiler_params=PARAMS,
            name="pick_rows",
        )(choice, records, records_other)

    sent = pick(1)
    came = exchange(sent, SRC_DEV * (planes // 2) + 1, 0)
    kept = pick(0)
    for index in range(plane_bits - 2, -1, -1):
        kept = jnp.where(take[index + 1][:, :1] > 0.0, came, kept)
        came = exchange(kept, SRC_DEV << index, 0)

    points = length // RADIX
    table, twiddle = pl.pallas_call(
        functools.partial(tables_kernel, length),
        out_shape=[
            jax.ShapeDtypeStruct((2, 4 * points, 2 * points), jnp.bfloat16),
            jax.ShapeDtypeStruct((2, RADIX, points), jnp.float32),
        ],
        in_specs=[VMEM],
        out_specs=[VMEM] * 2,
        compiler_params=PARAMS,
        cost_estimate=AHEAD,
        name="short_tables",
    )(sent)

    row_count = channels * windows
    pairs = len(order) * STEPS * channels
    receivers, inverse, inverse_theirs = pl.pallas_call(
        functools.partial(receiver_kernel, radius, order),
        out_shape=[
            jax.ShapeDtypeStruct((2 * row_count * blocks, width), jnp.bfloat16),
            jax.ShapeDtypeStruct((pairs, width), jnp.float32),
            jax.ShapeDtypeStruct((pairs, width), jnp.float32),
        ],
        in_specs=[VMEM] * 5,
        out_specs=[VMEM] * 3,
        scratch_shapes=[
            pltpu.VMEM((row_count, length), jnp.float32),
            pltpu.VMEM((2 * row_count * blocks, width), jnp.float32),
        ],
        compiler_params=PARAMS,
        cost_estimate=AHEAD,
        name="receiver_spectra",
    )(info, usable_rows, records, twiddle, table)

    piece, passed = pl.pallas_call(
        functools.partial(source_kernel, radius),
        out_shape=[
            jax.ShapeDtypeStruct((2 * source_rows * blocks, width), jnp.bfloat16),
            jax.ShapeDtypeStruct(receivers.shape, receivers.dtype),
        ],
        in_specs=[VMEM] * 7,
        out_specs=[VMEM] * 2,
        scratch_shapes=[pltpu.VMEM((2 * source_rows * blocks, width), jnp.float32)],
        compiler_params=PARAMS,
        name="source_spectra",
    )(take[0], mask, kept, came, twiddle, table, receivers)

    held = piece
    for bit in member_bits[:-2]:
        held = jnp.concatenate([held, exchange(held, 1, bit)], axis=0)
    theirs = exchange(passed, 1, 1)

    def pass_on(value, after):
        return pl.pallas_call(
            pass_kernel,
            out_shape=jax.ShapeDtypeStruct(value.shape, value.dtype),
            in_specs=[VMEM] * 2,
            out_specs=VMEM,
            compiler_params=PARAMS,
            name="pass_on",
        )(value, after)

    def part(first, sets, *buffers):
        rows = sum(b.shape[0] for b in buffers) // (2 * windows * blocks) * channels
        total = rows * len(sets)
        return pl.pallas_call(
            functools.partial(part_kernel, windows, first, len(sets)),
            out_shape=[jax.ShapeDtypeStruct((rows, NLAG), jnp.bfloat16)] * len(sets),
            in_specs=[VMEM] * (1 + 2 * len(sets) + len(buffers)),
            out_specs=[VMEM] * len(sets),
            scratch_shapes=[
                pltpu.VMEM((2, total * blocks, width), jnp.float32),
                pltpu.VMEM((total, 2 * bin_count), jnp.bfloat16),
            ],
            compiler_params=PARAMS,
            cost_estimate=BESIDE,
            name="correlate_part",
        )(ltable, *[array for pair in sets for array in pair], *buffers)

    mine, other = (receivers, inverse), (theirs, inverse_theirs)
    brought = exchange(held, 1, member_bits[-2])
    held_other = exchange(pass_on(held, theirs), 1, 0)
    early_theirs, early = part(0, [other, mine], held)
    (next_theirs,) = part(pairs // 4, [other], held_other)
    brought = pass_on(brought, next_theirs)
    brought_other = exchange(brought, 1, 0)
    (middle_theirs,) = part(pairs // 2, [other], brought)
    (late_theirs,) = part(pairs // 4 * 3, [other], brought_other)
    (late,) = part(pairs // 4, [mine], held_other, brought, brought_other)
    lag_rows = [early_theirs, next_theirs, middle_theirs, late_theirs]
    back = exchange(jnp.concatenate(lag_rows, axis=0), 1, 1)
    return pl.pallas_call(
        functools.partial(place_kernel, order),
        out_shape=jax.ShapeDtypeStruct(
            (STEPS, members * SRC_DEV, channels, NLAG), jnp.bfloat16
        ),
        in_specs=[VMEM] * 3,
        out_specs=VMEM,
        compiler_params=PARAMS,
        name="place_rows",
    )(early, late, back)


def solution(mesh):
    placed = (P(AXES, None, None), P(), P())
    return jax.shard_map(
        on_device,
        mesh=mesh,
        in_specs=placed,
        out_specs=P(None, None, AXES, None),
        check_vma=False,
    )
```

```python
import functools
import math

import jax
import jax.numpy as jnp
import ml_dtypes
import numpy as np
from jax import lax
from jax.experimental import pallas as pl
from jax.experimental.pallas import tpu as pltpu
from jax.sharding import PartitionSpec as P

NLAG = 512
SRC_DEV = 2
STEPS = 2
RADIX = 16
AXES = ("grp", "dev")
SMEM = pl.BlockSpec(memory_space=pltpu.SMEM)
VMEM = pl.BlockSpec(memory_space=pltpu.VMEM)
AHEAD = pl.CostEstimate(flops=5_000_000_000, bytes_accessed=1_000_000, transcendentals=0)
BESIDE = pl.CostEstimate(flops=1_000_000_000, bytes_accessed=1_000_000, transcendentals=0)
PARAMS = pltpu.CompilerParams(vmem_limit_bytes=16 * 1024 * 1024)


def bin_order(bin_count):
    per = bin_count // RADIX
    order = []
    for q in range(RADIX // 2):
        for h in range(2):
            order.append(RADIX * np.arange(per) + 2 * q + h + 1)
    return np.concatenate(order)


def tables_kernel(length, after_ref, table_ref, twiddle_ref):
    del after_ref
    points = length // RADIX
    per = points // 2
    row = lax.broadcasted_iota(jnp.int32, (points, points), 0)
    lane = lax.broadcasted_iota(jnp.int32, (points, points), 1)
    phases = (2.0 * math.pi / points) * (row * (lane % per) % points).astype(jnp.float32)
    cosine, sine = jnp.cos(phases), jnp.sin(phases)
    for h in range(2):
        inside = (lane >= per) if h else (lane < per)
        c, s = jnp.where(inside, cosine, 0.0), jnp.where(inside, sine, 0.0)
        for part, values in enumerate(((c, -s), (s, c))):
            rows = slice((2 * h + part) * points, (2 * h + part + 1) * points)
            whole = jnp.concatenate(values, axis=1)
            high = whole.astype(jnp.bfloat16)
            table_ref[0, rows, :] = high
            table_ref[1, rows, :] = (whole - high.astype(jnp.float32)).astype(jnp.bfloat16)
    residue = lax.broadcasted_iota(jnp.int32, (RADIX, points), 0) + 1
    sample = lax.broadcasted_iota(jnp.int32, (RADIX, points), 1)
    phases = (2.0 * math.pi / length) * (residue * sample).astype(jnp.float32)
    twiddle_ref[0] = jnp.cos(phases)
    twiddle_ref[1] = -jnp.sin(phases)


def lag_table(length, bin_count, lag_count):
    bins = bin_order(bin_count)[:, None]
    lags = np.arange(lag_count)[None, :] - lag_count // 2
    phases = 2.0 * np.pi / length * (bins * lags % length)
    factor = 1.0 / math.sqrt(bin_count)
    cosine, sine = np.cos(phases) * factor, -np.sin(phases) * factor
    return np.concatenate([cosine, sine], axis=0).astype(ml_dtypes.bfloat16)


def real_dft(values):
    n = len(values)
    if n == 1:
        return [(values[0], None)]
    if n == 2:
        return [(values[0] + values[1], None), (values[0] - values[1], None)]
    even, odd = real_dft(values[0::2]), real_dft(values[1::2])
    quarter = n // 4
    out = [None] * (n // 2 + 1)
    for r in range(quarter + 1):
        (er, ei), (orr, oi) = even[r], odd[r]
        cosine, sine = math.cos(2 * math.pi * r / n), math.sin(2 * math.pi * r / n)
        if r == 0:
            tr, ti = orr, None
        elif r == quarter:
            tr, ti = None, -orr
        elif 8 * r == n:
            tr, ti = (orr + oi) * cosine, (oi - orr) * cosine
        else:
            tr, ti = orr * cosine + oi * sine, oi * cosine - orr * sine
        plus_re = er if tr is None else er + tr
        minus_re = er if tr is None else er - tr
        if ei is None:
            plus_im, minus_im = ti, ti
        elif ti is None:
            plus_im, minus_im = ei, -ei
        else:
            plus_im, minus_im = ei + ti, ti - ei
        out[r] = (plus_re, plus_im)
        if r < quarter:
            out[n // 2 - r] = (minus_re, minus_im)
    return out


def spectrum(samples, twiddle_ref, table_ref):
    rows, length = samples.shape
    points = length // RADIX
    half = real_dft([samples[:, i * points : (i + 1) * points] for i in range(RADIX)])
    lanes = []
    for residue in range(1, RADIX + 1):
        folded = min(residue, RADIX - residue)
        re, im = half[folded]
        if residue > RADIX // 2 and im is not None:
            im = -im
        cosine = twiddle_ref[0, residue - 1 : residue, :]
        sine = twiddle_ref[1, residue - 1 : residue, :]
        if im is None:
            lanes.append((re * cosine, re * sine))
        else:
            lanes.append((re * cosine - im * sine, re * sine + im * cosine))
    blocks = []
    for q in range(RADIX // 2):
        (ar, ai), (br, bi) = lanes[2 * q], lanes[2 * q + 1]
        blocks.append(jnp.concatenate([ar, ai, br, bi], axis=1))
    stacked = jnp.concatenate(blocks, axis=0)
    high = stacked.astype(jnp.bfloat16)
    low = (stacked - high.astype(jnp.float32)).astype(jnp.bfloat16)
    both = jnp.dot(
        jnp.concatenate([high, low], axis=0), table_ref[0], preferred_element_type=jnp.float32
    )
    count = stacked.shape[0]
    out = both[:count] + both[count:]
    out = out + jnp.dot(high, table_ref[1], preferred_element_type=jnp.float32)
    width = out.shape[1] // 2
    re = [out[q * rows : (q + 1) * rows, :width] for q in range(RADIX // 2)]
    im = [out[q * rows : (q + 1) * rows, width:] for q in range(RADIX // 2)]
    return re, im


def scales(re, im, radius, mask):
    amp = [jnp.sqrt(a * a + b * b) for a, b in zip(re, im)]
    rows, width = amp[0].shape
    per = width // 2
    reach = radius // RADIX
    lane = lax.broadcasted_iota(jnp.int32, (rows, width), 1)
    place = lane % per
    upper = lane >= per
    swapped = [pltpu.roll(a, per, 1) for a in amp]
    pair = [a + b for a, b in zip(amp, swapped)]
    total = pair[0]
    for value in pair[1:]:
        total = total + value

    def shifted(value, by):
        moved = pltpu.roll(value, (-by) % width, 1)
        inside = (place + by >= 0) & (place + by < per)
        return jnp.where(inside, moved, 0.0)

    centre = total
    for by in range(1, reach):
        centre = centre + shifted(total, by) + shifted(total, -by)
    before = jnp.zeros_like(total)
    out = []
    for a, b, both in zip(amp, swapped, pair):
        upto = before + a + jnp.where(upper, b, 0.0)
        before_here = before + jnp.where(upper, b, 0.0)
        onward = total - before_here
        before = before + both
        out.append((upto, onward))
    result = []
    for upto, onward in out:
        summed = centre + shifted(upto, reach) + shifted(onward, -reach)
        result.append(mask / (summed * (1.0 / (2 * radius + 1)) + 1e-06))
    return result


def whiten_rows(samples, radius, mask, twiddle_ref, table_ref, relay_ref, out_ref):
    rows = samples.shape[0]
    blocks = RADIX // 2
    re, im = spectrum(samples, twiddle_ref, table_ref)
    scale = scales(re, im, radius, mask)
    for part, values in enumerate((re, im)):
        for q in range(blocks):
            relay_ref[pl.ds(part * rows * blocks + q, rows, stride=blocks), :] = (
                values[q] * scale[q]
            )
    out_ref[...] = relay_ref[...].astype(jnp.bfloat16)


def panel_order(member_bits):
    held = [(0, 0)]
    for bit in member_bits:
        held += [(k ^ bit, 1 - odd) for k, odd in held]
    return held


MINE, MATE, CROSS, SAME = (0, 0), (1, 0), (1, 1), (0, 1)


def flags_of(picks, flags):
    return lax.dot_general(
        picks.astype(jnp.bfloat16),
        flags,
        (((1,), (1,)), ((), ())),
        preferred_element_type=jnp.float32,
    )


def at_window(rows_flags):
    row = lax.broadcasted_iota(jnp.int32, rows_flags.shape, 0)
    column = lax.broadcasted_iota(jnp.int32, rows_flags.shape, 1)
    kept = jnp.where(row % rows_flags.shape[1] == column, rows_flags, 0.0)
    return jnp.sum(kept, axis=1, keepdims=True)


def first_kernel(out_ref):
    out_ref[...] = jnp.zeros_like(out_ref)


def choice_kernel(halves, channels, ids_ref, usable_ref, after_ref, *outs):
    del after_ref
    choice_ref, mask_ref, take_ref, info_ref = outs
    windows, total = usable_ref.shape
    members = lax.axis_size("dev")
    group, member = lax.axis_index("grp"), lax.axis_index("dev")
    core, plane = group % SRC_DEV, group // SRC_DEV
    flags = usable_ref[...].astype(jnp.float32).astype(jnp.bfloat16)
    owning = [ids_ref[t] // halves for t in range(STEPS)]
    within = [ids_ref[t] % halves for t in range(STEPS)]

    row = lax.broadcasted_iota(jnp.int32, choice_ref.shape, 0)
    choice = jnp.zeros(choice_ref.shape, jnp.float32)
    for t in range(STEPS):
        apart = (owning[t] + core) % SRC_DEV
        choice = jnp.where(row == (t * SRC_DEV + apart) * halves + within[t], 1.0, choice)
    choice_ref[...] = choice

    row = lax.broadcasted_iota(jnp.int32, info_ref.shape, 0)
    info = jnp.zeros(info_ref.shape, jnp.int32)
    for t in range(STEPS):
        start = owning[t] * members * channels + within[t] * SRC_DEV
        info = jnp.where(row == t, start, info)
    info_ref[...] = info

    rows = STEPS * windows
    row = lax.broadcasted_iota(jnp.int32, (rows, total), 0)
    lane = lax.broadcasted_iota(jnp.int32, (rows, total), 1)
    picks = jnp.zeros((rows, total), jnp.float32)
    for t in range(STEPS):
        channel = (owning[t] * members + member) * channels + within[t] * SRC_DEV + core
        picks = jnp.where((row // windows == t) & (lane == channel), 1.0, picks)
    mask_ref[...] = jnp.broadcast_to(at_window(flags_of(picks, flags)), mask_ref.shape)

    row = lax.broadcasted_iota(jnp.int32, take_ref.shape[1:], 0)
    for index in range(take_ref.shape[0]):
        take = jnp.zeros(take_ref.shape[1:], jnp.float32)
        for t in range(STEPS):
            differs = ((owning[t] // SRC_DEV) ^ plane) >> index & 1
            take = jnp.where(row // windows == t, differs.astype(jnp.float32), take)
        take_ref[index] = take


def pick_kernel(flip, choice_ref, own_ref, other_ref, out_ref, samples):
    channels, windows, length = own_ref.shape
    halves = channels // SRC_DEV
    half = (lax.axis_index("grp") + flip) % SRC_DEV
    points = length // RADIX
    for step in range(STEPS):
        held = [jnp.zeros((windows, points), jnp.float32)] * RADIX
        for k, raw_ref in enumerate((own_ref, other_ref)):
            for h in range(halves):
                index = (step * SRC_DEV + k) * halves + h
                here = jnp.broadcast_to(choice_ref[index : index + 1, :], (windows, points)) > 0.0
                row = raw_ref[h * SRC_DEV + half].astype(jnp.float32)
                for n in range(RADIX):
                    held[n] = jnp.where(here, row[:, n * points : (n + 1) * points], held[n])
        for n in range(RADIX):
            samples[step * windows : (step + 1) * windows, n * points : (n + 1) * points] = held[n]
    out_ref[...] = samples[...].astype(out_ref.dtype)


def receiver_kernel(radius, order, info_ref, usable_ref, raw_ref, twiddle_ref, table_ref, *rest):
    spectra_ref, samples, relay = rest[0], rest[-2], rest[-1]
    factor_refs = rest[1:-2]
    channels, windows, _ = raw_ref.shape
    members = lax.axis_size("dev")
    group, member = lax.axis_index("grp"), lax.axis_index("dev")
    core = group % SRC_DEV
    first = (group * members + member) * channels
    flags = usable_ref[...].astype(jnp.float32).astype(jnp.bfloat16)
    total = flags.shape[1]

    for r in range(channels):
        samples[r * windows : (r + 1) * windows, :] = raw_ref[r].astype(jnp.float32)
    rows = channels * windows
    row = lax.broadcasted_iota(jnp.int32, (rows, total), 0)
    lane = lax.broadcasted_iota(jnp.int32, (rows, total), 1)
    own = jnp.where(lane == first + row // windows, 1.0, 0.0)
    mask = at_window(flags_of(own, flags))
    whiten_rows(samples[...], radius, mask, twiddle_ref, table_ref, relay, spectra_ref)

    rows = STEPS * channels
    row = lax.broadcasted_iota(jnp.int32, (rows, total), 0)
    lane = lax.broadcasted_iota(jnp.int32, (rows, total), 1)
    start = jnp.zeros((rows, total), jnp.int32)
    for t in range(STEPS):
        here = jnp.broadcast_to(info_ref[t : t + 1, :1], (rows, total))
        start = jnp.where(row // channels == t, here, start)
    blocks = []
    for k, odd in order:
        offset = (member ^ k) * channels + (core + odd) % SRC_DEV
        blocks.append(jnp.where(lane == start + offset, 1.0, 0.0))
    sent = flags_of(jnp.concatenate(blocks, axis=0), flags)
    for ref, (core_flip, member_flip) in zip(factor_refs, (MINE, MATE, CROSS, SAME)):
        whose = ((group ^ core_flip) * members + (member ^ member_flip)) * channels
        received = flags_of(jnp.where(lane == whose + row % channels, 1.0, 0.0), flags)
        both = sent * jnp.concatenate([received] * len(order), axis=0)
        counts = jnp.sum(both, axis=1, keepdims=True)
        ref[...] = jnp.broadcast_to(1.0 / jnp.maximum(counts, 1.0), ref.shape)


def source_kernel(radius, *refs):
    take_ref, mask_ref, kept_ref, came_ref, twiddle_ref, table_ref, spectra_ref = refs[:7]
    out_ref, passed_ref, relay = refs[7:]
    passed_ref[...] = spectra_ref[...]
    rows, length = kept_ref.shape
    points = length // RADIX
    here = take_ref[...] > 0.0
    kept, came = kept_ref[...].astype(jnp.float32), came_ref[...].astype(jnp.float32)
    here = jnp.concatenate([here] * RADIX, axis=1)
    samples = jnp.where(here, came, kept)
    whiten_rows(samples, radius, mask_ref[:, :1], twiddle_ref, table_ref, relay, out_ref)


def lagged_rows(windows, pieces, sets, table_ref, products, stacked):
    blocks = RADIX // 2

    def row_set(ref, base, first, rows):
        out = []
        for part in range(2):
            held = []
            for w in range(0, windows, 2):
                start = base + (part * rows + first + w) * blocks
                both = ref[start : start + 2 * blocks, :].astype(jnp.float32)
                held += [both[:blocks], both[blocks:]]
            out.append(held)
        return out

    pair = 0
    for recv_ref, _ in sets:
        receivers = recv_ref.shape[0] // (2 * windows * blocks)
        own = [row_set(recv_ref, 0, r * windows, receivers * windows) for r in range(receivers)]
        for ref, base in pieces:
            for step in range(STEPS):
                a, b = row_set(ref, base, step * windows, STEPS * windows)
                for r in range(receivers):
                    c, e = own[r]
                    re = im = None
                    for w in range(windows):
                        re_w = a[w] * c[w] + b[w] * e[w]
                        im_w = b[w] * c[w] - a[w] * e[w]
                        re = re_w if re is None else re + re_w
                        im = im_w if im is None else im + im_w
                    products[0, pair * blocks : (pair + 1) * blocks, :] = re
                    products[1, pair * blocks : (pair + 1) * blocks, :] = im
                    pair += 1
    width = products.shape[2]
    inverse = jnp.concatenate([factors for _, factors in sets], axis=0)
    for part in range(2):
        for q in range(blocks):
            column = (part * blocks + q) * width
            values = products[part, pl.ds(q, pair, stride=blocks), :] * inverse
            stacked[:, column : column + width] = values.astype(jnp.bfloat16)
    return jnp.dot(stacked[...], table_ref[...], preferred_element_type=jnp.float32)


def pieces_of(ref, windows):
    rows = 2 * STEPS * windows * (RADIX // 2)
    return [(ref, base) for base in range(0, ref.shape[0], rows)]


def part_kernel(windows, first, n_sets, *refs):
    table_ref, set_refs, refs = refs[0], refs[1 : 1 + 2 * n_sets], refs[1 + 2 * n_sets :]
    products, stacked = refs[-2:]
    buffers, outs = refs[: -2 - n_sets], refs[-2 - n_sets : -2]
    pieces = [piece for ref in buffers for piece in pieces_of(ref, windows)]
    rows = outs[0].shape[0]
    sets = [
        (set_refs[2 * i], set_refs[2 * i + 1][first : first + rows, :]) for i in range(n_sets)
    ]
    lagged = lagged_rows(windows, pieces, sets, table_ref, products, stacked)
    for i, out_ref in enumerate(outs):
        out_ref[...] = lagged[i * rows : (i + 1) * rows].astype(jnp.bfloat16)


def pass_kernel(value_ref, after_ref, out_ref):
    del after_ref
    out_ref[...] = value_ref[...]


def place_kernel(order, *refs):
    out_ref = refs[-1]
    member = lax.axis_index("dev")
    core = lax.axis_index("grp") % SRC_DEV
    receivers = out_ref.shape[2]
    whole = []
    for core_flip, member_flip in (MINE, MATE, CROSS, SAME):
        whole += [(k ^ member_flip, odd ^ core_flip) for k, odd in order]
    block = STEPS * receivers
    done = 0
    for ref in refs[:-1]:
        for p in range(ref.shape[0] // block):
            k, odd = whole[done]
            source = (member ^ k) * SRC_DEV + (core + odd) % SRC_DEV
            for step in range(STEPS):
                row = p * block + step * receivers
                out_ref[step, source] = ref[row : row + receivers, :]
            done += 1


def on_device(records, usable, panel_ids):
    channels, windows, length = records.shape
    bin_count = length // 2
    radius = bin_count // 16
    halves = channels // SRC_DEV
    groups = lax.axis_size("grp")
    members = lax.axis_size("dev")
    blocks = RADIX // 2
    width = bin_count // blocks

    def exchange(value, group_bit, member_bit):
        flip = group_bit * members + member_bit
        pairs = [(i, i ^ flip) for i in range(groups * members)]
        return lax.ppermute(value, AXES, pairs)

    ltable = jnp.asarray(lag_table(length, bin_count, NLAG))
    member_bits = []
    bit = members // 2
    while bit:
        member_bits.append(bit)
        bit //= 2
    order = panel_order(member_bits[:-1])

    usable_rows = usable.T
    planes = groups // SRC_DEV
    source_rows = STEPS * windows
    plane_bits = planes.bit_length() - 1

    records_other = exchange(records, 1, 0)
    ahead = pl.pallas_call(
        first_kernel,
        out_shape=jax.ShapeDtypeStruct((8, width), jnp.float32),
        in_specs=[],
        out_specs=VMEM,
        compiler_params=PARAMS,
        cost_estimate=AHEAD,
        name="ahead",
    )()
    choice, mask, take, info = pl.pallas_call(
        functools.partial(choice_kernel, halves, channels),
        out_shape=[
            jax.ShapeDtypeStruct((STEPS * SRC_DEV * halves, width), jnp.float32),
            jax.ShapeDtypeStruct((source_rows, width), jnp.float32),
            jax.ShapeDtypeStruct((plane_bits, source_rows, width), jnp.float32),
            jax.ShapeDtypeStruct((8, width), jnp.int32),
        ],
        in_specs=[SMEM] + [VMEM] * 2,
        out_specs=[VMEM] * 4,
        compiler_params=PARAMS,
        name="choose_rows",
    )(panel_ids, usable_rows, ahead)

    def pick(flip):
        return pl.pallas_call(
            functools.partial(pick_kernel, flip),
            out_shape=jax.ShapeDtypeStruct((source_rows, length), records.dtype),
            in_specs=[VMEM] * 3,
            out_specs=VMEM,
            scratch_shapes=[pltpu.VMEM((source_rows, length), jnp.float32)],
            compiler_params=PARAMS,
            name="pick_rows",
        )(choice, records, records_other)

    sent = pick(1)
    came = exchange(sent, SRC_DEV * (planes // 2) + 1, 0)
    kept = pick(0)
    for index in range(plane_bits - 2, -1, -1):
        kept = jnp.where(take[index + 1][:, :1] > 0.0, came, kept)
        came = exchange(kept, SRC_DEV << index, 0)

    points = length // RADIX
    table, twiddle = pl.pallas_call(
        functools.partial(tables_kernel, length),
        out_shape=[
            jax.ShapeDtypeStruct((2, 4 * points, 2 * points), jnp.bfloat16),
            jax.ShapeDtypeStruct((2, RADIX, points), jnp.float32),
        ],
        in_specs=[VMEM],
        out_specs=[VMEM] * 2,
        compiler_params=PARAMS,
        cost_estimate=AHEAD,
        name="short_tables",
    )(sent)

    row_count = channels * windows
    pairs = len(order) * STEPS * channels
    receivers, *factors = pl.pallas_call(
        functools.partial(receiver_kernel, radius, order),
        out_shape=[
            jax.ShapeDtypeStruct((2 * row_count * blocks, width), jnp.bfloat16),
        ]
        + [jax.ShapeDtypeStruct((pairs, width), jnp.float32)] * 4,
        in_specs=[VMEM] * 5,
        out_specs=[VMEM] * 5,
        scratch_shapes=[
            pltpu.VMEM((row_count, length), jnp.float32),
            pltpu.VMEM((2 * row_count * blocks, width), jnp.float32),
        ],
        compiler_params=PARAMS,
        cost_estimate=AHEAD,
        name="receiver_spectra",
    )(info, usable_rows, records, twiddle, table)

    piece, passed = pl.pallas_call(
        functools.partial(source_kernel, radius),
        out_shape=[
            jax.ShapeDtypeStruct((2 * source_rows * blocks, width), jnp.bfloat16),
            jax.ShapeDtypeStruct(receivers.shape, receivers.dtype),
        ],
        in_specs=[VMEM] * 7,
        out_specs=[VMEM] * 2,
        scratch_shapes=[pltpu.VMEM((2 * source_rows * blocks, width), jnp.float32)],
        compiler_params=PARAMS,
        name="source_spectra",
    )(take[0], mask, kept, came, twiddle, table, receivers)

    held = piece
    for bit in member_bits[:-2]:
        held = jnp.concatenate([held, exchange(held, 1, bit)], axis=0)
    cross = exchange(passed, *CROSS)
    brought = exchange(held, 1, member_bits[-2])

    def pass_on(value, after):
        return pl.pallas_call(
            pass_kernel,
            out_shape=jax.ShapeDtypeStruct(value.shape, value.dtype),
            in_specs=[VMEM] * 2,
            out_specs=VMEM,
            compiler_params=PARAMS,
            name="pass_on",
        )(value, after)

    def part(first, sets, *buffers):
        rows = sum(b.shape[0] for b in buffers) // (2 * windows * blocks) * channels
        total = rows * len(sets)
        return pl.pallas_call(
            functools.partial(part_kernel, windows, first, len(sets)),
            out_shape=[jax.ShapeDtypeStruct((rows, NLAG), jnp.bfloat16)] * len(sets),
            in_specs=[VMEM] * (1 + 2 * len(sets) + len(buffers)),
            out_specs=[VMEM] * len(sets),
            scratch_shapes=[
                pltpu.VMEM((2, total * blocks, width), jnp.float32),
                pltpu.VMEM((total, 2 * bin_count), jnp.bfloat16),
            ],
            compiler_params=PARAMS,
            cost_estimate=BESIDE,
            name="correlate_part",
        )(ltable, *[array for pair in sets for array in pair], *buffers)

    same = exchange(pass_on(cross, receivers), *MATE)
    mate = exchange(pass_on(receivers, same), *MATE)
    sets = list(zip((receivers, mate, cross, same), factors))
    early = part(0, sets[2:3], held) + part(0, sets[3:], held)
    later = part(pairs // 2, sets[2:], brought)
    back_cross, back_same = [
        exchange(jnp.concatenate([a, b], axis=0), *which)
        for a, b, which in zip(early, later, (CROSS, SAME))
    ]
    (mate_rows,) = part(0, sets[1:2], held, brought)
    back_mate = exchange(mate_rows, *MATE)
    (rows,) = part(0, sets[:1], held, brought)
    return pl.pallas_call(
        functools.partial(place_kernel, order),
        out_shape=jax.ShapeDtypeStruct(
            (STEPS, members * SRC_DEV, channels, NLAG), jnp.bfloat16
        ),
        in_specs=[VMEM] * 4,
        out_specs=VMEM,
        compiler_params=PARAMS,
        name="place_rows",
    )(rows, back_mate, back_cross, back_same)


def solution(mesh):
    placed = (P(AXES, None, None), P(), P())
    return jax.shard_map(
        on_device,
        mesh=mesh,
        in_specs=placed,
        out_specs=P(None, None, AXES, None),
        check_vma=False,
    )
```

```python
import functools
import math

import jax
import jax.numpy as jnp
import ml_dtypes
import numpy as np
from jax import lax
from jax.experimental import pallas as pl
from jax.experimental.pallas import tpu as pltpu
from jax.sharding import PartitionSpec as P

NLAG = 512
SRC_DEV = 2
STEPS = 2
RADIX = 16
AXES = ("grp", "dev")
TURN_PLANE, TURN_GATHER, TURN_LAST = 1, (1, 1), 1
BIT_ORDER = (2, 1, 0)
SMEM = pl.BlockSpec(memory_space=pltpu.SMEM)
VMEM = pl.BlockSpec(memory_space=pltpu.VMEM)
AHEAD = pl.CostEstimate(flops=5_000_000_000, bytes_accessed=1_000_000, transcendentals=0)
BESIDE = pl.CostEstimate(flops=1_000_000_000, bytes_accessed=1_000_000, transcendentals=0)
PARAMS = pltpu.CompilerParams(vmem_limit_bytes=16 * 1024 * 1024)


def bin_order(bin_count):
    per = bin_count // RADIX
    order = []
    for q in range(RADIX // 2):
        for h in range(2):
            order.append(RADIX * np.arange(per) + 2 * q + h + 1)
    return np.concatenate(order)


def tables_kernel(length, after_ref, table_ref, twiddle_ref):
    del after_ref
    points = length // RADIX
    per = points // 2
    row = lax.broadcasted_iota(jnp.int32, (points, points), 0)
    lane = lax.broadcasted_iota(jnp.int32, (points, points), 1)
    phases = (2.0 * math.pi / points) * (row * (lane % per) % points).astype(jnp.float32)
    cosine, sine = jnp.cos(phases), jnp.sin(phases)
    for h in range(2):
        inside = (lane >= per) if h else (lane < per)
        c, s = jnp.where(inside, cosine, 0.0), jnp.where(inside, sine, 0.0)
        for part, values in enumerate(((c, -s), (s, c))):
            rows = slice((2 * h + part) * points, (2 * h + part + 1) * points)
            whole = jnp.concatenate(values, axis=1)
            high = whole.astype(jnp.bfloat16)
            table_ref[0, rows, :] = high
            table_ref[1, rows, :] = (whole - high.astype(jnp.float32)).astype(jnp.bfloat16)
    residue = lax.broadcasted_iota(jnp.int32, (RADIX, points), 0) + 1
    sample = lax.broadcasted_iota(jnp.int32, (RADIX, points), 1)
    phases = (2.0 * math.pi / length) * (residue * sample).astype(jnp.float32)
    twiddle_ref[0] = jnp.cos(phases)
    twiddle_ref[1] = -jnp.sin(phases)


def lag_table(length, bin_count, lag_count):
    bins = bin_order(bin_count)[:, None]
    lags = np.arange(lag_count)[None, :] - lag_count // 2
    phases = 2.0 * np.pi / length * (bins * lags % length)
    factor = 1.0 / math.sqrt(bin_count)
    cosine, sine = np.cos(phases) * factor, -np.sin(phases) * factor
    return np.concatenate([cosine, sine], axis=0).astype(ml_dtypes.bfloat16)


def real_dft(values):
    n = len(values)
    if n == 1:
        return [(values[0], None)]
    if n == 2:
        return [(values[0] + values[1], None), (values[0] - values[1], None)]
    even, odd = real_dft(values[0::2]), real_dft(values[1::2])
    quarter = n // 4
    out = [None] * (n // 2 + 1)
    for r in range(quarter + 1):
        (er, ei), (orr, oi) = even[r], odd[r]
        cosine, sine = math.cos(2 * math.pi * r / n), math.sin(2 * math.pi * r / n)
        if r == 0:
            tr, ti = orr, None
        elif r == quarter:
            tr, ti = None, -orr
        elif 8 * r == n:
            tr, ti = (orr + oi) * cosine, (oi - orr) * cosine
        else:
            tr, ti = orr * cosine + oi * sine, oi * cosine - orr * sine
        plus_re = er if tr is None else er + tr
        minus_re = er if tr is None else er - tr
        if ei is None:
            plus_im, minus_im = ti, ti
        elif ti is None:
            plus_im, minus_im = ei, -ei
        else:
            plus_im, minus_im = ei + ti, ti - ei
        out[r] = (plus_re, plus_im)
        if r < quarter:
            out[n // 2 - r] = (minus_re, minus_im)
    return out


def spectrum(samples, twiddle_ref, table_ref):
    rows, length = samples.shape
    points = length // RADIX
    half = real_dft([samples[:, i * points : (i + 1) * points] for i in range(RADIX)])
    lanes = []
    for residue in range(1, RADIX + 1):
        folded = min(residue, RADIX - residue)
        re, im = half[folded]
        if residue > RADIX // 2 and im is not None:
            im = -im
        cosine = twiddle_ref[0, residue - 1 : residue, :]
        sine = twiddle_ref[1, residue - 1 : residue, :]
        if im is None:
            lanes.append((re * cosine, re * sine))
        else:
            lanes.append((re * cosine - im * sine, re * sine + im * cosine))
    blocks = []
    for q in range(RADIX // 2):
        (ar, ai), (br, bi) = lanes[2 * q], lanes[2 * q + 1]
        blocks.append(jnp.concatenate([ar, ai, br, bi], axis=1))
    stacked = jnp.concatenate(blocks, axis=0)
    high = stacked.astype(jnp.bfloat16)
    low = (stacked - high.astype(jnp.float32)).astype(jnp.bfloat16)
    both = jnp.dot(
        jnp.concatenate([high, low], axis=0), table_ref[0], preferred_element_type=jnp.float32
    )
    count = stacked.shape[0]
    out = both[:count] + both[count:]
    out = out + jnp.dot(high, table_ref[1], preferred_element_type=jnp.float32)
    width = out.shape[1] // 2
    re = [out[q * rows : (q + 1) * rows, :width] for q in range(RADIX // 2)]
    im = [out[q * rows : (q + 1) * rows, width:] for q in range(RADIX // 2)]
    return re, im


def scales(re, im, radius, mask):
    amp = [jnp.sqrt(a * a + b * b) for a, b in zip(re, im)]
    rows, width = amp[0].shape
    per = width // 2
    reach = radius // RADIX
    lane = lax.broadcasted_iota(jnp.int32, (rows, width), 1)
    place = lane % per
    upper = lane >= per
    swapped = [pltpu.roll(a, per, 1) for a in amp]
    pair = [a + b for a, b in zip(amp, swapped)]
    total = pair[0]
    for value in pair[1:]:
        total = total + value

    def shifted(value, by):
        moved = pltpu.roll(value, (-by) % width, 1)
        inside = (place + by >= 0) & (place + by < per)
        return jnp.where(inside, moved, 0.0)

    centre = total
    for by in range(1, reach):
        centre = centre + shifted(total, by) + shifted(total, -by)
    before = jnp.zeros_like(total)
    out = []
    for a, b, both in zip(amp, swapped, pair):
        upto = before + a + jnp.where(upper, b, 0.0)
        before_here = before + jnp.where(upper, b, 0.0)
        onward = total - before_here
        before = before + both
        out.append((upto, onward))
    result = []
    for upto, onward in out:
        summed = centre + shifted(upto, reach) + shifted(onward, -reach)
        result.append(mask / (summed * (1.0 / (2 * radius + 1)) + 1e-06))
    return result


def whiten_rows(samples, radius, mask, twiddle_ref, table_ref, relay_ref, out_ref):
    rows = samples.shape[0]
    blocks = RADIX // 2
    re, im = spectrum(samples, twiddle_ref, table_ref)
    scale = scales(re, im, radius, mask)
    for part, values in enumerate((re, im)):
        for q in range(blocks):
            relay_ref[pl.ds(part * rows * blocks + q, rows, stride=blocks), :] = (
                values[q] * scale[q]
            )
    out_ref[...] = relay_ref[...].astype(jnp.bfloat16)


def turn(index):
    return TURN_GATHER[min(index, len(TURN_GATHER) - 1)]


def panel_order(bits):
    held = [(0, 0)]
    for index, bit in enumerate(bits):
        brought = [(k ^ bit, odd ^ turn(index)) for k, odd in held]
        if index < len(bits) - 1:
            held = held + brought
    flip = lambda pieces: [(k, 1 - odd) for k, odd in pieces]
    return held + flip(held) + brought + flip(brought)


def flags_of(picks, flags):
    return lax.dot_general(
        picks.astype(jnp.bfloat16),
        flags,
        (((1,), (1,)), ((), ())),
        preferred_element_type=jnp.float32,
    )


def at_window(rows_flags):
    row = lax.broadcasted_iota(jnp.int32, rows_flags.shape, 0)
    column = lax.broadcasted_iota(jnp.int32, rows_flags.shape, 1)
    kept = jnp.where(row % rows_flags.shape[1] == column, rows_flags, 0.0)
    return jnp.sum(kept, axis=1, keepdims=True)


def first_kernel(out_ref):
    out_ref[...] = jnp.zeros_like(out_ref)


def choice_kernel(halves, channels, ids_ref, usable_ref, after_ref, *outs):
    del after_ref
    choice_ref, mask_ref, take_ref, info_ref = outs
    windows, total = usable_ref.shape
    members = lax.axis_size("dev")
    group, member = lax.axis_index("grp"), lax.axis_index("dev")
    core, plane = group % SRC_DEV, group // SRC_DEV
    flags = usable_ref[...].astype(jnp.float32).astype(jnp.bfloat16)
    owning = [ids_ref[t] // halves for t in range(STEPS)]
    within = [ids_ref[t] % halves for t in range(STEPS)]

    row = lax.broadcasted_iota(jnp.int32, choice_ref.shape, 0)
    choice = jnp.zeros(choice_ref.shape, jnp.float32)
    for t in range(STEPS):
        apart = (owning[t] + core) % SRC_DEV
        choice = jnp.where(row == (t * SRC_DEV + apart) * halves + within[t], 1.0, choice)
    choice_ref[...] = choice

    row = lax.broadcasted_iota(jnp.int32, info_ref.shape, 0)
    info = jnp.zeros(info_ref.shape, jnp.int32)
    for t in range(STEPS):
        start = owning[t] * members * channels + within[t] * SRC_DEV
        info = jnp.where(row == t, start, info)
    info_ref[...] = info

    rows = STEPS * windows
    row = lax.broadcasted_iota(jnp.int32, (rows, total), 0)
    lane = lax.broadcasted_iota(jnp.int32, (rows, total), 1)
    picks = jnp.zeros((rows, total), jnp.float32)
    for t in range(STEPS):
        channel = (owning[t] * members + member) * channels + within[t] * SRC_DEV + core
        picks = jnp.where((row // windows == t) & (lane == channel), 1.0, picks)
    mask_ref[...] = jnp.broadcast_to(at_window(flags_of(picks, flags)), mask_ref.shape)

    row = lax.broadcasted_iota(jnp.int32, take_ref.shape[1:], 0)
    for index in range(take_ref.shape[0]):
        take = jnp.zeros(take_ref.shape[1:], jnp.float32)
        for t in range(STEPS):
            differs = ((owning[t] // SRC_DEV) ^ plane) >> index & 1
            take = jnp.where(row // windows == t, differs.astype(jnp.float32), take)
        take_ref[index] = take


def pick_kernel(flip, choice_ref, own_ref, other_ref, out_ref, samples):
    channels, windows, length = own_ref.shape
    halves = channels // SRC_DEV
    half = (lax.axis_index("grp") + flip) % SRC_DEV
    points = length // RADIX
    for step in range(STEPS):
        held = [jnp.zeros((windows, points), jnp.float32)] * RADIX
        for k, raw_ref in enumerate((own_ref, other_ref)):
            for h in range(halves):
                index = (step * SRC_DEV + k) * halves + h
                here = jnp.broadcast_to(choice_ref[index : index + 1, :], (windows, points)) > 0.0
                row = raw_ref[h * SRC_DEV + half].astype(jnp.float32)
                for n in range(RADIX):
                    held[n] = jnp.where(here, row[:, n * points : (n + 1) * points], held[n])
        for n in range(RADIX):
            samples[step * windows : (step + 1) * windows, n * points : (n + 1) * points] = held[n]
    out_ref[...] = samples[...].astype(out_ref.dtype)


def receiver_kernel(radius, order, last_bit, info_ref, usable_ref, raw_ref, twiddle_ref, table_ref, *rest):
    spectra_ref, inverse_ref, other_ref, samples, relay = rest
    channels, windows, _ = raw_ref.shape
    members = lax.axis_size("dev")
    group, member = lax.axis_index("grp"), lax.axis_index("dev")
    core = group % SRC_DEV
    first = (group * members + member) * channels
    flags = usable_ref[...].astype(jnp.float32).astype(jnp.bfloat16)
    total = flags.shape[1]

    for r in range(channels):
        samples[r * windows : (r + 1) * windows, :] = raw_ref[r].astype(jnp.float32)
    rows = channels * windows
    row = lax.broadcasted_iota(jnp.int32, (rows, total), 0)
    lane = lax.broadcasted_iota(jnp.int32, (rows, total), 1)
    own = jnp.where(lane == first + row // windows, 1.0, 0.0)
    mask = at_window(flags_of(own, flags))
    whiten_rows(samples[...], radius, mask, twiddle_ref, table_ref, relay, spectra_ref)

    rows = STEPS * channels
    row = lax.broadcasted_iota(jnp.int32, (rows, total), 0)
    lane = lax.broadcasted_iota(jnp.int32, (rows, total), 1)
    start = jnp.zeros((rows, total), jnp.int32)
    for t in range(STEPS):
        here = jnp.broadcast_to(info_ref[t : t + 1, :1], (rows, total))
        start = jnp.where(row // channels == t, here, start)
    blocks = []
    for k, odd in order:
        offset = (member ^ k) * channels + (core + odd) % SRC_DEV
        blocks.append(jnp.where(lane == start + offset, 1.0, 0.0))
    sent = flags_of(jnp.concatenate(blocks, axis=0), flags)
    theirs = ((group ^ TURN_LAST) * members + (member ^ last_bit)) * channels
    for ref, start in ((inverse_ref, first), (other_ref, theirs)):
        received = flags_of(jnp.where(lane == start + row % channels, 1.0, 0.0), flags)
        both = sent * jnp.concatenate([received] * len(order), axis=0)
        counts = jnp.sum(both, axis=1, keepdims=True)
        ref[...] = jnp.broadcast_to(1.0 / jnp.maximum(counts, 1.0), ref.shape)


def source_kernel(radius, *refs):
    take_ref, mask_ref, kept_ref, came_ref, twiddle_ref, table_ref, spectra_ref = refs[:7]
    out_ref, passed_ref, relay = refs[7:]
    passed_ref[...] = spectra_ref[...]
    rows, length = kept_ref.shape
    points = length // RADIX
    here = take_ref[...] > 0.0
    kept, came = kept_ref[...].astype(jnp.float32), came_ref[...].astype(jnp.float32)
    here = jnp.concatenate([here] * RADIX, axis=1)
    samples = jnp.where(here, came, kept)
    whiten_rows(samples, radius, mask_ref[:, :1], twiddle_ref, table_ref, relay, out_ref)


def lagged_rows(windows, pieces, sets, table_ref, products, stacked):
    blocks = RADIX // 2

    def row_set(ref, base, first, rows):
        out = []
        for part in range(2):
            held = []
            for w in range(0, windows, 2):
                start = base + (part * rows + first + w) * blocks
                both = ref[start : start + 2 * blocks, :].astype(jnp.float32)
                held += [both[:blocks], both[blocks:]]
            out.append(held)
        return out

    pair = 0
    for recv_ref, _ in sets:
        receivers = recv_ref.shape[0] // (2 * windows * blocks)
        own = [row_set(recv_ref, 0, r * windows, receivers * windows) for r in range(receivers)]
        for ref, base in pieces:
            for step in range(STEPS):
                a, b = row_set(ref, base, step * windows, STEPS * windows)
                for r in range(receivers):
                    c, e = own[r]
                    re = im = None
                    for w in range(windows):
                        re_w = a[w] * c[w] + b[w] * e[w]
                        im_w = b[w] * c[w] - a[w] * e[w]
                        re = re_w if re is None else re + re_w
                        im = im_w if im is None else im + im_w
                    products[0, pair * blocks : (pair + 1) * blocks, :] = re
                    products[1, pair * blocks : (pair + 1) * blocks, :] = im
                    pair += 1
    width = products.shape[2]
    inverse = jnp.concatenate([factors for _, factors in sets], axis=0)
    for part in range(2):
        for q in range(blocks):
            column = (part * blocks + q) * width
            values = products[part, pl.ds(q, pair, stride=blocks), :] * inverse
            stacked[:, column : column + width] = values.astype(jnp.bfloat16)
    return jnp.dot(stacked[...], table_ref[...], preferred_element_type=jnp.float32)


def pieces_of(ref, windows):
    rows = 2 * STEPS * windows * (RADIX // 2)
    return [(ref, base) for base in range(0, ref.shape[0], rows)]


def part_kernel(windows, first, n_sets, *refs):
    table_ref, set_refs, refs = refs[0], refs[1 : 1 + 2 * n_sets], refs[1 + 2 * n_sets :]
    products, stacked = refs[-2:]
    buffers, outs = refs[: -2 - n_sets], refs[-2 - n_sets : -2]
    pieces = [piece for ref in buffers for piece in pieces_of(ref, windows)]
    rows = outs[0].shape[0]
    sets = [
        (set_refs[2 * i], set_refs[2 * i + 1][first : first + rows, :]) for i in range(n_sets)
    ]
    lagged = lagged_rows(windows, pieces, sets, table_ref, products, stacked)
    for i, out_ref in enumerate(outs):
        out_ref[...] = lagged[i * rows : (i + 1) * rows].astype(jnp.bfloat16)


def pass_kernel(value_ref, after_ref, out_ref):
    del after_ref
    out_ref[...] = value_ref[...]


def place_kernel(order, last_bit, *refs):
    out_ref = refs[-1]
    member = lax.axis_index("dev")
    core = lax.axis_index("grp") % SRC_DEV
    receivers = out_ref.shape[2]
    whole = order + [(k ^ last_bit, odd ^ TURN_LAST) for k, odd in order]
    block = STEPS * receivers
    done = 0
    for ref in refs[:-1]:
        for p in range(ref.shape[0] // block):
            k, odd = whole[done]
            source = (member ^ k) * SRC_DEV + (core + odd) % SRC_DEV
            for step in range(STEPS):
                row = p * block + step * receivers
                out_ref[step, source] = ref[row : row + receivers, :]
            done += 1


def on_device(records, usable, panel_ids):
    channels, windows, length = records.shape
    bin_count = length // 2
    radius = bin_count // 16
    halves = channels // SRC_DEV
    groups = lax.axis_size("grp")
    members = lax.axis_size("dev")
    blocks = RADIX // 2
    width = bin_count // blocks

    def exchange(value, group_bit, member_bit):
        flip = group_bit * members + member_bit
        pairs = [(i, i ^ flip) for i in range(groups * members)]
        return lax.ppermute(value, AXES, pairs)

    ltable = jnp.asarray(lag_table(length, bin_count, NLAG))
    all_bits = [1 << i for i in range(members.bit_length() - 1)]
    chosen = [all_bits[i] for i in BIT_ORDER]
    *gather_bits, last_bit = [b for b in all_bits[::-1] if b not in chosen] + chosen
    order = panel_order(gather_bits)

    usable_rows = usable.T
    planes = groups // SRC_DEV
    source_rows = STEPS * windows
    plane_bits = planes.bit_length() - 1

    records_other = exchange(records, 1, 0)
    ahead = pl.pallas_call(
        first_kernel,
        out_shape=jax.ShapeDtypeStruct((8, width), jnp.float32),
        in_specs=[],
        out_specs=VMEM,
        compiler_params=PARAMS,
        cost_estimate=AHEAD,
        name="ahead",
    )()
    choice, mask, take, info = pl.pallas_call(
        functools.partial(choice_kernel, halves, channels),
        out_shape=[
            jax.ShapeDtypeStruct((STEPS * SRC_DEV * halves, width), jnp.float32),
            jax.ShapeDtypeStruct((source_rows, width), jnp.float32),
            jax.ShapeDtypeStruct((plane_bits, source_rows, width), jnp.float32),
            jax.ShapeDtypeStruct((8, width), jnp.int32),
        ],
        in_specs=[SMEM] + [VMEM] * 2,
        out_specs=[VMEM] * 4,
        compiler_params=PARAMS,
        name="choose_rows",
    )(panel_ids, usable_rows, ahead)

    def pick(flip):
        return pl.pallas_call(
            functools.partial(pick_kernel, flip),
            out_shape=jax.ShapeDtypeStruct((source_rows, length), records.dtype),
            in_specs=[VMEM] * 3,
            out_specs=VMEM,
            scratch_shapes=[pltpu.VMEM((source_rows, length), jnp.float32)],
            compiler_params=PARAMS,
            name="pick_rows",
        )(choice, records, records_other)

    sent = pick(TURN_PLANE)
    came = exchange(sent, SRC_DEV * (planes // 2) + TURN_PLANE, 0)
    kept = pick(0) if TURN_PLANE else sent
    for index in range(plane_bits - 2, -1, -1):
        kept = jnp.where(take[index + 1][:, :1] > 0.0, came, kept)
        came = exchange(kept, SRC_DEV << index, 0)

    points = length // RADIX
    table, twiddle = pl.pallas_call(
        functools.partial(tables_kernel, length),
        out_shape=[
            jax.ShapeDtypeStruct((2, 4 * points, 2 * points), jnp.bfloat16),
            jax.ShapeDtypeStruct((2, RADIX, points), jnp.float32),
        ],
        in_specs=[VMEM],
        out_specs=[VMEM] * 2,
        compiler_params=PARAMS,
        cost_estimate=AHEAD,
        name="short_tables",
    )(sent)

    row_count = channels * windows
    pairs = len(order) * STEPS * channels
    receivers, inverse, inverse_theirs = pl.pallas_call(
        functools.partial(receiver_kernel, radius, order, last_bit),
        out_shape=[
            jax.ShapeDtypeStruct((2 * row_count * blocks, width), jnp.bfloat16),
            jax.ShapeDtypeStruct((pairs, width), jnp.float32),
            jax.ShapeDtypeStruct((pairs, width), jnp.float32),
        ],
        in_specs=[VMEM] * 5,
        out_specs=[VMEM] * 3,
        scratch_shapes=[
            pltpu.VMEM((row_count, length), jnp.float32),
            pltpu.VMEM((2 * row_count * blocks, width), jnp.float32),
        ],
        compiler_params=PARAMS,
        cost_estimate=AHEAD,
        name="receiver_spectra",
    )(info, usable_rows, records, twiddle, table)

    piece, passed = pl.pallas_call(
        functools.partial(source_kernel, radius),
        out_shape=[
            jax.ShapeDtypeStruct((2 * source_rows * blocks, width), jnp.bfloat16),
            jax.ShapeDtypeStruct(receivers.shape, receivers.dtype),
        ],
        in_specs=[VMEM] * 7,
        out_specs=[VMEM] * 2,
        scratch_shapes=[pltpu.VMEM((2 * source_rows * blocks, width), jnp.float32)],
        compiler_params=PARAMS,
        name="source_spectra",
    )(take[0], mask, kept, came, twiddle, table, receivers)

    held = piece
    for index, bit in enumerate(gather_bits[:-1]):
        held = jnp.concatenate([held, exchange(held, turn(index), bit)], axis=0)
    theirs = exchange(passed, TURN_LAST, last_bit)

    def pass_on(value, after):
        return pl.pallas_call(
            pass_kernel,
            out_shape=jax.ShapeDtypeStruct(value.shape, value.dtype),
            in_specs=[VMEM] * 2,
            out_specs=VMEM,
            compiler_params=PARAMS,
            name="pass_on",
        )(value, after)

    def part(first, sets, *buffers):
        rows = sum(b.shape[0] for b in buffers) // (2 * windows * blocks) * channels
        total = rows * len(sets)
        return pl.pallas_call(
            functools.partial(part_kernel, windows, first, len(sets)),
            out_shape=[jax.ShapeDtypeStruct((rows, NLAG), jnp.bfloat16)] * len(sets),
            in_specs=[VMEM] * (1 + 2 * len(sets) + len(buffers)),
            out_specs=[VMEM] * len(sets),
            scratch_shapes=[
                pltpu.VMEM((2, total * blocks, width), jnp.float32),
                pltpu.VMEM((total, 2 * bin_count), jnp.bfloat16),
            ],
            compiler_params=PARAMS,
            cost_estimate=BESIDE,
            name="correlate_part",
        )(ltable, *[array for pair in sets for array in pair], *buffers)

    mine, other = (receivers, inverse), (theirs, inverse_theirs)
    brought = exchange(held, turn(len(gather_bits) - 1), gather_bits[-1])
    held_other = exchange(pass_on(held, theirs), 1, 0)
    early_theirs, early = part(0, [other, mine], held)
    brought = pass_on(brought, early_theirs)
    brought_other = exchange(brought, 1, 0)
    (middle_theirs,) = part(pairs // 4, [other], held_other, brought)
    (late_theirs,) = part(pairs // 4 * 3, [other], brought_other)
    (late,) = part(pairs // 4, [mine], held_other, brought, brought_other)
    lag_rows = [early_theirs, middle_theirs, late_theirs]
    back = exchange(jnp.concatenate(lag_rows, axis=0), TURN_LAST, last_bit)
    return pl.pallas_call(
        functools.partial(place_kernel, order, last_bit),
        out_shape=jax.ShapeDtypeStruct(
            (STEPS, members * SRC_DEV, channels, NLAG), jnp.bfloat16
        ),
        in_specs=[VMEM] * 3,
        out_specs=VMEM,
        compiler_params=PARAMS,
        name="place_rows",
    )(early, late, back)


def solution(mesh):
    placed = (P(AXES, None, None), P(), P())
    return jax.shard_map(
        on_device,
        mesh=mesh,
        in_specs=placed,
        out_specs=P(None, None, AXES, None),
        check_vma=False,
    )
```

```python
import functools
import math

import jax
import jax.numpy as jnp
import ml_dtypes
import numpy as np
from jax import lax
from jax.experimental import pallas as pl
from jax.experimental.pallas import tpu as pltpu
from jax.sharding import PartitionSpec as P

NLAG = 512
SRC_DEV = 2
STEPS = 2
RADIX = 16
AXES = ("grp", "dev")
TURN_PLANE, TURN_GATHER, TURN_LAST = 1, (1, 1), 1
BIT_ORDER = (2, 1, 0)
SMEM = pl.BlockSpec(memory_space=pltpu.SMEM)
VMEM = pl.BlockSpec(memory_space=pltpu.VMEM)
AHEAD = pl.CostEstimate(flops=5_000_000_000, bytes_accessed=1_000_000, transcendentals=0)
BESIDE = pl.CostEstimate(flops=1_000_000_000, bytes_accessed=1_000_000, transcendentals=0)
PARAMS = pltpu.CompilerParams(vmem_limit_bytes=16 * 1024 * 1024)


def bin_order(bin_count):
    per = bin_count // RADIX
    order = []
    for q in range(RADIX // 2):
        for h in range(2):
            order.append(RADIX * np.arange(per) + 2 * q + h + 1)
    return np.concatenate(order)


def tables_kernel(length, table_ref, twiddle_ref):
    points = length // RADIX
    per = points // 2
    row = lax.broadcasted_iota(jnp.int32, (points, points), 0)
    lane = lax.broadcasted_iota(jnp.int32, (points, points), 1)
    phases = (2.0 * math.pi / points) * (row * (lane % per) % points).astype(jnp.float32)
    cosine, sine = jnp.cos(phases), jnp.sin(phases)
    for h in range(2):
        inside = (lane >= per) if h else (lane < per)
        c, s = jnp.where(inside, cosine, 0.0), jnp.where(inside, sine, 0.0)
        for part, values in enumerate(((c, -s), (s, c))):
            rows = slice((2 * h + part) * points, (2 * h + part + 1) * points)
            whole = jnp.concatenate(values, axis=1)
            high = whole.astype(jnp.bfloat16)
            table_ref[0, rows, :] = high
            table_ref[1, rows, :] = (whole - high.astype(jnp.float32)).astype(jnp.bfloat16)
    residue = lax.broadcasted_iota(jnp.int32, (RADIX, points), 0) + 1
    sample = lax.broadcasted_iota(jnp.int32, (RADIX, points), 1)
    phases = (2.0 * math.pi / length) * (residue * sample).astype(jnp.float32)
    twiddle_ref[0] = jnp.cos(phases)
    twiddle_ref[1] = -jnp.sin(phases)


def lag_table(length, bin_count, lag_count):
    bins = bin_order(bin_count)[:, None]
    lags = np.arange(lag_count)[None, :] - lag_count // 2
    phases = 2.0 * np.pi / length * (bins * lags % length)
    factor = 1.0 / math.sqrt(bin_count)
    cosine, sine = np.cos(phases) * factor, -np.sin(phases) * factor
    return np.concatenate([cosine, sine], axis=0).astype(ml_dtypes.bfloat16)


def real_dft(values):
    n = len(values)
    if n == 1:
        return [(values[0], None)]
    if n == 2:
        return [(values[0] + values[1], None), (values[0] - values[1], None)]
    even, odd = real_dft(values[0::2]), real_dft(values[1::2])
    quarter = n // 4
    out = [None] * (n // 2 + 1)
    for r in range(quarter + 1):
        (er, ei), (orr, oi) = even[r], odd[r]
        cosine, sine = math.cos(2 * math.pi * r / n), math.sin(2 * math.pi * r / n)
        if r == 0:
            tr, ti = orr, None
        elif r == quarter:
            tr, ti = None, -orr
        elif 8 * r == n:
            tr, ti = (orr + oi) * cosine, (oi - orr) * cosine
        else:
            tr, ti = orr * cosine + oi * sine, oi * cosine - orr * sine
        plus_re = er if tr is None else er + tr
        minus_re = er if tr is None else er - tr
        if ei is None:
            plus_im, minus_im = ti, ti
        elif ti is None:
            plus_im, minus_im = ei, -ei
        else:
            plus_im, minus_im = ei + ti, ti - ei
        out[r] = (plus_re, plus_im)
        if r < quarter:
            out[n // 2 - r] = (minus_re, minus_im)
    return out


def spectrum(samples, twiddle_ref, table_ref):
    rows, length = samples.shape
    points = length // RADIX
    half = real_dft([samples[:, i * points : (i + 1) * points] for i in range(RADIX)])
    lanes = []
    for residue in range(1, RADIX + 1):
        folded = min(residue, RADIX - residue)
        re, im = half[folded]
        if residue > RADIX // 2 and im is not None:
            im = -im
        cosine = twiddle_ref[0, residue - 1 : residue, :]
        sine = twiddle_ref[1, residue - 1 : residue, :]
        if im is None:
            lanes.append((re * cosine, re * sine))
        else:
            lanes.append((re * cosine - im * sine, re * sine + im * cosine))
    blocks = []
    for q in range(RADIX // 2):
        (ar, ai), (br, bi) = lanes[2 * q], lanes[2 * q + 1]
        blocks.append(jnp.concatenate([ar, ai, br, bi], axis=1))
    stacked = jnp.concatenate(blocks, axis=0)
    high = stacked.astype(jnp.bfloat16)
    low = (stacked - high.astype(jnp.float32)).astype(jnp.bfloat16)
    both = jnp.dot(
        jnp.concatenate([high, low], axis=0), table_ref[0], preferred_element_type=jnp.float32
    )
    count = stacked.shape[0]
    out = both[:count] + both[count:]
    out = out + jnp.dot(high, table_ref[1], preferred_element_type=jnp.float32)
    width = out.shape[1] // 2
    re = [out[q * rows : (q + 1) * rows, :width] for q in range(RADIX // 2)]
    im = [out[q * rows : (q + 1) * rows, width:] for q in range(RADIX // 2)]
    return re, im


def scales(re, im, radius, mask):
    amp = [jnp.sqrt(a * a + b * b) for a, b in zip(re, im)]
    rows, width = amp[0].shape
    per = width // 2
    reach = radius // RADIX
    lane = lax.broadcasted_iota(jnp.int32, (rows, width), 1)
    place = lane % per
    upper = lane >= per
    swapped = [pltpu.roll(a, per, 1) for a in amp]
    pair = [a + b for a, b in zip(amp, swapped)]
    total = pair[0]
    for value in pair[1:]:
        total = total + value

    def shifted(value, by):
        moved = pltpu.roll(value, (-by) % width, 1)
        inside = (place + by >= 0) & (place + by < per)
        return jnp.where(inside, moved, 0.0)

    centre = total
    for by in range(1, reach):
        centre = centre + shifted(total, by) + shifted(total, -by)
    before = jnp.zeros_like(total)
    out = []
    for a, b, both in zip(amp, swapped, pair):
        upto = before + a + jnp.where(upper, b, 0.0)
        before_here = before + jnp.where(upper, b, 0.0)
        onward = total - before_here
        before = before + both
        out.append((upto, onward))
    result = []
    for upto, onward in out:
        summed = centre + shifted(upto, reach) + shifted(onward, -reach)
        result.append(mask / (summed * (1.0 / (2 * radius + 1)) + 1e-06))
    return result


def whiten_rows(samples, radius, mask, twiddle_ref, table_ref, relay_ref, out_ref):
    rows = samples.shape[0]
    blocks = RADIX // 2
    re, im = spectrum(samples, twiddle_ref, table_ref)
    scale = scales(re, im, radius, mask)
    for part, values in enumerate((re, im)):
        for q in range(blocks):
            relay_ref[pl.ds(part * rows * blocks + q, rows, stride=blocks), :] = (
                values[q] * scale[q]
            )
    out_ref[...] = relay_ref[...].astype(jnp.bfloat16)


def turn(index):
    return TURN_GATHER[min(index, len(TURN_GATHER) - 1)]


def panel_order(bits):
    held = [(0, 0)]
    for index, bit in enumerate(bits[:-1]):
        first = len(held)
        held = held + [(k ^ bit, odd ^ turn(index)) for k, odd in held]
    last = [(k ^ bits[-1], odd ^ turn(len(bits) - 1)) for k, odd in held]
    order = []
    for pieces in (held, last[:first], last[first:]):
        order += pieces + [(k, 1 - odd) for k, odd in pieces]
    return order


def flags_of(picks, flags):
    return lax.dot_general(
        picks.astype(jnp.bfloat16),
        flags,
        (((1,), (1,)), ((), ())),
        preferred_element_type=jnp.float32,
    )


def at_window(rows_flags):
    row = lax.broadcasted_iota(jnp.int32, rows_flags.shape, 0)
    column = lax.broadcasted_iota(jnp.int32, rows_flags.shape, 1)
    kept = jnp.where(row % rows_flags.shape[1] == column, rows_flags, 0.0)
    return jnp.sum(kept, axis=1, keepdims=True)


def choice_kernel(halves, channels, ids_ref, usable_ref, after_ref, *outs):
    del after_ref
    choice_ref, mask_ref, take_ref, info_ref = outs
    windows, total = usable_ref.shape
    members = lax.axis_size("dev")
    group, member = lax.axis_index("grp"), lax.axis_index("dev")
    core, plane = group % SRC_DEV, group // SRC_DEV
    flags = usable_ref[...].astype(jnp.float32).astype(jnp.bfloat16)
    owning = [ids_ref[t] // halves for t in range(STEPS)]
    within = [ids_ref[t] % halves for t in range(STEPS)]

    row = lax.broadcasted_iota(jnp.int32, choice_ref.shape, 0)
    choice = jnp.zeros(choice_ref.shape, jnp.float32)
    for t in range(STEPS):
        apart = (owning[t] + core) % SRC_DEV
        choice = jnp.where(row == (t * SRC_DEV + apart) * halves + within[t], 1.0, choice)
    choice_ref[...] = choice

    row = lax.broadcasted_iota(jnp.int32, info_ref.shape, 0)
    info = jnp.zeros(info_ref.shape, jnp.int32)
    for t in range(STEPS):
        start = owning[t] * members * channels + within[t] * SRC_DEV
        info = jnp.where(row == t, start, info)
    info_ref[...] = info

    rows = STEPS * windows
    row = lax.broadcasted_iota(jnp.int32, (rows, total), 0)
    lane = lax.broadcasted_iota(jnp.int32, (rows, total), 1)
    picks = jnp.zeros((rows, total), jnp.float32)
    for t in range(STEPS):
        channel = (owning[t] * members + member) * channels + within[t] * SRC_DEV + core
        picks = jnp.where((row // windows == t) & (lane == channel), 1.0, picks)
    mask_ref[...] = jnp.broadcast_to(at_window(flags_of(picks, flags)), mask_ref.shape)

    row = lax.broadcasted_iota(jnp.int32, take_ref.shape[1:], 0)
    for index in range(take_ref.shape[0]):
        take = jnp.zeros(take_ref.shape[1:], jnp.float32)
        for t in range(STEPS):
            differs = ((owning[t] // SRC_DEV) ^ plane) >> index & 1
            take = jnp.where(row // windows == t, differs.astype(jnp.float32), take)
        take_ref[index] = take


def pick_kernel(flip, choice_ref, own_ref, other_ref, out_ref, samples):
    channels, windows, length = own_ref.shape
    halves = channels // SRC_DEV
    half = (lax.axis_index("grp") + flip) % SRC_DEV
    points = length // RADIX
    for step in range(STEPS):
        held = [jnp.zeros((windows, points), jnp.float32)] * RADIX
        for k, raw_ref in enumerate((own_ref, other_ref)):
            for h in range(halves):
                index = (step * SRC_DEV + k) * halves + h
                here = jnp.broadcast_to(choice_ref[index : index + 1, :], (windows, points)) > 0.0
                row = raw_ref[h * SRC_DEV + half].astype(jnp.float32)
                for n in range(RADIX):
                    held[n] = jnp.where(here, row[:, n * points : (n + 1) * points], held[n])
        for n in range(RADIX):
            samples[step * windows : (step + 1) * windows, n * points : (n + 1) * points] = held[n]
    out_ref[...] = samples[...].astype(out_ref.dtype)


def receiver_kernel(radius, order, last_bit, info_ref, usable_ref, raw_ref, twiddle_ref, table_ref, *rest):
    spectra_ref, inverse_ref, other_ref, samples, relay = rest
    channels, windows, _ = raw_ref.shape
    members = lax.axis_size("dev")
    group, member = lax.axis_index("grp"), lax.axis_index("dev")
    core = group % SRC_DEV
    first = (group * members + member) * channels
    flags = usable_ref[...].astype(jnp.float32).astype(jnp.bfloat16)
    total = flags.shape[1]

    for r in range(channels):
        samples[r * windows : (r + 1) * windows, :] = raw_ref[r].astype(jnp.float32)
    rows = channels * windows
    row = lax.broadcasted_iota(jnp.int32, (rows, total), 0)
    lane = lax.broadcasted_iota(jnp.int32, (rows, total), 1)
    own = jnp.where(lane == first + row // windows, 1.0, 0.0)
    mask = at_window(flags_of(own, flags))
    whiten_rows(samples[...], radius, mask, twiddle_ref, table_ref, relay, spectra_ref)

    rows = STEPS * channels
    row = lax.broadcasted_iota(jnp.int32, (rows, total), 0)
    lane = lax.broadcasted_iota(jnp.int32, (rows, total), 1)
    start = jnp.zeros((rows, total), jnp.int32)
    for t in range(STEPS):
        here = jnp.broadcast_to(info_ref[t : t + 1, :1], (rows, total))
        start = jnp.where(row // channels == t, here, start)
    blocks = []
    for k, odd in order:
        offset = (member ^ k) * channels + (core + odd) % SRC_DEV
        blocks.append(jnp.where(lane == start + offset, 1.0, 0.0))
    sent = flags_of(jnp.concatenate(blocks, axis=0), flags)
    theirs = ((group ^ TURN_LAST) * members + (member ^ last_bit)) * channels
    for ref, start in ((inverse_ref, first), (other_ref, theirs)):
        received = flags_of(jnp.where(lane == start + row % channels, 1.0, 0.0), flags)
        both = sent * jnp.concatenate([received] * len(order), axis=0)
        counts = jnp.sum(both, axis=1, keepdims=True)
        ref[...] = jnp.broadcast_to(1.0 / jnp.maximum(counts, 1.0), ref.shape)


def source_kernel(radius, *refs):
    take_ref, mask_ref, kept_ref, came_ref, twiddle_ref, table_ref = refs[:6]
    out_ref, relay = refs[-2:]
    rows, length = kept_ref.shape
    points = length // RADIX
    here = take_ref[...] > 0.0
    kept, came = kept_ref[...].astype(jnp.float32), came_ref[...].astype(jnp.float32)
    here = jnp.concatenate([here] * RADIX, axis=1)
    samples = jnp.where(here, came, kept)
    whiten_rows(samples, radius, mask_ref[:, :1], twiddle_ref, table_ref, relay, out_ref)


def lagged_rows(windows, pieces, sets, table_ref, products, stacked):
    blocks = RADIX // 2

    def row_set(ref, base, first, rows):
        out = []
        for part in range(2):
            held = []
            for w in range(0, windows, 2):
                start = base + (part * rows + first + w) * blocks
                both = ref[start : start + 2 * blocks, :].astype(jnp.float32)
                held += [both[:blocks], both[blocks:]]
            out.append(held)
        return out

    pair = 0
    for recv_ref, _ in sets:
        receivers = recv_ref.shape[0] // (2 * windows * blocks)
        own = [row_set(recv_ref, 0, r * windows, receivers * windows) for r in range(receivers)]
        for ref, base in pieces:
            for step in range(STEPS):
                a, b = row_set(ref, base, step * windows, STEPS * windows)
                for r in range(receivers):
                    c, e = own[r]
                    re = im = None
                    for w in range(windows):
                        re_w = a[w] * c[w] + b[w] * e[w]
                        im_w = b[w] * c[w] - a[w] * e[w]
                        re = re_w if re is None else re + re_w
                        im = im_w if im is None else im + im_w
                    products[0, pair * blocks : (pair + 1) * blocks, :] = re
                    products[1, pair * blocks : (pair + 1) * blocks, :] = im
                    pair += 1
    width = products.shape[2]
    inverse = jnp.concatenate([factors for _, factors in sets], axis=0)
    for part in range(2):
        for q in range(blocks):
            column = (part * blocks + q) * width
            values = products[part, pl.ds(q, pair, stride=blocks), :] * inverse
            stacked[:, column : column + width] = values.astype(jnp.bfloat16)
    return jnp.dot(stacked[...], table_ref[...], preferred_element_type=jnp.float32)


def pieces_of(ref, windows):
    rows = 2 * STEPS * windows * (RADIX // 2)
    return [(ref, base) for base in range(0, ref.shape[0], rows)]


def part_kernel(windows, first, n_sets, *refs):
    table_ref, set_refs, refs = refs[0], refs[1 : 1 + 2 * n_sets], refs[1 + 2 * n_sets :]
    products, stacked = refs[-2:]
    buffers, outs = refs[: -2 - n_sets], refs[-2 - n_sets : -2]
    pieces = [piece for ref in buffers for piece in pieces_of(ref, windows)]
    rows = outs[0].shape[0]
    sets = [
        (set_refs[2 * i], set_refs[2 * i + 1][first : first + rows, :]) for i in range(n_sets)
    ]
    lagged = lagged_rows(windows, pieces, sets, table_ref, products, stacked)
    for i, out_ref in enumerate(outs):
        out_ref[...] = lagged[i * rows : (i + 1) * rows].astype(jnp.bfloat16)


def pass_kernel(value_ref, after_ref, out_ref):
    del after_ref
    out_ref[...] = value_ref[...]


def place_kernel(order, last_bit, *refs):
    out_ref = refs[-1]
    member = lax.axis_index("dev")
    core = lax.axis_index("grp") % SRC_DEV
    receivers = out_ref.shape[2]
    whole = order + [(k ^ last_bit, odd ^ TURN_LAST) for k, odd in order]
    block = STEPS * receivers
    done = 0
    for ref in refs[:-1]:
        for p in range(ref.shape[0] // block):
            k, odd = whole[done]
            source = (member ^ k) * SRC_DEV + (core + odd) % SRC_DEV
            for step in range(STEPS):
                row = p * block + step * receivers
                out_ref[step, source] = ref[row : row + receivers, :]
            done += 1


def on_device(records, usable, panel_ids):
    channels, windows, length = records.shape
    bin_count = length // 2
    radius = bin_count // 16
    halves = channels // SRC_DEV
    groups = lax.axis_size("grp")
    members = lax.axis_size("dev")
    blocks = RADIX // 2
    width = bin_count // blocks

    def exchange(value, group_bit, member_bit):
        flip = group_bit * members + member_bit
        pairs = [(i, i ^ flip) for i in range(groups * members)]
        return lax.ppermute(value, AXES, pairs)

    ltable = jnp.asarray(lag_table(length, bin_count, NLAG))
    all_bits = [1 << i for i in range(members.bit_length() - 1)]
    chosen = [all_bits[i] for i in BIT_ORDER]
    *gather_bits, last_bit = [b for b in all_bits[::-1] if b not in chosen] + chosen
    order = panel_order(gather_bits)

    usable_rows = usable.T
    planes = groups // SRC_DEV
    source_rows = STEPS * windows
    plane_bits = planes.bit_length() - 1

    records_other = exchange(records, 1, 0)
    points = length // RADIX
    table, twiddle = pl.pallas_call(
        functools.partial(tables_kernel, length),
        out_shape=[
            jax.ShapeDtypeStruct((2, 4 * points, 2 * points), jnp.bfloat16),
            jax.ShapeDtypeStruct((2, RADIX, points), jnp.float32),
        ],
        in_specs=[],
        out_specs=[VMEM] * 2,
        compiler_params=PARAMS,
        cost_estimate=AHEAD,
        name="short_tables",
    )()

    choice, mask, take, info = pl.pallas_call(
        functools.partial(choice_kernel, halves, channels),
        out_shape=[
            jax.ShapeDtypeStruct((STEPS * SRC_DEV * halves, width), jnp.float32),
            jax.ShapeDtypeStruct((source_rows, width), jnp.float32),
            jax.ShapeDtypeStruct((plane_bits, source_rows, width), jnp.float32),
            jax.ShapeDtypeStruct((8, width), jnp.int32),
        ],
        in_specs=[SMEM] + [VMEM] * 2,
        out_specs=[VMEM] * 4,
        compiler_params=PARAMS,
        name="choose_rows",
    )(panel_ids, usable_rows, twiddle)

    def pick(flip):
        return pl.pallas_call(
            functools.partial(pick_kernel, flip),
            out_shape=jax.ShapeDtypeStruct((source_rows, length), records.dtype),
            in_specs=[VMEM] * 3,
            out_specs=VMEM,
            scratch_shapes=[pltpu.VMEM((source_rows, length), jnp.float32)],
            compiler_params=PARAMS,
            name="pick_rows",
        )(choice, records, records_other)

    sent = pick(TURN_PLANE)
    came = exchange(sent, SRC_DEV * (planes // 2) + TURN_PLANE, 0)
    kept = pick(0) if TURN_PLANE else sent
    for index in range(plane_bits - 2, -1, -1):
        kept = jnp.where(take[index + 1][:, :1] > 0.0, came, kept)
        came = exchange(kept, SRC_DEV << index, 0)

    row_count = channels * windows
    pairs = len(order) * STEPS * channels
    receivers, inverse, inverse_theirs = pl.pallas_call(
        functools.partial(receiver_kernel, radius, order, last_bit),
        out_shape=[
            jax.ShapeDtypeStruct((2 * row_count * blocks, width), jnp.bfloat16),
            jax.ShapeDtypeStruct((pairs, width), jnp.float32),
            jax.ShapeDtypeStruct((pairs, width), jnp.float32),
        ],
        in_specs=[VMEM] * 5,
        out_specs=[VMEM] * 3,
        scratch_shapes=[
            pltpu.VMEM((row_count, length), jnp.float32),
            pltpu.VMEM((2 * row_count * blocks, width), jnp.float32),
        ],
        compiler_params=PARAMS,
        cost_estimate=AHEAD,
        name="receiver_spectra",
    )(info, usable_rows, records, twiddle, table)

    piece = pl.pallas_call(
        functools.partial(source_kernel, radius),
        out_shape=jax.ShapeDtypeStruct((2 * source_rows * blocks, width), jnp.bfloat16),
        in_specs=[VMEM] * 7,
        out_specs=VMEM,
        scratch_shapes=[pltpu.VMEM((2 * source_rows * blocks, width), jnp.float32)],
        compiler_params=PARAMS,
        name="source_spectra",
    )(take[0], mask, kept, came, twiddle, table, receivers)

    def part(first, sets, *buffers, cost=BESIDE):
        rows = sum(b.shape[0] for b in buffers) // (2 * windows * blocks) * channels
        total = rows * len(sets)
        return pl.pallas_call(
            functools.partial(part_kernel, windows, first, len(sets)),
            out_shape=[jax.ShapeDtypeStruct((rows, NLAG), jnp.bfloat16)] * len(sets),
            in_specs=[VMEM] * (1 + 2 * len(sets) + len(buffers)),
            out_specs=[VMEM] * len(sets),
            scratch_shapes=[
                pltpu.VMEM((2, total * blocks, width), jnp.float32),
                pltpu.VMEM((total, 2 * bin_count), jnp.bfloat16),
            ],
            compiler_params=PARAMS,
            cost_estimate=cost,
            name="correlate_part",
        )(ltable, *[array for pair in sets for array in pair], *buffers)

    def pass_on(value, after):
        return pl.pallas_call(
            pass_kernel,
            out_shape=jax.ShapeDtypeStruct(value.shape, value.dtype),
            in_specs=[VMEM] * 2,
            out_specs=VMEM,
            compiler_params=PARAMS,
            name="pass_on",
        )(value, after)

    held = piece
    for index, bit in enumerate(gather_bits[:-2]):
        held = jnp.concatenate([held, exchange(held, turn(index), bit)], axis=0)
    rounds = len(gather_bits)
    theirs = exchange(receivers, TURN_LAST, last_bit)
    fresh = pass_on(exchange(held, turn(rounds - 2), gather_bits[-2]), theirs)
    first = exchange(held, turn(rounds - 1), gather_bits[-1])
    second = exchange(fresh, turn(rounds - 1), gather_bits[-1])
    held = jnp.concatenate([held, fresh], axis=0)
    pieces = [held, exchange(held, 1, 0), first, exchange(first, 1, 0)]
    pieces += [second, exchange(second, 1, 0)]
    mine, other = (receivers, inverse), (theirs, inverse_theirs)
    early_theirs, early = part(0, [other, mine], held)
    (next_theirs,) = part(pairs // 4, [other], *pieces[1:4])
    (late_theirs,) = part(pairs // 4 * 3, [other], *pieces[4:])
    (late,) = part(pairs // 4, [mine], *pieces[1:])
    back = exchange(jnp.concatenate([early_theirs, next_theirs, late_theirs], axis=0), TURN_LAST, last_bit)
    return pl.pallas_call(
        functools.partial(place_kernel, order, last_bit),
        out_shape=jax.ShapeDtypeStruct(
            (STEPS, members * SRC_DEV, channels, NLAG), jnp.bfloat16
        ),
        in_specs=[VMEM] * 3,
        out_specs=VMEM,
        compiler_params=PARAMS,
        name="place_rows",
    )(early, late, back)


def solution(mesh):
    placed = (P(AXES, None, None), P(), P())
    return jax.shard_map(
        on_device,
        mesh=mesh,
        in_specs=placed,
        out_specs=P(None, None, AXES, None),
        check_vma=False,
    )
```

```python
import functools
import math

import jax
import jax.numpy as jnp
import ml_dtypes
import numpy as np
from jax import lax
from jax.experimental import pallas as pl
from jax.experimental.pallas import tpu as pltpu
from jax.sharding import PartitionSpec as P

NLAG = 512
SRC_DEV = 2
STEPS = 2
RADIX = 16
AXES = ("grp", "dev")
TURN_PLANE, TURN_GATHER, TURN_LAST = 1, (1, 1), 1
BIT_ORDER = (2, 0, 1)
VMEM = pl.BlockSpec(memory_space=pltpu.VMEM)
AHEAD = pl.CostEstimate(flops=5_000_000_000, bytes_accessed=1_000_000, transcendentals=0)
BESIDE = pl.CostEstimate(flops=1_000_000_000, bytes_accessed=1_000_000, transcendentals=0)
PARAMS = pltpu.CompilerParams(vmem_limit_bytes=16 * 1024 * 1024)


def bin_order(bin_count):
    per = bin_count // RADIX
    order = []
    for q in range(RADIX // 2):
        for h in range(2):
            order.append(RADIX * np.arange(per) + 2 * q + h + 1)
    return np.concatenate(order)


def tables_kernel(length, table_ref, twiddle_ref):
    points = length // RADIX
    per = points // 2
    row = lax.broadcasted_iota(jnp.int32, (points, points), 0)
    lane = lax.broadcasted_iota(jnp.int32, (points, points), 1)
    phases = (2.0 * math.pi / points) * (row * (lane % per) % points).astype(jnp.float32)
    cosine, sine = jnp.cos(phases), jnp.sin(phases)
    for h in range(2):
        inside = (lane >= per) if h else (lane < per)
        c, s = jnp.where(inside, cosine, 0.0), jnp.where(inside, sine, 0.0)
        for part, values in enumerate(((c, -s), (s, c))):
            rows = slice((2 * h + part) * points, (2 * h + part + 1) * points)
            whole = jnp.concatenate(values, axis=1)
            high = whole.astype(jnp.bfloat16)
            table_ref[0, rows, :] = high
            table_ref[1, rows, :] = (whole - high.astype(jnp.float32)).astype(jnp.bfloat16)
    residue = lax.broadcasted_iota(jnp.int32, (RADIX, points), 0) + 1
    sample = lax.broadcasted_iota(jnp.int32, (RADIX, points), 1)
    phases = (2.0 * math.pi / length) * (residue * sample).astype(jnp.float32)
    twiddle_ref[0] = jnp.cos(phases)
    twiddle_ref[1] = -jnp.sin(phases)


def lag_table(length, bin_count, lag_count):
    bins = bin_order(bin_count)[:, None]
    lags = np.arange(lag_count)[None, :] - lag_count // 2
    phases = 2.0 * np.pi / length * (bins * lags % length)
    factor = 1.0 / math.sqrt(bin_count)
    cosine, sine = np.cos(phases) * factor, -np.sin(phases) * factor
    return np.concatenate([cosine, sine], axis=0).astype(ml_dtypes.bfloat16)


def real_dft(values):
    n = len(values)
    if n == 1:
        return [(values[0], None)]
    if n == 2:
        return [(values[0] + values[1], None), (values[0] - values[1], None)]
    even, odd = real_dft(values[0::2]), real_dft(values[1::2])
    quarter = n // 4
    out = [None] * (n // 2 + 1)
    for r in range(quarter + 1):
        (er, ei), (orr, oi) = even[r], odd[r]
        cosine, sine = math.cos(2 * math.pi * r / n), math.sin(2 * math.pi * r / n)
        if r == 0:
            tr, ti = orr, None
        elif r == quarter:
            tr, ti = None, -orr
        elif 8 * r == n:
            tr, ti = (orr + oi) * cosine, (oi - orr) * cosine
        else:
            tr, ti = orr * cosine + oi * sine, oi * cosine - orr * sine
        plus_re = er if tr is None else er + tr
        minus_re = er if tr is None else er - tr
        if ei is None:
            plus_im, minus_im = ti, ti
        elif ti is None:
            plus_im, minus_im = ei, -ei
        else:
            plus_im, minus_im = ei + ti, ti - ei
        out[r] = (plus_re, plus_im)
        if r < quarter:
            out[n // 2 - r] = (minus_re, minus_im)
    return out


def spectrum(samples, twiddle_ref, table_ref):
    rows, length = samples.shape
    points = length // RADIX
    half = real_dft([samples[:, i * points : (i + 1) * points] for i in range(RADIX)])
    lanes = []
    for residue in range(1, RADIX + 1):
        folded = min(residue, RADIX - residue)
        re, im = half[folded]
        if residue > RADIX // 2 and im is not None:
            im = -im
        cosine = twiddle_ref[0, residue - 1 : residue, :]
        sine = twiddle_ref[1, residue - 1 : residue, :]
        if im is None:
            lanes.append((re * cosine, re * sine))
        else:
            lanes.append((re * cosine - im * sine, re * sine + im * cosine))
    blocks = []
    for q in range(RADIX // 2):
        (ar, ai), (br, bi) = lanes[2 * q], lanes[2 * q + 1]
        blocks.append(jnp.concatenate([ar, ai, br, bi], axis=1))
    stacked = jnp.concatenate(blocks, axis=0)
    high = stacked.astype(jnp.bfloat16)
    low = (stacked - high.astype(jnp.float32)).astype(jnp.bfloat16)
    both = jnp.dot(
        jnp.concatenate([high, low], axis=0), table_ref[0], preferred_element_type=jnp.float32
    )
    count = stacked.shape[0]
    out = both[:count] + both[count:]
    out = out + jnp.dot(high, table_ref[1], preferred_element_type=jnp.float32)
    width = out.shape[1] // 2
    re = [out[q * rows : (q + 1) * rows, :width] for q in range(RADIX // 2)]
    im = [out[q * rows : (q + 1) * rows, width:] for q in range(RADIX // 2)]
    return re, im


def scales(re, im, radius, mask):
    amp = [jnp.sqrt(a * a + b * b) for a, b in zip(re, im)]
    rows, width = amp[0].shape
    per = width // 2
    reach = radius // RADIX
    lane = lax.broadcasted_iota(jnp.int32, (rows, width), 1)
    place = lane % per
    upper = lane >= per
    swapped = [pltpu.roll(a, per, 1) for a in amp]
    pair = [a + b for a, b in zip(amp, swapped)]
    total = pair[0]
    for value in pair[1:]:
        total = total + value

    def shifted(value, by):
        moved = pltpu.roll(value, (-by) % width, 1)
        inside = (place + by >= 0) & (place + by < per)
        return jnp.where(inside, moved, 0.0)

    centre = total
    for by in range(1, reach):
        centre = centre + shifted(total, by) + shifted(total, -by)
    before = jnp.zeros_like(total)
    out = []
    for a, b, both in zip(amp, swapped, pair):
        upto = before + a + jnp.where(upper, b, 0.0)
        before_here = before + jnp.where(upper, b, 0.0)
        onward = total - before_here
        before = before + both
        out.append((upto, onward))
    result = []
    for upto, onward in out:
        summed = centre + shifted(upto, reach) + shifted(onward, -reach)
        result.append(mask / (summed * (1.0 / (2 * radius + 1)) + 1e-06))
    return result


def whiten_rows(samples, radius, mask, twiddle_ref, table_ref, relay_ref, out_ref):
    rows = samples.shape[0]
    blocks = RADIX // 2
    re, im = spectrum(samples, twiddle_ref, table_ref)
    scale = scales(re, im, radius, mask)
    for part, values in enumerate((re, im)):
        for q in range(blocks):
            relay_ref[pl.ds(part * rows * blocks + q, rows, stride=blocks), :] = (
                values[q] * scale[q]
            )
    out_ref[...] = relay_ref[...].astype(jnp.bfloat16)


def turn(index):
    return TURN_GATHER[min(index, len(TURN_GATHER) - 1)]


def panel_order(bits):
    held = [(0, 0)]
    for index, bit in enumerate(bits[:-1]):
        first = len(held)
        held = held + [(k ^ bit, odd ^ turn(index)) for k, odd in held]
    last = [(k ^ bits[-1], odd ^ turn(len(bits) - 1)) for k, odd in held]
    order = []
    for pieces in (held, last[:first], last[first:]):
        order += pieces + [(k, 1 - odd) for k, odd in pieces]
    return order


def flags_of(picks, flags):
    return lax.dot_general(
        picks.astype(jnp.bfloat16),
        flags,
        (((1,), (1,)), ((), ())),
        preferred_element_type=jnp.float32,
    )


def at_window(rows_flags):
    row = lax.broadcasted_iota(jnp.int32, rows_flags.shape, 0)
    column = lax.broadcasted_iota(jnp.int32, rows_flags.shape, 1)
    kept = jnp.where(row % rows_flags.shape[1] == column, rows_flags, 0.0)
    return jnp.sum(kept, axis=1, keepdims=True)


def choice_kernel(halves, channels, ids_ref, usable_ref, after_ref, *outs):
    del after_ref
    choice_ref, mask_ref, take_ref, info_ref = outs
    windows, total = usable_ref.shape
    members = lax.axis_size("dev")
    group, member = lax.axis_index("grp"), lax.axis_index("dev")
    core, plane = group % SRC_DEV, group // SRC_DEV
    flags = usable_ref[...].astype(jnp.float32).astype(jnp.bfloat16)

    def panel(step, shape):
        chosen = jnp.broadcast_to(ids_ref[:, step : step + 1], shape)
        return lax.div(chosen, halves), lax.rem(chosen, halves)

    row = lax.broadcasted_iota(jnp.int32, choice_ref.shape, 0)
    choice = jnp.zeros(choice_ref.shape, jnp.float32)
    for t in range(STEPS):
        owning, within = panel(t, choice_ref.shape)
        apart = lax.rem(owning + core, SRC_DEV)
        choice = jnp.where(row == (t * SRC_DEV + apart) * halves + within, 1.0, choice)
    choice_ref[...] = choice

    row = lax.broadcasted_iota(jnp.int32, info_ref.shape, 0)
    info = jnp.zeros(info_ref.shape, jnp.int32)
    for t in range(STEPS):
        owning, within = panel(t, info_ref.shape)
        info = jnp.where(row == t, owning * (members * channels) + within * SRC_DEV, info)
    info_ref[...] = info

    shape = (STEPS * windows, total)
    row = lax.broadcasted_iota(jnp.int32, shape, 0)
    lane = lax.broadcasted_iota(jnp.int32, shape, 1)
    picks = jnp.zeros(shape, jnp.float32)
    for t in range(STEPS):
        owning, within = panel(t, shape)
        channel = (owning * members + member) * channels + within * SRC_DEV + core
        picks = jnp.where((row // windows == t) & (lane == channel), 1.0, picks)
    mask_ref[...] = jnp.broadcast_to(at_window(flags_of(picks, flags)), mask_ref.shape)

    shape = take_ref.shape[1:]
    row = lax.broadcasted_iota(jnp.int32, shape, 0)
    for index in range(take_ref.shape[0]):
        take = jnp.zeros(shape, jnp.float32)
        for t in range(STEPS):
            owning, _ = panel(t, shape)
            differs = (lax.div(owning, SRC_DEV) ^ plane) & (1 << index)
            take = jnp.where((row // windows == t) & (differs != 0), 1.0, take)
        take_ref[index] = take


def pick_kernel(flip, choice_ref, own_ref, other_ref, after_ref, out_ref, samples):
    del after_ref
    channels, windows, length = own_ref.shape
    halves = channels // SRC_DEV
    half = (lax.axis_index("grp") + flip) % SRC_DEV
    points = length // RADIX
    for step in range(STEPS):
        held = [jnp.zeros((windows, points), jnp.float32)] * RADIX
        for k, raw_ref in enumerate((own_ref, other_ref)):
            for h in range(halves):
                index = (step * SRC_DEV + k) * halves + h
                here = jnp.broadcast_to(choice_ref[index : index + 1, :], (windows, points)) > 0.0
                row = raw_ref[h * SRC_DEV + half].astype(jnp.float32)
                for n in range(RADIX):
                    held[n] = jnp.where(here, row[:, n * points : (n + 1) * points], held[n])
        for n in range(RADIX):
            samples[step * windows : (step + 1) * windows, n * points : (n + 1) * points] = held[n]
    out_ref[...] = samples[...].astype(out_ref.dtype)


def receiver_kernel(radius, order, last_bit, info_ref, usable_ref, raw_ref, twiddle_ref, table_ref, *rest):
    spectra_ref, inverse_ref, other_ref, samples, relay = rest
    channels, windows, _ = raw_ref.shape
    members = lax.axis_size("dev")
    group, member = lax.axis_index("grp"), lax.axis_index("dev")
    core = group % SRC_DEV
    first = (group * members + member) * channels
    flags = usable_ref[...].astype(jnp.float32).astype(jnp.bfloat16)
    total = flags.shape[1]

    for r in range(channels):
        samples[r * windows : (r + 1) * windows, :] = raw_ref[r].astype(jnp.float32)
    rows = channels * windows
    row = lax.broadcasted_iota(jnp.int32, (rows, total), 0)
    lane = lax.broadcasted_iota(jnp.int32, (rows, total), 1)
    own = jnp.where(lane == first + row // windows, 1.0, 0.0)
    mask = at_window(flags_of(own, flags))
    whiten_rows(samples[...], radius, mask, twiddle_ref, table_ref, relay, spectra_ref)

    rows = STEPS * channels
    row = lax.broadcasted_iota(jnp.int32, (rows, total), 0)
    lane = lax.broadcasted_iota(jnp.int32, (rows, total), 1)
    start = jnp.zeros((rows, total), jnp.int32)
    for t in range(STEPS):
        here = jnp.broadcast_to(info_ref[t : t + 1, :1], (rows, total))
        start = jnp.where(row // channels == t, here, start)
    blocks = []
    for k, odd in order:
        offset = (member ^ k) * channels + (core + odd) % SRC_DEV
        blocks.append(jnp.where(lane == start + offset, 1.0, 0.0))
    sent = flags_of(jnp.concatenate(blocks, axis=0), flags)
    theirs = ((group ^ TURN_LAST) * members + (member ^ last_bit)) * channels
    for ref, start in ((inverse_ref, first), (other_ref, theirs)):
        received = flags_of(jnp.where(lane == start + row % channels, 1.0, 0.0), flags)
        both = sent * jnp.concatenate([received] * len(order), axis=0)
        counts = jnp.sum(both, axis=1, keepdims=True)
        ref[...] = jnp.broadcast_to(1.0 / jnp.maximum(counts, 1.0), ref.shape)


def source_kernel(radius, *refs):
    take_ref, mask_ref, kept_ref, came_ref, twiddle_ref, table_ref = refs[:6]
    out_ref, relay = refs[-2:]
    rows, length = kept_ref.shape
    points = length // RADIX
    here = take_ref[...] > 0.0
    kept, came = kept_ref[...].astype(jnp.float32), came_ref[...].astype(jnp.float32)
    here = jnp.concatenate([here] * RADIX, axis=1)
    samples = jnp.where(here, came, kept)
    whiten_rows(samples, radius, mask_ref[:, :1], twiddle_ref, table_ref, relay, out_ref)


def lagged_rows(windows, pieces, sets, table_ref, products, stacked):
    blocks = RADIX // 2

    def row_set(ref, base, first, rows):
        out = []
        for part in range(2):
            held = []
            for w in range(0, windows, 2):
                start = base + (part * rows + first + w) * blocks
                both = ref[start : start + 2 * blocks, :].astype(jnp.float32)
                held += [both[:blocks], both[blocks:]]
            out.append(held)
        return out

    pair = 0
    for recv_ref, _ in sets:
        receivers = recv_ref.shape[0] // (2 * windows * blocks)
        own = [row_set(recv_ref, 0, r * windows, receivers * windows) for r in range(receivers)]
        for ref, base in pieces:
            for step in range(STEPS):
                a, b = row_set(ref, base, step * windows, STEPS * windows)
                for r in range(receivers):
                    c, e = own[r]
                    re = im = None
                    for w in range(windows):
                        re_w = a[w] * c[w] + b[w] * e[w]
                        im_w = b[w] * c[w] - a[w] * e[w]
                        re = re_w if re is None else re + re_w
                        im = im_w if im is None else im + im_w
                    products[0, pair * blocks : (pair + 1) * blocks, :] = re
                    products[1, pair * blocks : (pair + 1) * blocks, :] = im
                    pair += 1
    width = products.shape[2]
    inverse = jnp.concatenate([factors for _, factors in sets], axis=0)
    for part in range(2):
        for q in range(blocks):
            column = (part * blocks + q) * width
            values = products[part, pl.ds(q, pair, stride=blocks), :] * inverse
            stacked[:, column : column + width] = values.astype(jnp.bfloat16)
    return jnp.dot(stacked[...], table_ref[...], preferred_element_type=jnp.float32)


def pieces_of(ref, windows):
    rows = 2 * STEPS * windows * (RADIX // 2)
    return [(ref, base) for base in range(0, ref.shape[0], rows)]


def part_kernel(windows, first, n_sets, *refs):
    table_ref, set_refs, refs = refs[0], refs[1 : 1 + 2 * n_sets], refs[1 + 2 * n_sets :]
    products, stacked = refs[-2:]
    buffers, outs = refs[: -2 - n_sets], refs[-2 - n_sets : -2]
    pieces = [piece for ref in buffers for piece in pieces_of(ref, windows)]
    rows = outs[0].shape[0]
    sets = [
        (set_refs[2 * i], set_refs[2 * i + 1][first : first + rows, :]) for i in range(n_sets)
    ]
    lagged = lagged_rows(windows, pieces, sets, table_ref, products, stacked)
    for i, out_ref in enumerate(outs):
        out_ref[...] = lagged[i * rows : (i + 1) * rows].astype(jnp.bfloat16)


def pass_kernel(value_ref, after_ref, out_ref):
    del after_ref
    out_ref[...] = value_ref[...]


def place_kernel(order, last_bit, *refs):
    out_ref = refs[-1]
    member = lax.axis_index("dev")
    core = lax.axis_index("grp") % SRC_DEV
    receivers = out_ref.shape[2]
    whole = order + [(k ^ last_bit, odd ^ TURN_LAST) for k, odd in order]
    block = STEPS * receivers
    done = 0
    for ref in refs[:-1]:
        for p in range(ref.shape[0] // block):
            k, odd = whole[done]
            source = (member ^ k) * SRC_DEV + (core + odd) % SRC_DEV
            for step in range(STEPS):
                row = p * block + step * receivers
                out_ref[step, source] = ref[row : row + receivers, :]
            done += 1


def on_device(records, usable, panel_ids):
    channels, windows, length = records.shape
    bin_count = length // 2
    radius = bin_count // 16
    halves = channels // SRC_DEV
    groups = lax.axis_size("grp")
    members = lax.axis_size("dev")
    blocks = RADIX // 2
    width = bin_count // blocks

    def exchange(value, group_bit, member_bit):
        flip = group_bit * members + member_bit
        pairs = [(i, i ^ flip) for i in range(groups * members)]
        return lax.ppermute(value, AXES, pairs)

    ltable = jnp.asarray(lag_table(length, bin_count, NLAG))
    all_bits = [1 << i for i in range(members.bit_length() - 1)]
    chosen = [all_bits[i] for i in BIT_ORDER]
    *gather_bits, last_bit = [b for b in all_bits[::-1] if b not in chosen] + chosen
    order = panel_order(gather_bits)

    usable_rows = usable.T
    planes = groups // SRC_DEV
    source_rows = STEPS * windows
    plane_bits = planes.bit_length() - 1

    records_other = exchange(records, 1, 0)
    points = length // RADIX
    table, twiddle = pl.pallas_call(
        functools.partial(tables_kernel, length),
        out_shape=[
            jax.ShapeDtypeStruct((2, 4 * points, 2 * points), jnp.bfloat16),
            jax.ShapeDtypeStruct((2, RADIX, points), jnp.float32),
        ],
        in_specs=[],
        out_specs=[VMEM] * 2,
        compiler_params=PARAMS,
        cost_estimate=AHEAD,
        name="short_tables",
    )()

    choice, mask, take, info = pl.pallas_call(
        functools.partial(choice_kernel, halves, channels),
        out_shape=[
            jax.ShapeDtypeStruct((STEPS * SRC_DEV * halves, width), jnp.float32),
            jax.ShapeDtypeStruct((source_rows, width), jnp.float32),
            jax.ShapeDtypeStruct((plane_bits, source_rows, width), jnp.float32),
            jax.ShapeDtypeStruct((8, width), jnp.int32),
        ],
        in_specs=[VMEM] * 3,
        out_specs=[VMEM] * 4,
        compiler_params=PARAMS,
        name="choose_rows",
    )(panel_ids[None, :], usable_rows, twiddle)

    row_count = channels * windows
    pairs = len(order) * STEPS * channels
    receivers, inverse, inverse_theirs = pl.pallas_call(
        functools.partial(receiver_kernel, radius, order, last_bit),
        out_shape=[
            jax.ShapeDtypeStruct((2 * row_count * blocks, width), jnp.bfloat16),
            jax.ShapeDtypeStruct((pairs, width), jnp.float32),
            jax.ShapeDtypeStruct((pairs, width), jnp.float32),
        ],
        in_specs=[VMEM] * 5,
        out_specs=[VMEM] * 3,
        scratch_shapes=[
            pltpu.VMEM((row_count, length), jnp.float32),
            pltpu.VMEM((2 * row_count * blocks, width), jnp.float32),
        ],
        compiler_params=PARAMS,
        cost_estimate=AHEAD,
        name="receiver_spectra",
    )(info, usable_rows, records, twiddle, table)

    def pick(flip):
        return pl.pallas_call(
            functools.partial(pick_kernel, flip),
            out_shape=jax.ShapeDtypeStruct((source_rows, length), records.dtype),
            in_specs=[VMEM] * 4,
            out_specs=VMEM,
            scratch_shapes=[pltpu.VMEM((source_rows, length), jnp.float32)],
            compiler_params=PARAMS,
            name="pick_rows",
        )(choice, records, records_other, inverse)

    sent = pick(TURN_PLANE)
    came = exchange(sent, SRC_DEV * (planes // 2) + TURN_PLANE, 0)
    kept = pick(0) if TURN_PLANE else sent
    for index in range(plane_bits - 2, -1, -1):
        kept = jnp.where(take[index + 1][:, :1] > 0.0, came, kept)
        came = exchange(kept, SRC_DEV << index, 0)

    piece = pl.pallas_call(
        functools.partial(source_kernel, radius),
        out_shape=jax.ShapeDtypeStruct((2 * source_rows * blocks, width), jnp.bfloat16),
        in_specs=[VMEM] * 7,
        out_specs=VMEM,
        scratch_shapes=[pltpu.VMEM((2 * source_rows * blocks, width), jnp.float32)],
        compiler_params=PARAMS,
        name="source_spectra",
    )(take[0], mask, kept, came, twiddle, table, receivers)

    def part(first, sets, *buffers, cost=BESIDE):
        rows = sum(b.shape[0] for b in buffers) // (2 * windows * blocks) * channels
        total = rows * len(sets)
        return pl.pallas_call(
            functools.partial(part_kernel, windows, first, len(sets)),
            out_shape=[jax.ShapeDtypeStruct((rows, NLAG), jnp.bfloat16)] * len(sets),
            in_specs=[VMEM] * (1 + 2 * len(sets) + len(buffers)),
            out_specs=[VMEM] * len(sets),
            scratch_shapes=[
                pltpu.VMEM((2, total * blocks, width), jnp.float32),
                pltpu.VMEM((total, 2 * bin_count), jnp.bfloat16),
            ],
            compiler_params=PARAMS,
            cost_estimate=cost,
            name="correlate_part",
        )(ltable, *[array for pair in sets for array in pair], *buffers)

    def pass_on(value, after):
        return pl.pallas_call(
            pass_kernel,
            out_shape=jax.ShapeDtypeStruct(value.shape, value.dtype),
            in_specs=[VMEM] * 2,
            out_specs=VMEM,
            compiler_params=PARAMS,
            name="pass_on",
        )(value, after)

    held = piece
    for index, bit in enumerate(gather_bits[:-2]):
        held = jnp.concatenate([held, exchange(held, turn(index), bit)], axis=0)
    rounds = len(gather_bits)
    theirs = exchange(receivers, TURN_LAST, last_bit)
    fresh = pass_on(exchange(held, turn(rounds - 2), gather_bits[-2]), theirs)
    first = exchange(held, turn(rounds - 1), gather_bits[-1])
    second = exchange(fresh, turn(rounds - 1), gather_bits[-1])
    held = jnp.concatenate([held, fresh], axis=0)
    pieces = [held, exchange(held, 1, 0), first, exchange(first, 1, 0)]
    pieces += [second, exchange(second, 1, 0)]
    mine, other = (receivers, inverse), (theirs, inverse_theirs)
    early_theirs, early = part(0, [other, mine], held)
    (next_theirs,) = part(pairs // 4, [other], *pieces[1:4])
    (late_theirs,) = part(pairs // 4 * 3, [other], *pieces[4:])
    (late,) = part(pairs // 4, [mine], *pieces[1:])
    back = exchange(jnp.concatenate([early_theirs, next_theirs, late_theirs], axis=0), TURN_LAST, last_bit)
    return pl.pallas_call(
        functools.partial(place_kernel, order, last_bit),
        out_shape=jax.ShapeDtypeStruct(
            (STEPS, members * SRC_DEV, channels, NLAG), jnp.bfloat16
        ),
        in_specs=[VMEM] * 3,
        out_specs=VMEM,
        compiler_params=PARAMS,
        name="place_rows",
    )(early, late, back)


def solution(mesh):
    placed = (P(AXES, None, None), P(), P())
    return jax.shard_map(
        on_device,
        mesh=mesh,
        in_specs=placed,
        out_specs=P(None, None, AXES, None),
        check_vma=False,
    )
```

```python
import functools
import math

import jax
import jax.numpy as jnp
import ml_dtypes
import numpy as np
from jax import lax
from jax.experimental import pallas as pl
from jax.experimental.pallas import tpu as pltpu
from jax.sharding import PartitionSpec as P

NLAG = 512
SRC_DEV = 2
STEPS = 2
RADIX = 16
AXES = ("grp", "dev")
TURN_PLANE, TURN_GATHER, TURN_LAST = 1, (1, 1), 1
BIT_ORDER = (2, 0, 1)
VMEM = pl.BlockSpec(memory_space=pltpu.VMEM)
AHEAD = pl.CostEstimate(flops=5_000_000_000, bytes_accessed=1_000_000, transcendentals=0)
BESIDE = pl.CostEstimate(flops=1_000_000_000, bytes_accessed=1_000_000, transcendentals=0)
PARAMS = pltpu.CompilerParams(vmem_limit_bytes=16 * 1024 * 1024)


def bin_order(bin_count):
    per = bin_count // RADIX
    order = []
    for q in range(RADIX // 2):
        for h in range(2):
            order.append(RADIX * np.arange(per) + 2 * q + h + 1)
    return np.concatenate(order)


def tables_kernel(length, table_ref, twiddle_ref):
    points = length // RADIX
    per = points // 2
    row = lax.broadcasted_iota(jnp.int32, (points, points), 0)
    lane = lax.broadcasted_iota(jnp.int32, (points, points), 1)
    phases = (2.0 * math.pi / points) * (row * (lane % per) % points).astype(jnp.float32)
    cosine, sine = jnp.cos(phases), jnp.sin(phases)
    for h in range(2):
        inside = (lane >= per) if h else (lane < per)
        c, s = jnp.where(inside, cosine, 0.0), jnp.where(inside, sine, 0.0)
        for part, values in enumerate(((c, -s), (s, c))):
            rows = slice((2 * h + part) * points, (2 * h + part + 1) * points)
            whole = jnp.concatenate(values, axis=1)
            table_ref[rows, :] = whole.astype(jnp.bfloat16)
    residue = lax.broadcasted_iota(jnp.int32, (RADIX, points), 0) + 1
    sample = lax.broadcasted_iota(jnp.int32, (RADIX, points), 1)
    phases = (2.0 * math.pi / length) * (residue * sample).astype(jnp.float32)
    twiddle_ref[0] = jnp.cos(phases)
    twiddle_ref[1] = -jnp.sin(phases)


def lag_table(length, bin_count, lag_count):
    bins = bin_order(bin_count)[:, None]
    lags = np.arange(lag_count)[None, :] - lag_count // 2
    phases = 2.0 * np.pi / length * (bins * lags % length)
    factor = 1.0 / math.sqrt(bin_count)
    cosine, sine = np.cos(phases) * factor, -np.sin(phases) * factor
    return np.concatenate([cosine, sine], axis=0).astype(ml_dtypes.bfloat16)


def real_dft(values):
    n = len(values)
    if n == 1:
        return [(values[0], None)]
    if n == 2:
        return [(values[0] + values[1], None), (values[0] - values[1], None)]
    even, odd = real_dft(values[0::2]), real_dft(values[1::2])
    quarter = n // 4
    out = [None] * (n // 2 + 1)
    for r in range(quarter + 1):
        (er, ei), (orr, oi) = even[r], odd[r]
        cosine, sine = math.cos(2 * math.pi * r / n), math.sin(2 * math.pi * r / n)
        if r == 0:
            tr, ti = orr, None
        elif r == quarter:
            tr, ti = None, -orr
        elif 8 * r == n:
            tr, ti = (orr + oi) * cosine, (oi - orr) * cosine
        else:
            tr, ti = orr * cosine + oi * sine, oi * cosine - orr * sine
        plus_re = er if tr is None else er + tr
        minus_re = er if tr is None else er - tr
        if ei is None:
            plus_im, minus_im = ti, ti
        elif ti is None:
            plus_im, minus_im = ei, -ei
        else:
            plus_im, minus_im = ei + ti, ti - ei
        out[r] = (plus_re, plus_im)
        if r < quarter:
            out[n // 2 - r] = (minus_re, minus_im)
    return out


def spectrum(samples, twiddle_ref, table_ref):
    rows, length = samples.shape
    points = length // RADIX
    half = real_dft([samples[:, i * points : (i + 1) * points] for i in range(RADIX)])
    lanes = []
    for residue in range(1, RADIX + 1):
        folded = min(residue, RADIX - residue)
        re, im = half[folded]
        if residue > RADIX // 2 and im is not None:
            im = -im
        cosine = twiddle_ref[0, residue - 1 : residue, :]
        sine = twiddle_ref[1, residue - 1 : residue, :]
        if im is None:
            lanes.append((re * cosine, re * sine))
        else:
            lanes.append((re * cosine - im * sine, re * sine + im * cosine))
    blocks = []
    for q in range(RADIX // 2):
        (ar, ai), (br, bi) = lanes[2 * q], lanes[2 * q + 1]
        blocks.append(jnp.concatenate([ar, ai, br, bi], axis=1))
    stacked = jnp.concatenate(blocks, axis=0)
    high = stacked.astype(jnp.bfloat16)
    low = (stacked - high.astype(jnp.float32)).astype(jnp.bfloat16)
    both = jnp.dot(
        jnp.concatenate([high, low], axis=0), table_ref[...], preferred_element_type=jnp.float32
    )
    count = stacked.shape[0]
    out = both[:count] + both[count:]
    width = out.shape[1] // 2
    re = [out[q * rows : (q + 1) * rows, :width] for q in range(RADIX // 2)]
    im = [out[q * rows : (q + 1) * rows, width:] for q in range(RADIX // 2)]
    return re, im


def scales(re, im, radius, mask):
    amp = [jnp.sqrt(a * a + b * b) for a, b in zip(re, im)]
    rows, width = amp[0].shape
    per = width // 2
    reach = radius // RADIX
    lane = lax.broadcasted_iota(jnp.int32, (rows, width), 1)
    place = lane % per
    upper = lane >= per
    swapped = [pltpu.roll(a, per, 1) for a in amp]
    pair = [a + b for a, b in zip(amp, swapped)]
    total = pair[0]
    for value in pair[1:]:
        total = total + value

    def shifted(value, by):
        moved = pltpu.roll(value, (-by) % width, 1)
        inside = (place + by >= 0) & (place + by < per)
        return jnp.where(inside, moved, 0.0)

    centre = total
    for by in range(1, reach):
        centre = centre + shifted(total, by) + shifted(total, -by)
    before = jnp.zeros_like(total)
    out = []
    for a, b, both in zip(amp, swapped, pair):
        upto = before + a + jnp.where(upper, b, 0.0)
        before_here = before + jnp.where(upper, b, 0.0)
        onward = total - before_here
        before = before + both
        out.append((upto, onward))
    result = []
    for upto, onward in out:
        summed = centre + shifted(upto, reach) + shifted(onward, -reach)
        result.append(mask / (summed * (1.0 / (2 * radius + 1)) + 1e-06))
    return result


def whiten_rows(samples, radius, mask, twiddle_ref, table_ref, relay_ref, out_ref):
    rows = samples.shape[0]
    blocks = RADIX // 2
    re, im = spectrum(samples, twiddle_ref, table_ref)
    scale = scales(re, im, radius, mask)
    for part, values in enumerate((re, im)):
        for q in range(blocks):
            relay_ref[pl.ds(part * rows * blocks + q, rows, stride=blocks), :] = (
                values[q] * scale[q]
            )
    out_ref[...] = relay_ref[...].astype(jnp.bfloat16)


def turn(index):
    return TURN_GATHER[min(index, len(TURN_GATHER) - 1)]


def panel_order(bits):
    held = [(0, 0)]
    for index, bit in enumerate(bits[:-1]):
        first = len(held)
        held = held + [(k ^ bit, odd ^ turn(index)) for k, odd in held]
    last = [(k ^ bits[-1], odd ^ turn(len(bits) - 1)) for k, odd in held]
    order = []
    for pieces in (held, last[:first], last[first:]):
        order += pieces + [(k, 1 - odd) for k, odd in pieces]
    return order


def flags_of(picks, flags):
    return lax.dot_general(
        picks.astype(jnp.bfloat16),
        flags,
        (((1,), (1,)), ((), ())),
        preferred_element_type=jnp.float32,
    )


def at_window(rows_flags):
    row = lax.broadcasted_iota(jnp.int32, rows_flags.shape, 0)
    column = lax.broadcasted_iota(jnp.int32, rows_flags.shape, 1)
    kept = jnp.where(row % rows_flags.shape[1] == column, rows_flags, 0.0)
    return jnp.sum(kept, axis=1, keepdims=True)


def choice_kernel(halves, channels, ids_ref, usable_ref, after_ref, *outs):
    del after_ref
    choice_ref, mask_ref, take_ref, info_ref = outs
    windows, total = usable_ref.shape
    members = lax.axis_size("dev")
    group, member = lax.axis_index("grp"), lax.axis_index("dev")
    core, plane = group % SRC_DEV, group // SRC_DEV
    flags = usable_ref[...].astype(jnp.float32).astype(jnp.bfloat16)

    def panel(step, shape):
        chosen = jnp.broadcast_to(ids_ref[:, step : step + 1], shape)
        return lax.div(chosen, halves), lax.rem(chosen, halves)

    row = lax.broadcasted_iota(jnp.int32, choice_ref.shape, 0)
    choice = jnp.zeros(choice_ref.shape, jnp.float32)
    for t in range(STEPS):
        owning, within = panel(t, choice_ref.shape)
        apart = lax.rem(owning + core, SRC_DEV)
        choice = jnp.where(row == (t * SRC_DEV + apart) * halves + within, 1.0, choice)
    choice_ref[...] = choice

    row = lax.broadcasted_iota(jnp.int32, info_ref.shape, 0)
    info = jnp.zeros(info_ref.shape, jnp.int32)
    for t in range(STEPS):
        owning, within = panel(t, info_ref.shape)
        info = jnp.where(row == t, owning * (members * channels) + within * SRC_DEV, info)
    info_ref[...] = info

    shape = (STEPS * windows, total)
    row = lax.broadcasted_iota(jnp.int32, shape, 0)
    lane = lax.broadcasted_iota(jnp.int32, shape, 1)
    picks = jnp.zeros(shape, jnp.float32)
    for t in range(STEPS):
        owning, within = panel(t, shape)
        channel = (owning * members + member) * channels + within * SRC_DEV + core
        picks = jnp.where((row // windows == t) & (lane == channel), 1.0, picks)
    mask_ref[...] = jnp.broadcast_to(at_window(flags_of(picks, flags)), mask_ref.shape)

    shape = take_ref.shape[1:]
    row = lax.broadcasted_iota(jnp.int32, shape, 0)
    for index in range(take_ref.shape[0]):
        take = jnp.zeros(shape, jnp.float32)
        for t in range(STEPS):
            owning, _ = panel(t, shape)
            differs = (lax.div(owning, SRC_DEV) ^ plane) & (1 << index)
            take = jnp.where((row // windows == t) & (differs != 0), 1.0, take)
        take_ref[index] = take


def pick_kernel(flip, choice_ref, own_ref, other_ref, after_ref, out_ref, samples):
    del after_ref
    channels, windows, length = own_ref.shape
    halves = channels // SRC_DEV
    half = (lax.axis_index("grp") + flip) % SRC_DEV
    points = length // RADIX
    for step in range(STEPS):
        held = [jnp.zeros((windows, points), jnp.float32)] * RADIX
        for k, raw_ref in enumerate((own_ref, other_ref)):
            for h in range(halves):
                index = (step * SRC_DEV + k) * halves + h
                here = jnp.broadcast_to(choice_ref[index : index + 1, :], (windows, points)) > 0.0
                row = raw_ref[h * SRC_DEV + half].astype(jnp.float32)
                for n in range(RADIX):
                    held[n] = jnp.where(here, row[:, n * points : (n + 1) * points], held[n])
        for n in range(RADIX):
            samples[step * windows : (step + 1) * windows, n * points : (n + 1) * points] = held[n]
    out_ref[...] = samples[...].astype(out_ref.dtype)


def receiver_kernel(radius, order, last_bit, info_ref, usable_ref, raw_ref, twiddle_ref, table_ref, *rest):
    spectra_ref, inverse_ref, other_ref, samples, relay = rest
    channels, windows, _ = raw_ref.shape
    members = lax.axis_size("dev")
    group, member = lax.axis_index("grp"), lax.axis_index("dev")
    core = group % SRC_DEV
    first = (group * members + member) * channels
    flags = usable_ref[...].astype(jnp.float32).astype(jnp.bfloat16)
    total = flags.shape[1]

    for r in range(channels):
        samples[r * windows : (r + 1) * windows, :] = raw_ref[r].astype(jnp.float32)
    rows = channels * windows
    row = lax.broadcasted_iota(jnp.int32, (rows, total), 0)
    lane = lax.broadcasted_iota(jnp.int32, (rows, total), 1)
    own = jnp.where(lane == first + row // windows, 1.0, 0.0)
    mask = at_window(flags_of(own, flags))
    whiten_rows(samples[...], radius, mask, twiddle_ref, table_ref, relay, spectra_ref)

    rows = STEPS * channels
    row = lax.broadcasted_iota(jnp.int32, (rows, total), 0)
    lane = lax.broadcasted_iota(jnp.int32, (rows, total), 1)
    start = jnp.zeros((rows, total), jnp.int32)
    for t in range(STEPS):
        here = jnp.broadcast_to(info_ref[t : t + 1, :1], (rows, total))
        start = jnp.where(row // channels == t, here, start)
    blocks = []
    for k, odd in order:
        offset = (member ^ k) * channels + (core + odd) % SRC_DEV
        blocks.append(jnp.where(lane == start + offset, 1.0, 0.0))
    sent = flags_of(jnp.concatenate(blocks, axis=0), flags)
    theirs = ((group ^ TURN_LAST) * members + (member ^ last_bit)) * channels
    for ref, start in ((inverse_ref, first), (other_ref, theirs)):
        received = flags_of(jnp.where(lane == start + row % channels, 1.0, 0.0), flags)
        both = sent * jnp.concatenate([received] * len(order), axis=0)
        counts = jnp.sum(both, axis=1, keepdims=True)
        ref[...] = jnp.broadcast_to(1.0 / jnp.maximum(counts, 1.0), ref.shape)


def source_kernel(radius, *refs):
    take_ref, mask_ref, kept_ref, came_ref, twiddle_ref, table_ref = refs[:6]
    out_ref, relay = refs[-2:]
    rows, length = kept_ref.shape
    points = length // RADIX
    here = take_ref[...] > 0.0
    kept, came = kept_ref[...].astype(jnp.float32), came_ref[...].astype(jnp.float32)
    here = jnp.concatenate([here] * RADIX, axis=1)
    samples = jnp.where(here, came, kept)
    whiten_rows(samples, radius, mask_ref[:, :1], twiddle_ref, table_ref, relay, out_ref)


def lagged_rows(windows, pieces, sets, table_ref, products, stacked):
    blocks = RADIX // 2

    def row_set(ref, base, first, rows):
        out = []
        for part in range(2):
            held = []
            for w in range(0, windows, 2):
                start = base + (part * rows + first + w) * blocks
                both = ref[start : start + 2 * blocks, :].astype(jnp.float32)
                held += [both[:blocks], both[blocks:]]
            out.append(held)
        return out

    pair = 0
    for recv_ref, _ in sets:
        receivers = recv_ref.shape[0] // (2 * windows * blocks)
        own = [row_set(recv_ref, 0, r * windows, receivers * windows) for r in range(receivers)]
        for ref, base in pieces:
            for step in range(STEPS):
                a, b = row_set(ref, base, step * windows, STEPS * windows)
                for r in range(receivers):
                    c, e = own[r]
                    re = im = None
                    for w in range(windows):
                        re_w = a[w] * c[w] + b[w] * e[w]
                        im_w = b[w] * c[w] - a[w] * e[w]
                        re = re_w if re is None else re + re_w
                        im = im_w if im is None else im + im_w
                    products[0, pair * blocks : (pair + 1) * blocks, :] = re
                    products[1, pair * blocks : (pair + 1) * blocks, :] = im
                    pair += 1
    width = products.shape[2]
    inverse = jnp.concatenate([factors for _, factors in sets], axis=0)
    for part in range(2):
        for q in range(blocks):
            column = (part * blocks + q) * width
            values = products[part, pl.ds(q, pair, stride=blocks), :] * inverse
            stacked[:, column : column + width] = values.astype(jnp.bfloat16)
    return jnp.dot(stacked[...], table_ref[...], preferred_element_type=jnp.float32)


def pieces_of(ref, windows):
    rows = 2 * STEPS * windows * (RADIX // 2)
    return [(ref, base) for base in range(0, ref.shape[0], rows)]


def part_kernel(windows, first, n_sets, *refs):
    table_ref, set_refs, refs = refs[0], refs[1 : 1 + 2 * n_sets], refs[1 + 2 * n_sets :]
    products, stacked = refs[-2:]
    buffers, outs = refs[: -2 - n_sets], refs[-2 - n_sets : -2]
    pieces = [piece for ref in buffers for piece in pieces_of(ref, windows)]
    rows = outs[0].shape[0]
    sets = [
        (set_refs[2 * i], set_refs[2 * i + 1][first : first + rows, :]) for i in range(n_sets)
    ]
    lagged = lagged_rows(windows, pieces, sets, table_ref, products, stacked)
    for i, out_ref in enumerate(outs):
        out_ref[...] = lagged[i * rows : (i + 1) * rows].astype(jnp.bfloat16)


def pass_kernel(value_ref, after_ref, out_ref):
    del after_ref
    out_ref[...] = value_ref[...]


def place_kernel(order, last_bit, *refs):
    out_ref = refs[-1]
    member = lax.axis_index("dev")
    core = lax.axis_index("grp") % SRC_DEV
    receivers = out_ref.shape[2]
    whole = order + [(k ^ last_bit, odd ^ TURN_LAST) for k, odd in order]
    block = STEPS * receivers
    done = 0
    for ref in refs[:-1]:
        for p in range(ref.shape[0] // block):
            k, odd = whole[done]
            source = (member ^ k) * SRC_DEV + (core + odd) % SRC_DEV
            for step in range(STEPS):
                row = p * block + step * receivers
                out_ref[step, source] = ref[row : row + receivers, :]
            done += 1


def on_device(records, usable, panel_ids):
    channels, windows, length = records.shape
    bin_count = length // 2
    radius = bin_count // 16
    halves = channels // SRC_DEV
    groups = lax.axis_size("grp")
    members = lax.axis_size("dev")
    blocks = RADIX // 2
    width = bin_count // blocks

    def exchange(value, group_bit, member_bit):
        flip = group_bit * members + member_bit
        pairs = [(i, i ^ flip) for i in range(groups * members)]
        return lax.ppermute(value, AXES, pairs)

    ltable = jnp.asarray(lag_table(length, bin_count, NLAG))
    all_bits = [1 << i for i in range(members.bit_length() - 1)]
    chosen = [all_bits[i] for i in BIT_ORDER]
    *gather_bits, last_bit = [b for b in all_bits[::-1] if b not in chosen] + chosen
    order = panel_order(gather_bits)

    usable_rows = usable.T
    planes = groups // SRC_DEV
    source_rows = STEPS * windows
    plane_bits = planes.bit_length() - 1

    records_other = exchange(records, 1, 0)
    points = length // RADIX
    table, twiddle = pl.pallas_call(
        functools.partial(tables_kernel, length),
        out_shape=[
            jax.ShapeDtypeStruct((4 * points, 2 * points), jnp.bfloat16),
            jax.ShapeDtypeStruct((2, RADIX, points), jnp.float32),
        ],
        in_specs=[],
        out_specs=[VMEM] * 2,
        compiler_params=PARAMS,
        cost_estimate=AHEAD,
        name="short_tables",
    )()

    choice, mask, take, info = pl.pallas_call(
        functools.partial(choice_kernel, halves, channels),
        out_shape=[
            jax.ShapeDtypeStruct((STEPS * SRC_DEV * halves, width), jnp.float32),
            jax.ShapeDtypeStruct((source_rows, width), jnp.float32),
            jax.ShapeDtypeStruct((plane_bits, source_rows, width), jnp.float32),
            jax.ShapeDtypeStruct((8, width), jnp.int32),
        ],
        in_specs=[VMEM] * 3,
        out_specs=[VMEM] * 4,
        compiler_params=PARAMS,
        name="choose_rows",
    )(panel_ids[None, :], usable_rows, twiddle)

    row_count = channels * windows
    pairs = len(order) * STEPS * channels
    receivers, inverse, inverse_theirs = pl.pallas_call(
        functools.partial(receiver_kernel, radius, order, last_bit),
        out_shape=[
            jax.ShapeDtypeStruct((2 * row_count * blocks, width), jnp.bfloat16),
            jax.ShapeDtypeStruct((pairs, width), jnp.float32),
            jax.ShapeDtypeStruct((pairs, width), jnp.float32),
        ],
        in_specs=[VMEM] * 5,
        out_specs=[VMEM] * 3,
        scratch_shapes=[
            pltpu.VMEM((row_count, length), jnp.float32),
            pltpu.VMEM((2 * row_count * blocks, width), jnp.float32),
        ],
        compiler_params=PARAMS,
        cost_estimate=AHEAD,
        name="receiver_spectra",
    )(info, usable_rows, records, twiddle, table)

    def pick(flip):
        return pl.pallas_call(
            functools.partial(pick_kernel, flip),
            out_shape=jax.ShapeDtypeStruct((source_rows, length), records.dtype),
            in_specs=[VMEM] * 4,
            out_specs=VMEM,
            scratch_shapes=[pltpu.VMEM((source_rows, length), jnp.float32)],
            compiler_params=PARAMS,
            name="pick_rows",
        )(choice, records, records_other, inverse)

    sent = pick(TURN_PLANE)
    came = exchange(sent, SRC_DEV * (planes // 2) + TURN_PLANE, 0)
    kept = pick(0) if TURN_PLANE else sent
    for index in range(plane_bits - 2, -1, -1):
        kept = jnp.where(take[index + 1][:, :1] > 0.0, came, kept)
        came = exchange(kept, SRC_DEV << index, 0)

    piece = pl.pallas_call(
        functools.partial(source_kernel, radius),
        out_shape=jax.ShapeDtypeStruct((2 * source_rows * blocks, width), jnp.bfloat16),
        in_specs=[VMEM] * 7,
        out_specs=VMEM,
        scratch_shapes=[pltpu.VMEM((2 * source_rows * blocks, width), jnp.float32)],
        compiler_params=PARAMS,
        name="source_spectra",
    )(take[0], mask, kept, came, twiddle, table, receivers)

    def part(first, sets, *buffers, cost=BESIDE):
        rows = sum(b.shape[0] for b in buffers) // (2 * windows * blocks) * channels
        total = rows * len(sets)
        return pl.pallas_call(
            functools.partial(part_kernel, windows, first, len(sets)),
            out_shape=[jax.ShapeDtypeStruct((rows, NLAG), jnp.bfloat16)] * len(sets),
            in_specs=[VMEM] * (1 + 2 * len(sets) + len(buffers)),
            out_specs=[VMEM] * len(sets),
            scratch_shapes=[
                pltpu.VMEM((2, total * blocks, width), jnp.float32),
                pltpu.VMEM((total, 2 * bin_count), jnp.bfloat16),
            ],
            compiler_params=PARAMS,
            cost_estimate=cost,
            name="correlate_part",
        )(ltable, *[array for pair in sets for array in pair], *buffers)

    def pass_on(value, after):
        return pl.pallas_call(
            pass_kernel,
            out_shape=jax.ShapeDtypeStruct(value.shape, value.dtype),
            in_specs=[VMEM] * 2,
            out_specs=VMEM,
            compiler_params=PARAMS,
            name="pass_on",
        )(value, after)

    held = piece
    for index, bit in enumerate(gather_bits[:-2]):
        held = jnp.concatenate([held, exchange(held, turn(index), bit)], axis=0)
    rounds = len(gather_bits)
    theirs = exchange(receivers, TURN_LAST, last_bit)
    fresh = pass_on(exchange(held, turn(rounds - 2), gather_bits[-2]), theirs)
    first = exchange(held, turn(rounds - 1), gather_bits[-1])
    second = exchange(fresh, turn(rounds - 1), gather_bits[-1])
    held = jnp.concatenate([held, fresh], axis=0)
    pieces = [held, exchange(held, 1, 0), first, exchange(first, 1, 0)]
    pieces += [second, exchange(second, 1, 0)]
    mine, other = (receivers, inverse), (theirs, inverse_theirs)
    early_theirs, early = part(0, [other, mine], held)
    (next_theirs,) = part(pairs // 4, [other], *pieces[1:4])
    (late_theirs,) = part(pairs // 4 * 3, [other], *pieces[4:])
    (late,) = part(pairs // 4, [mine], *pieces[1:])
    back = exchange(jnp.concatenate([early_theirs, next_theirs, late_theirs], axis=0), TURN_LAST, last_bit)
    return pl.pallas_call(
        functools.partial(place_kernel, order, last_bit),
        out_shape=jax.ShapeDtypeStruct(
            (STEPS, members * SRC_DEV, channels, NLAG), jnp.bfloat16
        ),
        in_specs=[VMEM] * 3,
        out_specs=VMEM,
        compiler_params=PARAMS,
        name="place_rows",
    )(early, late, back)


def solution(mesh):
    placed = (P(AXES, None, None), P(), P())
    return jax.shard_map(
        on_device,
        mesh=mesh,
        in_specs=placed,
        out_specs=P(None, None, AXES, None),
        check_vma=False,
    )
```

```python
import functools
import math

import jax
import jax.numpy as jnp
import ml_dtypes
import numpy as np
from jax import lax
from jax.experimental import pallas as pl
from jax.experimental.pallas import tpu as pltpu
from jax.sharding import PartitionSpec as P

NLAG = 512
SRC_DEV = 2
STEPS = 2
RADIX = 16
AXES = ("grp", "dev")
TURN_PLANE, TURN_GATHER, TURN_LAST = 1, (1, 1), 1
BIT_ORDER = (2, 0, 1)
VMEM = pl.BlockSpec(memory_space=pltpu.VMEM)
AHEAD = pl.CostEstimate(flops=5_000_000_000, bytes_accessed=1_000_000, transcendentals=0)
BESIDE = pl.CostEstimate(flops=1_000_000_000, bytes_accessed=1_000_000, transcendentals=0)
PARAMS = pltpu.CompilerParams(vmem_limit_bytes=16 * 1024 * 1024)


def bin_order(bin_count):
    per = bin_count // RADIX
    order = []
    for q in range(RADIX // 2):
        for h in range(2):
            order.append(RADIX * np.arange(per) + 2 * q + h + 1)
    return np.concatenate(order)


def turned_cos_sin(index, count):
    angle = (index - count // 2).astype(jnp.float32) * (2.0 * math.pi / count)
    square = angle * angle
    cosine = sine = jnp.zeros_like(angle)
    for n in range(8, -1, -1):
        cosine = cosine * square + (-1) ** n / math.factorial(2 * n)
        sine = sine * square + (-1) ** n / math.factorial(2 * n + 1)
    return -cosine, -sine * angle


def tables_kernel(length, table_ref, twiddle_ref):
    points = length // RADIX
    per = points // 2
    row = lax.broadcasted_iota(jnp.int32, (points, points), 0)
    lane = lax.broadcasted_iota(jnp.int32, (points, points), 1)
    cosine, sine = turned_cos_sin(row * (lane % per) % points, points)
    for h in range(2):
        inside = (lane >= per) if h else (lane < per)
        c, s = jnp.where(inside, cosine, 0.0), jnp.where(inside, sine, 0.0)
        for part, values in enumerate(((c, -s), (s, c))):
            rows = slice((2 * h + part) * points, (2 * h + part + 1) * points)
            whole = jnp.concatenate(values, axis=1)
            table_ref[rows, :] = whole.astype(jnp.bfloat16)
    residue = lax.broadcasted_iota(jnp.int32, (RADIX, points), 0) + 1
    sample = lax.broadcasted_iota(jnp.int32, (RADIX, points), 1)
    cosine, sine = turned_cos_sin(residue * sample % length, length)
    twiddle_ref[0] = cosine
    twiddle_ref[1] = -sine


def lag_table(length, bin_count, lag_count):
    bins = bin_order(bin_count)[:, None]
    lags = np.arange(lag_count)[None, :] - lag_count // 2
    phases = 2.0 * np.pi / length * (bins * lags % length)
    factor = 1.0 / math.sqrt(bin_count)
    cosine, sine = np.cos(phases) * factor, -np.sin(phases) * factor
    return np.concatenate([cosine, sine], axis=0).astype(ml_dtypes.bfloat16)


def real_dft(values):
    n = len(values)
    if n == 1:
        return [(values[0], None)]
    if n == 2:
        return [(values[0] + values[1], None), (values[0] - values[1], None)]
    even, odd = real_dft(values[0::2]), real_dft(values[1::2])
    quarter = n // 4
    out = [None] * (n // 2 + 1)
    for r in range(quarter + 1):
        (er, ei), (orr, oi) = even[r], odd[r]
        cosine, sine = math.cos(2 * math.pi * r / n), math.sin(2 * math.pi * r / n)
        if r == 0:
            tr, ti = orr, None
        elif r == quarter:
            tr, ti = None, -orr
        elif 8 * r == n:
            tr, ti = (orr + oi) * cosine, (oi - orr) * cosine
        else:
            tr, ti = orr * cosine + oi * sine, oi * cosine - orr * sine
        plus_re = er if tr is None else er + tr
        minus_re = er if tr is None else er - tr
        if ei is None:
            plus_im, minus_im = ti, ti
        elif ti is None:
            plus_im, minus_im = ei, -ei
        else:
            plus_im, minus_im = ei + ti, ti - ei
        out[r] = (plus_re, plus_im)
        if r < quarter:
            out[n // 2 - r] = (minus_re, minus_im)
    return out


def spectrum(samples, twiddle_ref, table_ref):
    rows, length = samples.shape
    points = length // RADIX
    half = real_dft([samples[:, i * points : (i + 1) * points] for i in range(RADIX)])
    lanes = []
    for residue in range(1, RADIX + 1):
        folded = min(residue, RADIX - residue)
        re, im = half[folded]
        if residue > RADIX // 2 and im is not None:
            im = -im
        cosine = twiddle_ref[0, residue - 1 : residue, :]
        sine = twiddle_ref[1, residue - 1 : residue, :]
        if im is None:
            lanes.append((re * cosine, re * sine))
        else:
            lanes.append((re * cosine - im * sine, re * sine + im * cosine))
    blocks = []
    for q in range(RADIX // 2):
        (ar, ai), (br, bi) = lanes[2 * q], lanes[2 * q + 1]
        blocks.append(jnp.concatenate([ar, ai, br, bi], axis=1))
    stacked = jnp.concatenate(blocks, axis=0)
    high = stacked.astype(jnp.bfloat16)
    low = (stacked - high.astype(jnp.float32)).astype(jnp.bfloat16)
    both = jnp.dot(
        jnp.concatenate([high, low], axis=0), table_ref[...], preferred_element_type=jnp.float32
    )
    count = stacked.shape[0]
    out = both[:count] + both[count:]
    width = out.shape[1] // 2
    re = [out[q * rows : (q + 1) * rows, :width] for q in range(RADIX // 2)]
    im = [out[q * rows : (q + 1) * rows, width:] for q in range(RADIX // 2)]
    return re, im


def scales(re, im, radius, mask):
    amp = [jnp.sqrt(a * a + b * b) for a, b in zip(re, im)]
    rows, width = amp[0].shape
    per = width // 2
    reach = radius // RADIX
    lane = lax.broadcasted_iota(jnp.int32, (rows, width), 1)
    place = lane % per
    upper = lane >= per
    swapped = [pltpu.roll(a, per, 1) for a in amp]
    pair = [a + b for a, b in zip(amp, swapped)]
    total = pair[0]
    for value in pair[1:]:
        total = total + value

    def shifted(value, by):
        moved = pltpu.roll(value, (-by) % width, 1)
        inside = (place + by >= 0) & (place + by < per)
        return jnp.where(inside, moved, 0.0)

    centre = total
    for by in range(1, reach):
        centre = centre + shifted(total, by) + shifted(total, -by)
    before = jnp.zeros_like(total)
    out = []
    for a, b, both in zip(amp, swapped, pair):
        upto = before + a + jnp.where(upper, b, 0.0)
        before_here = before + jnp.where(upper, b, 0.0)
        onward = total - before_here
        before = before + both
        out.append((upto, onward))
    result = []
    for upto, onward in out:
        summed = centre + shifted(upto, reach) + shifted(onward, -reach)
        result.append(mask / (summed * (1.0 / (2 * radius + 1)) + 1e-06))
    return result


def whiten_rows(samples, radius, mask, twiddle_ref, table_ref, relay_ref, out_ref):
    rows = samples.shape[0]
    blocks = RADIX // 2
    re, im = spectrum(samples, twiddle_ref, table_ref)
    scale = scales(re, im, radius, mask)
    for part, values in enumerate((re, im)):
        for q in range(blocks):
            relay_ref[pl.ds(part * rows * blocks + q, rows, stride=blocks), :] = (
                values[q] * scale[q]
            )
    out_ref[...] = relay_ref[...].astype(jnp.bfloat16)


def turn(index):
    return TURN_GATHER[min(index, len(TURN_GATHER) - 1)]


def panel_order(bits):
    held = [(0, 0)]
    for index, bit in enumerate(bits[:-1]):
        first = len(held)
        held = held + [(k ^ bit, odd ^ turn(index)) for k, odd in held]
    last = [(k ^ bits[-1], odd ^ turn(len(bits) - 1)) for k, odd in held]
    order = []
    for pieces in (held, last[:first], last[first:]):
        order += pieces + [(k, 1 - odd) for k, odd in pieces]
    return order


def flags_of(picks, flags):
    return lax.dot_general(
        picks.astype(jnp.bfloat16),
        flags,
        (((1,), (1,)), ((), ())),
        preferred_element_type=jnp.float32,
    )


def at_window(rows_flags):
    row = lax.broadcasted_iota(jnp.int32, rows_flags.shape, 0)
    column = lax.broadcasted_iota(jnp.int32, rows_flags.shape, 1)
    kept = jnp.where(row % rows_flags.shape[1] == column, rows_flags, 0.0)
    return jnp.sum(kept, axis=1, keepdims=True)


def choice_kernel(halves, channels, ids_ref, usable_ref, after_ref, *outs):
    del after_ref
    choice_ref, mask_ref, take_ref, info_ref = outs
    windows, total = usable_ref.shape
    members = lax.axis_size("dev")
    group, member = lax.axis_index("grp"), lax.axis_index("dev")
    core, plane = group % SRC_DEV, group // SRC_DEV
    flags = usable_ref[...].astype(jnp.float32).astype(jnp.bfloat16)

    def panel(step, shape):
        chosen = jnp.broadcast_to(ids_ref[:, step : step + 1], shape)
        return lax.div(chosen, halves), lax.rem(chosen, halves)

    row = lax.broadcasted_iota(jnp.int32, choice_ref.shape, 0)
    choice = jnp.zeros(choice_ref.shape, jnp.float32)
    for t in range(STEPS):
        owning, within = panel(t, choice_ref.shape)
        apart = lax.rem(owning + core, SRC_DEV)
        choice = jnp.where(row == (t * SRC_DEV + apart) * halves + within, 1.0, choice)
    choice_ref[...] = choice

    row = lax.broadcasted_iota(jnp.int32, info_ref.shape, 0)
    info = jnp.zeros(info_ref.shape, jnp.int32)
    for t in range(STEPS):
        owning, within = panel(t, info_ref.shape)
        info = jnp.where(row == t, owning * (members * channels) + within * SRC_DEV, info)
    info_ref[...] = info

    shape = (STEPS * windows, total)
    row = lax.broadcasted_iota(jnp.int32, shape, 0)
    lane = lax.broadcasted_iota(jnp.int32, shape, 1)
    picks = jnp.zeros(shape, jnp.float32)
    for t in range(STEPS):
        owning, within = panel(t, shape)
        channel = (owning * members + member) * channels + within * SRC_DEV + core
        picks = jnp.where((row // windows == t) & (lane == channel), 1.0, picks)
    mask_ref[...] = jnp.broadcast_to(at_window(flags_of(picks, flags)), mask_ref.shape)

    shape = take_ref.shape[1:]
    row = lax.broadcasted_iota(jnp.int32, shape, 0)
    for index in range(take_ref.shape[0]):
        take = jnp.zeros(shape, jnp.float32)
        for t in range(STEPS):
            owning, _ = panel(t, shape)
            differs = (lax.div(owning, SRC_DEV) ^ plane) & (1 << index)
            take = jnp.where((row // windows == t) & (differs != 0), 1.0, take)
        take_ref[index] = take


def pick_kernel(flip, choice_ref, own_ref, other_ref, after_ref, out_ref, samples):
    del after_ref
    channels, windows, length = own_ref.shape
    halves = channels // SRC_DEV
    half = (lax.axis_index("grp") + flip) % SRC_DEV
    points = length // RADIX
    for step in range(STEPS):
        held = [jnp.zeros((windows, points), jnp.float32)] * RADIX
        for k, raw_ref in enumerate((own_ref, other_ref)):
            for h in range(halves):
                index = (step * SRC_DEV + k) * halves + h
                here = jnp.broadcast_to(choice_ref[index : index + 1, :], (windows, points)) > 0.0
                row = raw_ref[h * SRC_DEV + half].astype(jnp.float32)
                for n in range(RADIX):
                    held[n] = jnp.where(here, row[:, n * points : (n + 1) * points], held[n])
        for n in range(RADIX):
            samples[step * windows : (step + 1) * windows, n * points : (n + 1) * points] = held[n]
    out_ref[...] = samples[...].astype(out_ref.dtype)


def receiver_kernel(radius, order, last_bit, info_ref, usable_ref, raw_ref, twiddle_ref, table_ref, *rest):
    spectra_ref, inverse_ref, other_ref, samples, relay = rest
    channels, windows, _ = raw_ref.shape
    members = lax.axis_size("dev")
    group, member = lax.axis_index("grp"), lax.axis_index("dev")
    core = group % SRC_DEV
    first = (group * members + member) * channels
    flags = usable_ref[...].astype(jnp.float32).astype(jnp.bfloat16)
    total = flags.shape[1]

    for r in range(channels):
        samples[r * windows : (r + 1) * windows, :] = raw_ref[r].astype(jnp.float32)
    rows = channels * windows
    row = lax.broadcasted_iota(jnp.int32, (rows, total), 0)
    lane = lax.broadcasted_iota(jnp.int32, (rows, total), 1)
    own = jnp.where(lane == first + row // windows, 1.0, 0.0)
    mask = at_window(flags_of(own, flags))
    whiten_rows(samples[...], radius, mask, twiddle_ref, table_ref, relay, spectra_ref)

    rows = STEPS * channels
    row = lax.broadcasted_iota(jnp.int32, (rows, total), 0)
    lane = lax.broadcasted_iota(jnp.int32, (rows, total), 1)
    start = jnp.zeros((rows, total), jnp.int32)
    for t in range(STEPS):
        here = jnp.broadcast_to(info_ref[t : t + 1, :1], (rows, total))
        start = jnp.where(row // channels == t, here, start)
    blocks = []
    for k, odd in order:
        offset = (member ^ k) * channels + (core + odd) % SRC_DEV
        blocks.append(jnp.where(lane == start + offset, 1.0, 0.0))
    sent = flags_of(jnp.concatenate(blocks, axis=0), flags)
    theirs = ((group ^ TURN_LAST) * members + (member ^ last_bit)) * channels
    for ref, start in ((inverse_ref, first), (other_ref, theirs)):
        received = flags_of(jnp.where(lane == start + row % channels, 1.0, 0.0), flags)
        both = sent * jnp.concatenate([received] * len(order), axis=0)
        counts = jnp.sum(both, axis=1, keepdims=True)
        ref[...] = jnp.broadcast_to(1.0 / jnp.maximum(counts, 1.0), ref.shape)


def source_kernel(radius, *refs):
    take_ref, mask_ref, kept_ref, came_ref, twiddle_ref, table_ref = refs[:6]
    out_ref, relay = refs[-2:]
    rows, length = kept_ref.shape
    points = length // RADIX
    here = take_ref[...] > 0.0
    kept, came = kept_ref[...].astype(jnp.float32), came_ref[...].astype(jnp.float32)
    here = jnp.concatenate([here] * RADIX, axis=1)
    samples = jnp.where(here, came, kept)
    whiten_rows(samples, radius, mask_ref[:, :1], twiddle_ref, table_ref, relay, out_ref)


def lagged_rows(windows, pieces, sets, table_ref, products, stacked):
    blocks = RADIX // 2

    def row_set(ref, base, first, rows):
        out = []
        for part in range(2):
            held = []
            for w in range(0, windows, 2):
                start = base + (part * rows + first + w) * blocks
                both = ref[start : start + 2 * blocks, :].astype(jnp.float32)
                held += [both[:blocks], both[blocks:]]
            out.append(held)
        return out

    pair = 0
    for recv_ref, _ in sets:
        receivers = recv_ref.shape[0] // (2 * windows * blocks)
        own = [row_set(recv_ref, 0, r * windows, receivers * windows) for r in range(receivers)]
        for ref, base in pieces:
            for step in range(STEPS):
                a, b = row_set(ref, base, step * windows, STEPS * windows)
                for r in range(receivers):
                    c, e = own[r]
                    re = im = None
                    for w in range(windows):
                        re_w = a[w] * c[w] + b[w] * e[w]
                        im_w = b[w] * c[w] - a[w] * e[w]
                        re = re_w if re is None else re + re_w
                        im = im_w if im is None else im + im_w
                    products[0, pair * blocks : (pair + 1) * blocks, :] = re
                    products[1, pair * blocks : (pair + 1) * blocks, :] = im
                    pair += 1
    width = products.shape[2]
    inverse = jnp.concatenate([factors for _, factors in sets], axis=0)
    for part in range(2):
        for q in range(blocks):
            column = (part * blocks + q) * width
            values = products[part, pl.ds(q, pair, stride=blocks), :] * inverse
            stacked[:, column : column + width] = values.astype(jnp.bfloat16)
    return jnp.dot(stacked[...], table_ref[...], preferred_element_type=jnp.float32)


def pieces_of(ref, windows):
    rows = 2 * STEPS * windows * (RADIX // 2)
    return [(ref, base) for base in range(0, ref.shape[0], rows)]


def part_kernel(windows, first, n_sets, *refs):
    table_ref, set_refs, refs = refs[0], refs[1 : 1 + 2 * n_sets], refs[1 + 2 * n_sets :]
    products, stacked = refs[-2:]
    buffers, outs = refs[: -2 - n_sets], refs[-2 - n_sets : -2]
    pieces = [piece for ref in buffers for piece in pieces_of(ref, windows)]
    rows = outs[0].shape[0]
    sets = [
        (set_refs[2 * i], set_refs[2 * i + 1][first : first + rows, :]) for i in range(n_sets)
    ]
    lagged = lagged_rows(windows, pieces, sets, table_ref, products, stacked)
    for i, out_ref in enumerate(outs):
        out_ref[...] = lagged[i * rows : (i + 1) * rows].astype(jnp.bfloat16)


def pass_kernel(value_ref, after_ref, out_ref):
    del after_ref
    out_ref[...] = value_ref[...]


def place_kernel(order, last_bit, *refs):
    out_ref = refs[-1]
    member = lax.axis_index("dev")
    core = lax.axis_index("grp") % SRC_DEV
    receivers = out_ref.shape[2]
    whole = order + [(k ^ last_bit, odd ^ TURN_LAST) for k, odd in order]
    block = STEPS * receivers
    done = 0
    for ref in refs[:-1]:
        for p in range(ref.shape[0] // block):
            k, odd = whole[done]
            source = (member ^ k) * SRC_DEV + (core + odd) % SRC_DEV
            for step in range(STEPS):
                row = p * block + step * receivers
                out_ref[step, source] = ref[row : row + receivers, :]
            done += 1


def on_device(records, usable, panel_ids):
    channels, windows, length = records.shape
    bin_count = length // 2
    radius = bin_count // 16
    halves = channels // SRC_DEV
    groups = lax.axis_size("grp")
    members = lax.axis_size("dev")
    blocks = RADIX // 2
    width = bin_count // blocks

    def exchange(value, group_bit, member_bit):
        flip = group_bit * members + member_bit
        pairs = [(i, i ^ flip) for i in range(groups * members)]
        return lax.ppermute(value, AXES, pairs)

    ltable = jnp.asarray(lag_table(length, bin_count, NLAG))
    all_bits = [1 << i for i in range(members.bit_length() - 1)]
    chosen = [all_bits[i] for i in BIT_ORDER]
    *gather_bits, last_bit = [b for b in all_bits[::-1] if b not in chosen] + chosen
    order = panel_order(gather_bits)

    usable_rows = usable.T
    planes = groups // SRC_DEV
    source_rows = STEPS * windows
    plane_bits = planes.bit_length() - 1

    records_other = exchange(records, 1, 0)
    points = length // RADIX
    table, twiddle = pl.pallas_call(
        functools.partial(tables_kernel, length),
        out_shape=[
            jax.ShapeDtypeStruct((4 * points, 2 * points), jnp.bfloat16),
            jax.ShapeDtypeStruct((2, RADIX, points), jnp.float32),
        ],
        in_specs=[],
        out_specs=[VMEM] * 2,
        compiler_params=PARAMS,
        cost_estimate=AHEAD,
        name="short_tables",
    )()

    choice, mask, take, info = pl.pallas_call(
        functools.partial(choice_kernel, halves, channels),
        out_shape=[
            jax.ShapeDtypeStruct((STEPS * SRC_DEV * halves, width), jnp.float32),
            jax.ShapeDtypeStruct((source_rows, width), jnp.float32),
            jax.ShapeDtypeStruct((plane_bits, source_rows, width), jnp.float32),
            jax.ShapeDtypeStruct((8, width), jnp.int32),
        ],
        in_specs=[VMEM] * 3,
        out_specs=[VMEM] * 4,
        compiler_params=PARAMS,
        name="choose_rows",
    )(panel_ids[None, :], usable_rows, twiddle)

    row_count = channels * windows
    pairs = len(order) * STEPS * channels
    receivers, inverse, inverse_theirs = pl.pallas_call(
        functools.partial(receiver_kernel, radius, order, last_bit),
        out_shape=[
            jax.ShapeDtypeStruct((2 * row_count * blocks, width), jnp.bfloat16),
            jax.ShapeDtypeStruct((pairs, width), jnp.float32),
            jax.ShapeDtypeStruct((pairs, width), jnp.float32),
        ],
        in_specs=[VMEM] * 5,
        out_specs=[VMEM] * 3,
        scratch_shapes=[
            pltpu.VMEM((row_count, length), jnp.float32),
            pltpu.VMEM((2 * row_count * blocks, width), jnp.float32),
        ],
        compiler_params=PARAMS,
        cost_estimate=AHEAD,
        name="receiver_spectra",
    )(info, usable_rows, records, twiddle, table)

    def pick(flip):
        return pl.pallas_call(
            functools.partial(pick_kernel, flip),
            out_shape=jax.ShapeDtypeStruct((source_rows, length), records.dtype),
            in_specs=[VMEM] * 4,
            out_specs=VMEM,
            scratch_shapes=[pltpu.VMEM((source_rows, length), jnp.float32)],
            compiler_params=PARAMS,
            name="pick_rows",
        )(choice, records, records_other, inverse)

    sent = pick(TURN_PLANE)
    came = exchange(sent, SRC_DEV * (planes // 2) + TURN_PLANE, 0)
    kept = pick(0) if TURN_PLANE else sent
    for index in range(plane_bits - 2, -1, -1):
        kept = jnp.where(take[index + 1][:, :1] > 0.0, came, kept)
        came = exchange(kept, SRC_DEV << index, 0)

    piece = pl.pallas_call(
        functools.partial(source_kernel, radius),
        out_shape=jax.ShapeDtypeStruct((2 * source_rows * blocks, width), jnp.bfloat16),
        in_specs=[VMEM] * 7,
        out_specs=VMEM,
        scratch_shapes=[pltpu.VMEM((2 * source_rows * blocks, width), jnp.float32)],
        compiler_params=PARAMS,
        name="source_spectra",
    )(take[0], mask, kept, came, twiddle, table, receivers)

    def part(first, sets, *buffers, cost=BESIDE):
        rows = sum(b.shape[0] for b in buffers) // (2 * windows * blocks) * channels
        total = rows * len(sets)
        return pl.pallas_call(
            functools.partial(part_kernel, windows, first, len(sets)),
            out_shape=[jax.ShapeDtypeStruct((rows, NLAG), jnp.bfloat16)] * len(sets),
            in_specs=[VMEM] * (1 + 2 * len(sets) + len(buffers)),
            out_specs=[VMEM] * len(sets),
            scratch_shapes=[
                pltpu.VMEM((2, total * blocks, width), jnp.float32),
                pltpu.VMEM((total, 2 * bin_count), jnp.bfloat16),
            ],
            compiler_params=PARAMS,
            cost_estimate=cost,
            name="correlate_part",
        )(ltable, *[array for pair in sets for array in pair], *buffers)

    def pass_on(value, after):
        return pl.pallas_call(
            pass_kernel,
            out_shape=jax.ShapeDtypeStruct(value.shape, value.dtype),
            in_specs=[VMEM] * 2,
            out_specs=VMEM,
            compiler_params=PARAMS,
            name="pass_on",
        )(value, after)

    held = piece
    for index, bit in enumerate(gather_bits[:-2]):
        held = jnp.concatenate([held, exchange(held, turn(index), bit)], axis=0)
    rounds = len(gather_bits)
    theirs = exchange(receivers, TURN_LAST, last_bit)
    fresh = pass_on(exchange(held, turn(rounds - 2), gather_bits[-2]), theirs)
    first = exchange(held, turn(rounds - 1), gather_bits[-1])
    second = exchange(fresh, turn(rounds - 1), gather_bits[-1])
    held = jnp.concatenate([held, fresh], axis=0)
    pieces = [held, exchange(held, 1, 0), first, exchange(first, 1, 0)]
    pieces += [second, exchange(second, 1, 0)]
    mine, other = (receivers, inverse), (theirs, inverse_theirs)
    early_theirs, early = part(0, [other, mine], held)
    (next_theirs,) = part(pairs // 4, [other], *pieces[1:4])
    (late_theirs,) = part(pairs // 4 * 3, [other], *pieces[4:])
    (late,) = part(pairs // 4, [mine], *pieces[1:])
    back = exchange(jnp.concatenate([early_theirs, next_theirs, late_theirs], axis=0), TURN_LAST, last_bit)
    return pl.pallas_call(
        functools.partial(place_kernel, order, last_bit),
        out_shape=jax.ShapeDtypeStruct(
            (STEPS, members * SRC_DEV, channels, NLAG), jnp.bfloat16
        ),
        in_specs=[VMEM] * 3,
        out_specs=VMEM,
        compiler_params=PARAMS,
        name="place_rows",
    )(early, late, back)


def solution(mesh):
    placed = (P(AXES, None, None), P(), P())
    return jax.shard_map(
        on_device,
        mesh=mesh,
        in_specs=placed,
        out_specs=P(None, None, AXES, None),
        check_vma=False,
    )
```

```python
import functools
import math

import jax
import jax.numpy as jnp
import ml_dtypes
import numpy as np
from jax import lax
from jax.experimental import pallas as pl
from jax.experimental.pallas import tpu as pltpu
from jax.sharding import PartitionSpec as P

NLAG = 512
SRC_DEV = 2
STEPS = 2
RADIX = 16
AXES = ("grp", "dev")
TURN_PLANE, TURN_GATHER, TURN_LAST = 1, (1, 1), 1
BIT_ORDER = (2, 0, 1)
VMEM = pl.BlockSpec(memory_space=pltpu.VMEM)
AHEAD = pl.CostEstimate(flops=5_000_000_000, bytes_accessed=1_000_000, transcendentals=0)
BESIDE = pl.CostEstimate(flops=1_000_000_000, bytes_accessed=1_000_000, transcendentals=0)
PARAMS = pltpu.CompilerParams(vmem_limit_bytes=16 * 1024 * 1024)


def bin_order(bin_count):
    per = bin_count // RADIX
    order = []
    for q in range(RADIX // 2):
        for h in range(2):
            order.append(RADIX * np.arange(per) + 2 * q + h + 1)
    return np.concatenate(order)


def tables_kernel(length, table_ref, twiddle_ref):
    points = length // RADIX
    per = points // 2
    row = lax.broadcasted_iota(jnp.int32, (points, points), 0)
    lane = lax.broadcasted_iota(jnp.int32, (points, points), 1)
    phases = (2.0 * math.pi / points) * (row * (lane % per) % points).astype(jnp.float32)
    cosine, sine = jnp.cos(phases), jnp.sin(phases)
    for h in range(2):
        inside = (lane >= per) if h else (lane < per)
        c, s = jnp.where(inside, cosine, 0.0), jnp.where(inside, sine, 0.0)
        for part, values in enumerate(((c, -s), (s, c))):
            rows = slice((2 * h + part) * points, (2 * h + part + 1) * points)
            whole = jnp.concatenate(values, axis=1)
            table_ref[rows, :] = whole.astype(jnp.bfloat16)
    residue = lax.broadcasted_iota(jnp.int32, (RADIX, points), 0) + 1
    sample = lax.broadcasted_iota(jnp.int32, (RADIX, points), 1)
    phases = (2.0 * math.pi / length) * (residue * sample).astype(jnp.float32)
    twiddle_ref[0] = jnp.cos(phases)
    twiddle_ref[1] = -jnp.sin(phases)


def lag_table(length, bin_count, lag_count):
    bins = bin_order(bin_count)[:, None]
    lags = np.arange(lag_count)[None, :] - lag_count // 2
    phases = 2.0 * np.pi / length * (bins * lags % length)
    factor = 1.0 / math.sqrt(bin_count)
    cosine, sine = np.cos(phases) * factor, -np.sin(phases) * factor
    return np.concatenate([cosine, sine], axis=0).astype(ml_dtypes.bfloat16)


def real_dft(values):
    n = len(values)
    if n == 1:
        return [(values[0], None)]
    if n == 2:
        return [(values[0] + values[1], None), (values[0] - values[1], None)]
    even, odd = real_dft(values[0::2]), real_dft(values[1::2])
    quarter = n // 4
    out = [None] * (n // 2 + 1)
    for r in range(quarter + 1):
        (er, ei), (orr, oi) = even[r], odd[r]
        cosine, sine = math.cos(2 * math.pi * r / n), math.sin(2 * math.pi * r / n)
        if r == 0:
            tr, ti = orr, None
        elif r == quarter:
            tr, ti = None, -orr
        elif 8 * r == n:
            tr, ti = (orr + oi) * cosine, (oi - orr) * cosine
        else:
            tr, ti = orr * cosine + oi * sine, oi * cosine - orr * sine
        plus_re = er if tr is None else er + tr
        minus_re = er if tr is None else er - tr
        if ei is None:
            plus_im, minus_im = ti, ti
        elif ti is None:
            plus_im, minus_im = ei, -ei
        else:
            plus_im, minus_im = ei + ti, ti - ei
        out[r] = (plus_re, plus_im)
        if r < quarter:
            out[n // 2 - r] = (minus_re, minus_im)
    return out


def spectrum(samples, twiddle_ref, table_ref):
    rows, length = samples.shape
    points = length // RADIX
    half = real_dft([samples[:, i * points : (i + 1) * points] for i in range(RADIX)])
    lanes = []
    for residue in range(1, RADIX + 1):
        folded = min(residue, RADIX - residue)
        re, im = half[folded]
        if residue > RADIX // 2 and im is not None:
            im = -im
        cosine = twiddle_ref[0, residue - 1 : residue, :]
        sine = twiddle_ref[1, residue - 1 : residue, :]
        if im is None:
            lanes.append((re * cosine, re * sine))
        else:
            lanes.append((re * cosine - im * sine, re * sine + im * cosine))
    blocks = []
    for q in range(RADIX // 2):
        (ar, ai), (br, bi) = lanes[2 * q], lanes[2 * q + 1]
        blocks.append(jnp.concatenate([ar, ai, br, bi], axis=1))
    stacked = jnp.concatenate(blocks, axis=0)
    high = stacked.astype(jnp.bfloat16)
    low = (stacked - high.astype(jnp.float32)).astype(jnp.bfloat16)
    both = jnp.dot(
        jnp.concatenate([high, low], axis=0), table_ref[...], preferred_element_type=jnp.float32
    )
    count = stacked.shape[0]
    out = both[:count] + both[count:]
    width = out.shape[1] // 2
    re = [out[q * rows : (q + 1) * rows, :width] for q in range(RADIX // 2)]
    im = [out[q * rows : (q + 1) * rows, width:] for q in range(RADIX // 2)]
    return re, im


def scales(re, im, radius, mask):
    amp = [jnp.sqrt(a * a + b * b) for a, b in zip(re, im)]
    rows, width = amp[0].shape
    per = width // 2
    reach = radius // RADIX
    lane = lax.broadcasted_iota(jnp.int32, (rows, width), 1)
    place = lane % per
    upper = lane >= per
    swapped = [pltpu.roll(a, per, 1) for a in amp]
    pair = [a + b for a, b in zip(amp, swapped)]
    total = pair[0]
    for value in pair[1:]:
        total = total + value

    def shifted(value, by):
        moved = pltpu.roll(value, (-by) % width, 1)
        inside = (place + by >= 0) & (place + by < per)
        return jnp.where(inside, moved, 0.0)

    centre = total
    for by in range(1, reach):
        centre = centre + shifted(total, by) + shifted(total, -by)
    before = jnp.zeros_like(total)
    out = []
    for a, b, both in zip(amp, swapped, pair):
        upto = before + a + jnp.where(upper, b, 0.0)
        before_here = before + jnp.where(upper, b, 0.0)
        onward = total - before_here
        before = before + both
        out.append((upto, onward))
    result = []
    for upto, onward in out:
        summed = centre + shifted(upto, reach) + shifted(onward, -reach)
        result.append(mask / (summed * (1.0 / (2 * radius + 1)) + 1e-06))
    return result


def whiten_rows(samples, radius, mask, twiddle_ref, table_ref, relay_ref, out_ref):
    rows = samples.shape[0]
    blocks = RADIX // 2
    re, im = spectrum(samples, twiddle_ref, table_ref)
    scale = scales(re, im, radius, mask)
    for part, values in enumerate((re, im)):
        for q in range(blocks):
            relay_ref[pl.ds(part * rows * blocks + q, rows, stride=blocks), :] = (
                values[q] * scale[q]
            )
    out_ref[...] = relay_ref[...].astype(jnp.bfloat16)


def turn(index):
    return TURN_GATHER[min(index, len(TURN_GATHER) - 1)]


def panel_order(bits):
    held = [(0, 0)]
    for index, bit in enumerate(bits[:-1]):
        first = len(held)
        held = held + [(k ^ bit, odd ^ turn(index)) for k, odd in held]
    last = [(k ^ bits[-1], odd ^ turn(len(bits) - 1)) for k, odd in held]
    order = []
    for pieces in (held, last[:first], last[first:]):
        order += pieces + [(k, 1 - odd) for k, odd in pieces]
    return order


def flags_of(picks, flags):
    return lax.dot_general(
        picks.astype(jnp.bfloat16),
        flags,
        (((1,), (1,)), ((), ())),
        preferred_element_type=jnp.float32,
    )


def at_window(rows_flags):
    row = lax.broadcasted_iota(jnp.int32, rows_flags.shape, 0)
    column = lax.broadcasted_iota(jnp.int32, rows_flags.shape, 1)
    kept = jnp.where(row % rows_flags.shape[1] == column, rows_flags, 0.0)
    return jnp.sum(kept, axis=1, keepdims=True)


def choice_kernel(halves, channels, ids_ref, usable_ref, after_ref, *outs):
    del after_ref
    choice_ref, mask_ref, take_ref, info_ref = outs
    windows, total = usable_ref.shape
    members = lax.axis_size("dev")
    group, member = lax.axis_index("grp"), lax.axis_index("dev")
    core, plane = group % SRC_DEV, group // SRC_DEV
    flags = usable_ref[...].astype(jnp.float32).astype(jnp.bfloat16)

    def panel(step, shape):
        chosen = jnp.broadcast_to(ids_ref[:, step : step + 1], shape)
        return lax.div(chosen, halves), lax.rem(chosen, halves)

    row = lax.broadcasted_iota(jnp.int32, choice_ref.shape, 0)
    choice = jnp.zeros(choice_ref.shape, jnp.float32)
    for t in range(STEPS):
        owning, within = panel(t, choice_ref.shape)
        apart = lax.rem(owning + core, SRC_DEV)
        choice = jnp.where(row == (t * SRC_DEV + apart) * halves + within, 1.0, choice)
    choice_ref[...] = choice

    row = lax.broadcasted_iota(jnp.int32, info_ref.shape, 0)
    info = jnp.zeros(info_ref.shape, jnp.int32)
    for t in range(STEPS):
        owning, within = panel(t, info_ref.shape)
        info = jnp.where(row == t, owning * (members * channels) + within * SRC_DEV, info)
    info_ref[...] = info

    shape = (STEPS * windows, total)
    row = lax.broadcasted_iota(jnp.int32, shape, 0)
    lane = lax.broadcasted_iota(jnp.int32, shape, 1)
    picks = jnp.zeros(shape, jnp.float32)
    for t in range(STEPS):
        owning, within = panel(t, shape)
        channel = (owning * members + member) * channels + within * SRC_DEV + core
        picks = jnp.where((row // windows == t) & (lane == channel), 1.0, picks)
    mask_ref[...] = jnp.broadcast_to(at_window(flags_of(picks, flags)), mask_ref.shape)

    shape = take_ref.shape[1:]
    row = lax.broadcasted_iota(jnp.int32, shape, 0)
    for index in range(take_ref.shape[0]):
        take = jnp.zeros(shape, jnp.float32)
        for t in range(STEPS):
            owning, _ = panel(t, shape)
            differs = (lax.div(owning, SRC_DEV) ^ plane) & (1 << index)
            take = jnp.where((row // windows == t) & (differs != 0), 1.0, take)
        take_ref[index] = take


def pick_kernel(flip, choice_ref, own_ref, other_ref, after_ref, out_ref, samples):
    del after_ref
    channels, windows, length = own_ref.shape
    halves = channels // SRC_DEV
    half = (lax.axis_index("grp") + flip) % SRC_DEV
    points = length // RADIX
    for step in range(STEPS):
        held = [jnp.zeros((windows, points), jnp.float32)] * RADIX
        for k, raw_ref in enumerate((own_ref, other_ref)):
            for h in range(halves):
                index = (step * SRC_DEV + k) * halves + h
                here = jnp.broadcast_to(choice_ref[index : index + 1, :], (windows, points)) > 0.0
                row = raw_ref[h * SRC_DEV + half].astype(jnp.float32)
                for n in range(RADIX):
                    held[n] = jnp.where(here, row[:, n * points : (n + 1) * points], held[n])
        for n in range(RADIX):
            samples[step * windows : (step + 1) * windows, n * points : (n + 1) * points] = held[n]
    out_ref[...] = samples[...].astype(out_ref.dtype)


def receiver_kernel(radius, order, last_bit, info_ref, usable_ref, raw_ref, twiddle_ref, table_ref, *rest):
    spectra_ref, inverse_ref, other_ref, samples, relay = rest
    channels, windows, _ = raw_ref.shape
    members = lax.axis_size("dev")
    group, member = lax.axis_index("grp"), lax.axis_index("dev")
    core = group % SRC_DEV
    first = (group * members + member) * channels
    flags = usable_ref[...].astype(jnp.float32).astype(jnp.bfloat16)
    total = flags.shape[1]

    for r in range(channels):
        samples[r * windows : (r + 1) * windows, :] = raw_ref[r].astype(jnp.float32)
    rows = channels * windows
    row = lax.broadcasted_iota(jnp.int32, (rows, total), 0)
    lane = lax.broadcasted_iota(jnp.int32, (rows, total), 1)
    own = jnp.where(lane == first + row // windows, 1.0, 0.0)
    mask = at_window(flags_of(own, flags))
    whiten_rows(samples[...], radius, mask, twiddle_ref, table_ref, relay, spectra_ref)

    rows = STEPS * channels
    row = lax.broadcasted_iota(jnp.int32, (rows, total), 0)
    lane = lax.broadcasted_iota(jnp.int32, (rows, total), 1)
    start = jnp.zeros((rows, total), jnp.int32)
    for t in range(STEPS):
        here = jnp.broadcast_to(info_ref[t : t + 1, :1], (rows, total))
        start = jnp.where(row // channels == t, here, start)
    blocks = []
    for k, odd in order:
        offset = (member ^ k) * channels + (core + odd) % SRC_DEV
        blocks.append(jnp.where(lane == start + offset, 1.0, 0.0))
    sent = flags_of(jnp.concatenate(blocks, axis=0), flags)
    theirs = ((group ^ TURN_LAST) * members + (member ^ last_bit)) * channels
    for ref, start in ((inverse_ref, first), (other_ref, theirs)):
        received = flags_of(jnp.where(lane == start + row % channels, 1.0, 0.0), flags)
        both = sent * jnp.concatenate([received] * len(order), axis=0)
        counts = jnp.sum(both, axis=1, keepdims=True)
        ref[...] = jnp.broadcast_to(1.0 / jnp.maximum(counts, 1.0), ref.shape)


def source_kernel(radius, *refs):
    take_ref, mask_ref, kept_ref, came_ref, twiddle_ref, table_ref = refs[:6]
    out_ref, relay = refs[-2:]
    rows, length = kept_ref.shape
    points = length // RADIX
    here = take_ref[...] > 0.0
    kept, came = kept_ref[...].astype(jnp.float32), came_ref[...].astype(jnp.float32)
    here = jnp.concatenate([here] * RADIX, axis=1)
    samples = jnp.where(here, came, kept)
    whiten_rows(samples, radius, mask_ref[:, :1], twiddle_ref, table_ref, relay, out_ref)


def lagged_rows(windows, pieces, sets, table_ref, products, stacked):
    blocks = RADIX // 2

    def row_set(ref, base, first, rows):
        out = []
        for part in range(2):
            held = []
            for w in range(0, windows, 2):
                start = base + (part * rows + first + w) * blocks
                both = ref[start : start + 2 * blocks, :].astype(jnp.float32)
                held += [both[:blocks], both[blocks:]]
            out.append(held)
        return out

    pair = 0
    for recv_ref, _ in sets:
        receivers = recv_ref.shape[0] // (2 * windows * blocks)
        own = [row_set(recv_ref, 0, r * windows, receivers * windows) for r in range(receivers)]
        for ref, base in pieces:
            for step in range(STEPS):
                a, b = row_set(ref, base, step * windows, STEPS * windows)
                for r in range(receivers):
                    c, e = own[r]
                    re = im = None
                    for w in range(windows):
                        re_w = a[w] * c[w] + b[w] * e[w]
                        im_w = b[w] * c[w] - a[w] * e[w]
                        re = re_w if re is None else re + re_w
                        im = im_w if im is None else im + im_w
                    products[0, pair * blocks : (pair + 1) * blocks, :] = re
                    products[1, pair * blocks : (pair + 1) * blocks, :] = im
                    pair += 1
    width = products.shape[2]
    inverse = jnp.concatenate([factors for _, factors in sets], axis=0)
    for part in range(2):
        for q in range(blocks):
            column = (part * blocks + q) * width
            values = products[part, pl.ds(q, pair, stride=blocks), :] * inverse
            stacked[:, column : column + width] = values.astype(jnp.bfloat16)
    return jnp.dot(stacked[...], table_ref[...], preferred_element_type=jnp.float32)


def pieces_of(ref, windows):
    rows = 2 * STEPS * windows * (RADIX // 2)
    return [(ref, base) for base in range(0, ref.shape[0], rows)]


def part_kernel(windows, first, n_sets, *refs):
    table_ref, set_refs, refs = refs[0], refs[1 : 1 + 2 * n_sets], refs[1 + 2 * n_sets :]
    products, stacked = refs[-2:]
    buffers, outs = refs[: -2 - n_sets], refs[-2 - n_sets : -2]
    pieces = [piece for ref in buffers for piece in pieces_of(ref, windows)]
    rows = outs[0].shape[0]
    sets = [
        (set_refs[2 * i], set_refs[2 * i + 1][first : first + rows, :]) for i in range(n_sets)
    ]
    lagged = lagged_rows(windows, pieces, sets, table_ref, products, stacked)
    for i, out_ref in enumerate(outs):
        out_ref[...] = lagged[i * rows : (i + 1) * rows].astype(jnp.bfloat16)


def pass_kernel(value_ref, after_ref, out_ref):
    del after_ref
    out_ref[...] = value_ref[...]


def place_kernel(order, last_bit, *refs):
    out_ref = refs[-1]
    member = lax.axis_index("dev")
    core = lax.axis_index("grp") % SRC_DEV
    receivers = out_ref.shape[2]
    whole = order + [(k ^ last_bit, odd ^ TURN_LAST) for k, odd in order]
    block = STEPS * receivers
    done = 0
    for ref in refs[:-1]:
        for p in range(ref.shape[0] // block):
            k, odd = whole[done]
            source = (member ^ k) * SRC_DEV + (core + odd) % SRC_DEV
            for step in range(STEPS):
                row = p * block + step * receivers
                out_ref[step, source] = ref[row : row + receivers, :]
            done += 1


def on_device(records, usable, panel_ids):
    channels, windows, length = records.shape
    bin_count = length // 2
    radius = bin_count // 16
    halves = channels // SRC_DEV
    groups = lax.axis_size("grp")
    members = lax.axis_size("dev")
    blocks = RADIX // 2
    width = bin_count // blocks

    def exchange(value, group_bit, member_bit):
        flip = group_bit * members + member_bit
        pairs = [(i, i ^ flip) for i in range(groups * members)]
        return lax.ppermute(value, AXES, pairs)

    ltable = jnp.asarray(lag_table(length, bin_count, NLAG))
    all_bits = [1 << i for i in range(members.bit_length() - 1)]
    chosen = [all_bits[i] for i in BIT_ORDER]
    *gather_bits, last_bit = [b for b in all_bits[::-1] if b not in chosen] + chosen
    order = panel_order(gather_bits)

    usable_rows = usable.T
    planes = groups // SRC_DEV
    source_rows = STEPS * windows
    plane_bits = planes.bit_length() - 1

    records_other = exchange(records, 1, 0)
    points = length // RADIX
    table, twiddle = pl.pallas_call(
        functools.partial(tables_kernel, length),
        out_shape=[
            jax.ShapeDtypeStruct((4 * points, 2 * points), jnp.bfloat16),
            jax.ShapeDtypeStruct((2, RADIX, points), jnp.float32),
        ],
        in_specs=[],
        out_specs=[VMEM] * 2,
        compiler_params=PARAMS,
        cost_estimate=AHEAD,
        name="short_tables",
    )()

    choice, mask, take, info = pl.pallas_call(
        functools.partial(choice_kernel, halves, channels),
        out_shape=[
            jax.ShapeDtypeStruct((STEPS * SRC_DEV * halves, width), jnp.float32),
            jax.ShapeDtypeStruct((source_rows, width), jnp.float32),
            jax.ShapeDtypeStruct((plane_bits, source_rows, width), jnp.float32),
            jax.ShapeDtypeStruct((8, width), jnp.int32),
        ],
        in_specs=[VMEM] * 3,
        out_specs=[VMEM] * 4,
        compiler_params=PARAMS,
        name="choose_rows",
    )(panel_ids[None, :], usable_rows, twiddle)

    row_count = channels * windows
    pairs = len(order) * STEPS * channels
    receivers, inverse, inverse_theirs = pl.pallas_call(
        functools.partial(receiver_kernel, radius, order, last_bit),
        out_shape=[
            jax.ShapeDtypeStruct((2 * row_count * blocks, width), jnp.bfloat16),
            jax.ShapeDtypeStruct((pairs, width), jnp.float32),
            jax.ShapeDtypeStruct((pairs, width), jnp.float32),
        ],
        in_specs=[VMEM] * 5,
        out_specs=[VMEM] * 3,
        scratch_shapes=[
            pltpu.VMEM((row_count, length), jnp.float32),
            pltpu.VMEM((2 * row_count * blocks, width), jnp.float32),
        ],
        compiler_params=PARAMS,
        cost_estimate=AHEAD,
        name="receiver_spectra",
    )(info, usable_rows, records, twiddle, table)

    def pick(flip):
        return pl.pallas_call(
            functools.partial(pick_kernel, flip),
            out_shape=jax.ShapeDtypeStruct((source_rows, length), records.dtype),
            in_specs=[VMEM] * 4,
            out_specs=VMEM,
            scratch_shapes=[pltpu.VMEM((source_rows, length), jnp.float32)],
            compiler_params=PARAMS,
            name="pick_rows",
        )(choice, records, records_other, inverse)

    sent = pick(TURN_PLANE)
    came = exchange(sent, SRC_DEV * (planes // 2) + TURN_PLANE, 0)
    kept = pick(0) if TURN_PLANE else sent
    for index in range(plane_bits - 2, -1, -1):
        kept = jnp.where(take[index + 1][:, :1] > 0.0, came, kept)
        came = exchange(kept, SRC_DEV << index, 0)

    piece = pl.pallas_call(
        functools.partial(source_kernel, radius),
        out_shape=jax.ShapeDtypeStruct((2 * source_rows * blocks, width), jnp.bfloat16),
        in_specs=[VMEM] * 7,
        out_specs=VMEM,
        scratch_shapes=[pltpu.VMEM((2 * source_rows * blocks, width), jnp.float32)],
        compiler_params=PARAMS,
        name="source_spectra",
    )(take[0], mask, kept, came, twiddle, table, receivers)

    def part(first, sets, *buffers, cost=BESIDE):
        rows = sum(b.shape[0] for b in buffers) // (2 * windows * blocks) * channels
        total = rows * len(sets)
        return pl.pallas_call(
            functools.partial(part_kernel, windows, first, len(sets)),
            out_shape=[jax.ShapeDtypeStruct((rows, NLAG), jnp.bfloat16)] * len(sets),
            in_specs=[VMEM] * (1 + 2 * len(sets) + len(buffers)),
            out_specs=[VMEM] * len(sets),
            scratch_shapes=[
                pltpu.VMEM((2, total * blocks, width), jnp.float32),
                pltpu.VMEM((total, 2 * bin_count), jnp.bfloat16),
            ],
            compiler_params=PARAMS,
            cost_estimate=cost,
            name="correlate_part",
        )(ltable, *[array for pair in sets for array in pair], *buffers)

    def pass_on(value, after):
        return pl.pallas_call(
            pass_kernel,
            out_shape=jax.ShapeDtypeStruct(value.shape, value.dtype),
            in_specs=[VMEM] * 2,
            out_specs=VMEM,
            compiler_params=PARAMS,
            name="pass_on",
        )(value, after)

    held = piece
    for index, bit in enumerate(gather_bits[:-2]):
        held = jnp.concatenate([held, exchange(held, turn(index), bit)], axis=0)
    rounds = len(gather_bits)
    theirs = exchange(receivers, TURN_LAST, last_bit)
    fresh = pass_on(exchange(held, turn(rounds - 2), gather_bits[-2]), theirs)
    first = exchange(held, turn(rounds - 1), gather_bits[-1])
    second = exchange(fresh, turn(rounds - 1), gather_bits[-1])
    held = jnp.concatenate([held, fresh], axis=0)
    pieces = [held, exchange(held, 1, 0), first, exchange(first, 1, 0)]
    pieces += [second, exchange(second, 1, 0)]
    mine, other = (receivers, inverse), (theirs, inverse_theirs)
    early_theirs, early = part(0, [other, mine], held)
    (next_theirs,) = part(pairs // 4, [other], *pieces[1:3])
    (more_theirs,) = part(pairs // 8 * 5, [other], *pieces[3:5])
    (late_theirs,) = part(pairs // 8 * 7, [other], *pieces[5:])
    (late,) = part(pairs // 4, [mine], *pieces[1:])
    back = exchange(jnp.concatenate([early_theirs, next_theirs, more_theirs, late_theirs], axis=0), TURN_LAST, last_bit)
    return pl.pallas_call(
        functools.partial(place_kernel, order, last_bit),
        out_shape=jax.ShapeDtypeStruct(
            (STEPS, members * SRC_DEV, channels, NLAG), jnp.bfloat16
        ),
        in_specs=[VMEM] * 3,
        out_specs=VMEM,
        compiler_params=PARAMS,
        name="place_rows",
    )(early, late, back)


def solution(mesh):
    placed = (P(AXES, None, None), P(), P())
    return jax.shard_map(
        on_device,
        mesh=mesh,
        in_specs=placed,
        out_specs=P(None, None, AXES, None),
        check_vma=False,
    )
```
